32 devices in a mesh: groups: 2 (over y), sky: 16 (over z, x, core).
Axes of the slice: x: 2, y: 2, z: 4, core: 2. Of those that a mesh axis runs over, the one named last changes fastest.
Arguments:
- model: float32 [64, 6, 256, 128], P(('groups', 'sky')), parts along dimension 0, may hold values from 0 to 2
- exposures: bfloat16 [4096, 16, 128], P(('groups', 'sky')), parts along dimension 0, may hold values from -6 to 6
- inv_var: float32 [4096], P(('groups', 'sky')), parts along dimension 0, may hold values from 0.5 to 2
- step_size: float32 [6], replicated, may hold values from 0.2 to 0.6
- psf_taps: float32 [64, 56], P(('groups', 'sky')), parts along dimension 0, may hold values from 0.05 to 1
- exp_batch: int32 [4096], P(('groups', 'sky')), parts along dimension 0, may hold values from 0 to 31
- send_plane: int32 [512, 16], P(('groups', 'sky')), parts along dimension 0, may hold values from -1 to 11, as said below
- send_row: int32 [512, 16], P(('groups', 'sky')), parts along dimension 0, may hold values from 0 to 248, as said below
- send_cover: int32 [512, 16], P(('groups', 'sky')), parts along dimension 0, may hold values from 0 to 16, as said below
- use_slot: int32 [4096, 2], P(('groups', 'sky')), parts along dimension 0, may hold values from -1 to 255, as said below
- use_start: int32 [4096, 2], P(('groups', 'sky')), parts along dimension 0, may hold values from 0 to 8, as said below
- use_stop: int32 [4096, 2], P(('groups', 'sky')), parts along dimension 0, may hold values from 0 to 16
- foot_lo: int32 [64], P(('groups', 'sky')), parts along dimension 0, may hold values from 0 to 63
- foot_hi: int32 [64], P(('groups', 'sky')), parts along dimension 0, may hold values from 193 to 256
Outputs:
- updated_model: float32 [64, 6, 256, 128], P(('groups', 'sky')), parts along dimension 0
- residual: float32 [4096, 16, 128], P(('groups', 'sky')), parts along dimension 0
The draws below stay inside these ranges and needn't reach their ends.
There are 2 independent parts, one for each index of `groups`. The reference program is written for one: setup_inputs(seed, part) draws one part's arguments, and reference() takes and returns one part's arrays. A program takes and returns all parts, laid end to end along the dimension named above; an argument that names none is the same for every part. Nothing has to cross between parts.
Inputs may be any that keep to these rules, and one draw needn't show every extreme that they name: In each row of send_plane the covered rows of the live slots (send_cover) sum to at most 128, and on every device some row reaches it. A live slot of exposure owner d is used by exactly one intersection of one exposure on d, and every intersection with use_slot >= 0 names a live slot; all pieces of an exposure come from planes of one band. `send_row`: for a live slot, the tile rows that its piece covers lie inside the tile. send_cover of a live slot equals use_stop - use_start of the intersection that uses it. `use_slot`: each exposure has 1 to 2 live intersections, first in order; -1 after them. `use_start`: the live intersections of an exposure cover rows 0 to 15 in order without gaps; dead ones have start and stop 0.
All inputs are finite; a program needn't handle non-finite values.
Results may differ from the reference program's by a relative error of at most 0.0011.
Values may be sent and summed in bfloat16 or wider, within the bound.
No kernel may reach another device: no remote copies, remote signals or barrier semaphores. Data moves between devices by JAX's collectives and lax.ppermute only.
A program may use at most 128 MiB of HBM per device.

```python
import math
import jax
import jax.numpy as jnp
from jax import lax

B = 6
W = 128
TR = 256
H = 16
TILE_DEV = 2
EXP_DEV = 128
K = 2
NPSF = 4
TAPS = 7
ITERS = 2
NT = 32
NE = 2048
NBATCH = 32
CAP = 16
N_SKY = 16


def routing(key):
    base = jax.random.fold_in(key, 7919)
    keys = jax.random.split(base, 5)
    half = H // 2
    budget = CAP * H // 2
    count = jax.random.randint(keys[0], (N_SKY, EXP_DEV), 1, 3)
    count = count.at[:, 0].set(1)
    band_of = jax.random.randint(keys[1], (N_SKY, EXP_DEV), 0, B)
    source_order = jax.vmap(lambda subkey: jax.random.permutation(subkey, N_SKY))(jax.random.split(keys[2], N_SKY))
    tile_of = jax.random.randint(keys[3], (N_SKY, EXP_DEV, K), 0, TILE_DEV)
    raw_offset = jax.random.randint(keys[4], (N_SKY, EXP_DEV, K), 0, 1 << 20)
    intersection = jnp.arange(K, dtype=jnp.int32)[None, None, :]
    alive = intersection < count[:, :, None]
    split_two = count[:, :, None] == 2
    start = jnp.where(alive & (intersection == 1), half, 0)
    length = jnp.where(alive, jnp.where(split_two, jnp.where(intersection == 0, half, H - half), H), 0)
    stop = jnp.where(alive, start + length, 0)
    position = jnp.arange(EXP_DEV, dtype=jnp.int32)[None, :, None] * H + start
    source_rank = position // budget
    slot_column = position % budget // half
    source = jnp.take_along_axis(source_order, source_rank.reshape(N_SKY, -1), axis=1).reshape(N_SKY, EXP_DEV, K)
    slot = source * CAP + slot_column
    tile_row = raw_offset % (TR - length + 1)
    plane = tile_of * B + band_of[:, :, None]
    slot_alive = jnp.where(alive, slot, -1)
    target = jnp.where(alive, slot, N_SKY * CAP).reshape(N_SKY, -1)
    owners = jnp.arange(N_SKY, dtype=jnp.int32)[:, None]
    table_plane = jnp.full((N_SKY, N_SKY * CAP), -1, jnp.int32).at[owners, target].set(plane.reshape(N_SKY, -1), mode='drop')
    table_row = jnp.zeros((N_SKY, N_SKY * CAP), jnp.int32).at[owners, target].set(tile_row.reshape(N_SKY, -1), mode='drop')
    table_cover = jnp.zeros((N_SKY, N_SKY * CAP), jnp.int32).at[owners, target].set(length.reshape(N_SKY, -1), mode='drop')
    send_plane = table_plane.reshape(N_SKY, N_SKY, CAP).transpose(1, 0, 2).reshape(N_SKY * N_SKY, CAP)
    send_row = table_row.reshape(N_SKY, N_SKY, CAP).transpose(1, 0, 2).reshape(N_SKY * N_SKY, CAP)
    send_cover = table_cover.reshape(N_SKY, N_SKY, CAP).transpose(1, 0, 2).reshape(N_SKY * N_SKY, CAP)
    return (slot_alive.reshape(NE, K).astype(jnp.int32), start.reshape(NE, K).astype(jnp.int32), stop.reshape(NE, K).astype(jnp.int32), send_plane.astype(jnp.int32), send_row.astype(jnp.int32), send_cover.astype(jnp.int32))


def draw_use_slot(key, part):
    return routing(key)[0]


def draw_use_start(key, part):
    return routing(key)[1]


def draw_use_stop(key, part):
    return routing(key)[2]


def draw_send_plane(key, part):
    return routing(key)[3]


def draw_send_row(key, part):
    return routing(key)[4]


def draw_send_cover(key, part):
    return routing(key)[5]


def place_ends(drawn, stream_key, low, high):
    dims = drawn.shape
    place = [jax.random.randint(jax.random.fold_in(stream_key, axis), (), 0, dims[axis]) for axis in range(len(dims))]
    drawn = drawn.at[tuple(place)].set(low)
    longest = dims.index(max(dims))
    place[longest] = (place[longest] + 1) % dims[longest]
    return drawn.at[tuple(place)].set(high)


def levels(key, shape, cuts, low, top_value):
    def one(axis_at, shards_of):
        draws = jax.random.uniform(jax.random.fold_in(jax.random.fold_in(key, 6), axis_at), (shards_of,), jnp.float32, low / len(cuts), top_value / len(cuts))
        return jnp.repeat(jnp.exp(draws), shape[axis_at] // shards_of).reshape((-1,) + (1,) * (len(shape) - axis_at - 1))

    loudness = one(*cuts[0])
    for cut in cuts[1:]:
        loudness = loudness * one(*cut)
    return loudness


def noise(stream_key, shape, width, most, cuts=(), kind=jnp.bfloat16):
    array = jax.random.normal(stream_key, shape, jnp.float32) * width
    if len(cuts) > 0:
        array = levels(stream_key, shape, cuts, -0.22, 0.18) * array
    return jnp.clip(array, min=-most, max=most).astype(kind)


def setup_inputs(seed: int = 0, part: int = 0) -> dict:
    splits = jax.random.split(jax.random.key(seed), 15)
    part_keys = jax.random.split(jax.random.fold_in(splits[14], part), 15)
    return {
        "model": jnp.clip(2.0 * jax.random.uniform(part_keys[0], (NT, B, TR, W), jnp.float32) ** levels(part_keys[0], (NT, B, TR, W), ((0, 16),), -0.2, 0.2), 0.0, 2.0),
        "exposures": noise(part_keys[1], (NE, H, W), 1.0, 6.0, ((0, 16),)),
        "inv_var": jnp.clip(jnp.exp(math.log(2.0) - 1.3862944 * jax.random.uniform(part_keys[2], (NE,), jnp.float32) ** levels(part_keys[2], (NE,), ((0, 16),), -0.2, 0.2)), 0.5, 2.0),
        "step_size": jnp.clip(jnp.exp(jax.random.uniform(splits[3], (B,), jnp.float32, math.log(0.2), math.log(0.6))), 0.2, 0.6),
        "psf_taps": jnp.clip(0.05 + 0.95 * jax.random.uniform(part_keys[4], (NBATCH, 2 * NPSF * TAPS), jnp.float32) ** levels(part_keys[4], (NBATCH, 2 * NPSF * TAPS), ((0, 16),), -0.2, 0.2), 0.05, 1.0),
        "exp_batch": place_ends(jax.random.randint(part_keys[5], (NE,), 0, NBATCH), jax.random.fold_in(part_keys[5], 1), 0, NBATCH - 1).astype(jnp.int32),
        "send_plane": draw_send_plane(jax.random.fold_in(jax.random.fold_in(splits[14], part), 71), part),
        "send_row": draw_send_row(jax.random.fold_in(jax.random.fold_in(splits[14], part), 71), part),
        "send_cover": draw_send_cover(jax.random.fold_in(jax.random.fold_in(splits[14], part), 71), part),
        "use_slot": draw_use_slot(jax.random.fold_in(jax.random.fold_in(splits[14], part), 71), part),
        "use_start": draw_use_start(jax.random.fold_in(jax.random.fold_in(splits[14], part), 71), part),
        "use_stop": draw_use_stop(jax.random.fold_in(jax.random.fold_in(splits[14], part), 71), part),
        "foot_lo": place_ends(jax.random.randint(part_keys[12], (NT,), 0, TR // 4), jax.random.fold_in(part_keys[12], 1), 0, (TR // 4) - 1).astype(jnp.int32),
        "foot_hi": place_ends(jax.random.randint(part_keys[13], (NT,), TR - TR // 4 + 1, TR + 1), jax.random.fold_in(part_keys[13], 1), TR - TR // 4 + 1, TR).astype(jnp.int32),
    }


def build_ops(kernel_taps, extent):
    half_width = kernel_taps.shape[-1] // 2
    offset_grid = lax.broadcasted_iota(jnp.int32, (extent, extent), 0) - lax.broadcasted_iota(jnp.int32, (extent, extent), 1) + half_width
    onehot = (offset_grid[:, :, None] == jnp.arange(kernel_taps.shape[-1], dtype=jnp.int32)[None, None, :]).astype(jnp.float32)
    return jnp.einsum("ejt,abt->ejab", kernel_taps, onehot, precision=lax.Precision.HIGHEST).astype(jnp.bfloat16)


def block_step(padded, exposures, inv_var, taps_rows, use_slot, use_start, use_stop, send_plane, send_row, send_cover, owner):
    f32 = jnp.float32
    kernel_taps = taps_rows.reshape(taps_rows.shape[0], 2, NPSF, TAPS)
    kernel_taps = kernel_taps / jnp.sum(kernel_taps, axis=-1, keepdims=True)
    row_ops = build_ops(kernel_taps[:, 0], H)
    col_ops = build_ops(kernel_taps[:, 1], W)
    alive = use_slot >= 0
    slot_safe = jnp.maximum(use_slot, 0)
    source = slot_safe // CAP
    column = slot_safe % CAP
    table_row = source * N_SKY + owner
    plane = send_plane[table_row, column]
    cover = send_cover[table_row, column]
    row_first = send_row[table_row, column] + H - use_start
    global_plane = source * (TILE_DEV * B) + jnp.maximum(plane, 0)

    def take_piece(plane_id, row_start):
        return lax.dynamic_slice(padded, (plane_id, row_start, jnp.int32(0)), (1, H, W))[0]

    pieces = jax.vmap(jax.vmap(take_piece))(global_plane, row_first)
    row_pos = jnp.arange(H, dtype=jnp.int32)
    ahead = row_pos[None, None, :] >= use_start[:, :, None]
    forward = ahead & (row_pos[None, None, :] < use_start[:, :, None] + cover[:, :, None]) & alive[:, :, None]
    covered = ahead & (row_pos[None, None, :] < use_stop[:, :, None]) & alive[:, :, None]
    stamps = jnp.sum(jnp.where(forward[..., None], pieces.astype(f32), 0.0), axis=1).astype(jnp.bfloat16)
    blurred = jnp.einsum("erd,ejcd->erjc", stamps.astype(f32), col_ops.astype(f32)).astype(jnp.bfloat16)
    predicted = jnp.einsum("ejrs,esjc->erc", row_ops.astype(f32), blurred.astype(f32)) / NPSF
    residual = inv_var[:, None, None] * (predicted - exposures.astype(f32))
    back = jnp.einsum("ejsr,esc->erjc", row_ops.astype(f32), residual.astype(jnp.bfloat16).astype(f32)).astype(jnp.bfloat16)
    correlated = (jnp.einsum("erjc,ejcd->erd", back.astype(f32), col_ops.astype(f32)) / NPSF).astype(jnp.bfloat16)
    contrib = jnp.where(covered[..., None], correlated[:, None].astype(f32), 0.0)
    target = jnp.where(alive, global_plane, NT * B)
    return residual, target, row_first, contrib


def reference(model, exposures, inv_var, step_size, psf_taps, exp_batch, send_plane, send_row, send_cover, use_slot, use_start, use_stop, foot_lo, foot_hi):
    taps_all = psf_taps[exp_batch]
    current = model
    row_pos = jnp.arange(H, dtype=jnp.int32)
    tile_pos = jnp.arange(TR, dtype=jnp.int32)
    inside = (tile_pos[None, :] >= foot_lo[:, None]) & (tile_pos[None, :] < foot_hi[:, None])
    residual_all = None
    for sweep in range(ITERS):
        planes = current.astype(jnp.bfloat16).reshape(NT * B, TR, W)
        padded = jnp.pad(planes, ((0, 0), (H, H), (0, 0)))

        def one_block(gradient, owner):
            first = owner * EXP_DEV
            residual, target, row_first, contrib = block_step(
                padded,
                lax.dynamic_slice_in_dim(exposures, first, EXP_DEV, 0),
                lax.dynamic_slice_in_dim(inv_var, first, EXP_DEV, 0),
                lax.dynamic_slice_in_dim(taps_all, first, EXP_DEV, 0),
                lax.dynamic_slice_in_dim(use_slot, first, EXP_DEV, 0),
                lax.dynamic_slice_in_dim(use_start, first, EXP_DEV, 0),
                lax.dynamic_slice_in_dim(use_stop, first, EXP_DEV, 0),
                send_plane, send_row, send_cover, owner)
            gradient = gradient.at[target[:, :, None], row_first[:, :, None] + row_pos[None, None, :]].add(contrib, mode="drop")
            return gradient, residual

        gradient, residual_all = lax.scan(one_block, jnp.zeros((NT * B, TR + 2 * H, W), jnp.float32), jnp.arange(N_SKY, dtype=jnp.int32))
        gradient = gradient[:, H:H + TR].reshape(NT, B, TR, W)
        updated = jnp.maximum(current - step_size[None, :, None, None] * gradient, 0.0)
        current = jnp.where(inside[:, None, :, None], updated, 0.0)
    return current, residual_all.reshape(NE, H, W)
```

```python
import functools

import jax
import jax.numpy as jnp
from jax import lax
from jax.experimental import pallas as pl
from jax.experimental.pallas import tpu as pltpu
from jax.sharding import PartitionSpec as P

NPSF = 4
TAPS = 7
ITERS = 2
LANES = 128
HALF = TAPS // 2
FLIP = 64
F32 = jnp.float32
BF16 = jnp.bfloat16
I32 = jnp.int32
VMEM_BYTES = 24 * 1024 * 1024

smem = lambda: pl.BlockSpec(memory_space=pltpu.SMEM)
vmem = lambda: pl.BlockSpec(memory_space=pltpu.VMEM)
hbm = lambda: pl.BlockSpec(memory_space=pl.ANY)


def params():
    return pltpu.CompilerParams(vmem_limit_bytes=VMEM_BYTES)


def aligned(rows):
    return -(-rows // 16) * 16


def pack_slots(plane_ref, row_ref, cover_ref, tile_rows, height, rows_each, x_ref, packed_ref):
    peers, capacity = plane_ref.shape

    def peer(d, _):
        at = d * rows_each
        for c in range(capacity):
            first = jnp.maximum(plane_ref[d, c], 0) * tile_rows + row_ref[d, c]
            packed_ref[pl.ds(at, height), :] = x_ref[pl.ds(first, height), :]
            at = at + cover_ref[d, c]
        return 0

    lax.fori_loop(0, peers, peer, 0)


def bank_rows(taps):
    hp = lax.Precision.HIGHEST
    width = taps.shape[1]

    def grid(columns):
        return (
            lax.broadcasted_iota(I32, (width, columns), 0),
            lax.broadcasted_iota(I32, (width, columns), 1),
        )

    k, l = grid(width)
    total = jnp.dot(taps, (k // TAPS == l // TAPS).astype(F32), precision=hp, preferred_element_type=F32)
    unit = taps / total
    k, l = grid(NPSF * LANES)
    j, l = l // LANES, (l + HALF) % LANES
    wanted = jnp.where(l < TAPS, j * TAPS + TAPS - 1 - l, -1)
    wanted = jnp.where((l >= FLIP) & (l < FLIP + TAPS), j * TAPS + l - FLIP, wanted)
    row_part = jnp.dot(unit, (k == wanted).astype(F32), precision=hp, preferred_element_type=F32)
    k, l = grid(NPSF * TAPS * LANES)
    ji, l = l // LANES, (l + HALF) % LANES
    j, i = ji // TAPS, ji % TAPS
    wanted = NPSF * TAPS + j * TAPS + jnp.where(l < FLIP, i, TAPS - 1 - i)
    col_part = jnp.dot(unit, (k == wanted).astype(F32), precision=hp, preferred_element_type=F32)
    rows = []
    for i in range(TAPS):
        total = 0.0
        for j in range(NPSF):
            at = (j * TAPS + i) * LANES
            total = total + row_part[:, j * LANES : (j + 1) * LANES] * col_part[:, at : at + LANES]
        rows.append(total * (1.0 / NPSF))
    return rows


def first_send_kernel(
    tile_rows, height, rows_each, plane_ref, row_ref, cover_ref, taps_ref, model_ref, out_ref, x_ref, packed_ref, bank_ref, sem
):
    peers = plane_ref.shape[0]
    total = model_ref.shape[0]
    load = pltpu.make_async_copy(model_ref, x_ref.at[pl.ds(0, total), :], sem)
    load.start()
    bank_ref[...] = jnp.zeros(bank_ref.shape, F32)
    for i, row in enumerate(bank_rows(taps_ref[...])):
        for n in range(taps_ref.shape[0]):
            bank_ref[n * TAPS + i : n * TAPS + i + 1, :] = row[n : n + 1, :]
    bank = bank_ref[...].astype(BF16)
    load.wait()
    pack_slots(plane_ref, row_ref, cover_ref, tile_rows, height, rows_each, x_ref, packed_ref)
    for d in range(peers):
        out_ref[d, :rows_each, :] = packed_ref[d * rows_each : (d + 1) * rows_each, :].astype(BF16)
        out_ref[d, rows_each:, :] = bank


def update_kernel(
    bands,
    tile_rows,
    height,
    rows_each,
    last,
    plane_ref,
    row_ref,
    cover_ref,
    step_ref,
    lo_ref,
    hi_ref,
    returned_ref,
    model_ref,
    *rest,
):
    if last:
        new_ref, x_ref, back_ref, scale_ref, sem = rest
    else:
        new_ref, out_ref, x_ref, back_ref, scale_ref, sem, packed_ref = rest
    peers, capacity = plane_ref.shape
    total = model_ref.shape[0]
    planes = total // tile_rows
    load = pltpu.make_async_copy(model_ref, x_ref.at[pl.ds(0, total), :], sem)
    load.start()
    for p in range(planes):
        scale_ref[p] = step_ref[p % bands]
    for d in range(peers):
        back_ref[d * rows_each : (d + 1) * rows_each, :] = returned_ref[d].astype(F32)
    load.wait()
    place = lax.broadcasted_iota(I32, (height, LANES), 0)

    def peer(d, _):
        at = d * rows_each
        for c in range(capacity):
            p = jnp.maximum(plane_ref[d, c], 0)
            first = p * tile_rows + row_ref[d, c]
            cover = cover_ref[d, c]
            piece = jnp.where(place < cover, back_ref[pl.ds(at, height), :], 0.0)
            x_ref[pl.ds(first, height), :] = x_ref[pl.ds(first, height), :] - scale_ref[p] * piece
            at = at + cover
        return 0

    lax.fori_loop(0, peers, peer, 0)

    pos = lax.broadcasted_iota(I32, (tile_rows, LANES), 0)
    for p in range(planes):
        inside = (pos >= lo_ref[p // bands]) & (pos < hi_ref[p // bands])
        here = slice(p * tile_rows, (p + 1) * tile_rows)
        x_ref[here, :] = jnp.where(inside, jnp.maximum(x_ref[here, :], 0.0), 0.0)
    save = pltpu.make_async_copy(x_ref.at[pl.ds(0, total), :], new_ref, sem)
    save.start()
    if not last:
        pack_slots(plane_ref, row_ref, cover_ref, tile_rows, height, rows_each, x_ref, packed_ref)
        for d in range(peers):
            out_ref[d, :, :] = packed_ref[d * rows_each : (d + 1) * rows_each, :].astype(BF16)
    save.wait()


def tables_kernel(capacity, height, rows_each, slot_ref, start_ref, stop_ref, use_ref, move_ref, length_ref):
    exposures, pieces = slot_ref.shape
    slots = move_ref.shape[1]

    def clear(s, _):
        length_ref[s] = 0
        move_ref[0, s] = 0
        return 0

    lax.fori_loop(0, slots, clear, 0, unroll=8)

    def measure(e, _):
        for k in range(pieces):
            s = slot_ref[e, k]

            @pl.when(s >= 0)
            def _():
                length_ref[s] = stop_ref[e, k] - start_ref[e, k]
                move_ref[0, s] = e * height + start_ref[e, k]

        return 0

    lax.fori_loop(0, exposures, measure, 0, unroll=2)

    def lay(o, _):
        at = o * rows_each
        for c in range(capacity):
            s = o * capacity + c
            move_ref[1, s] = at
            at = at + length_ref[s]
        return 0

    lax.fori_loop(0, slots // capacity, lay, 0)

    def point(e, _):
        for k in range(pieces):
            s = slot_ref[e, k]
            live = s >= 0
            begin = move_ref[1, jnp.maximum(s, 0)]
            use_ref[2 * k, e] = jnp.where(live, height + begin - start_ref[e, k], 0)
            use_ref[2 * k + 1, e] = jnp.where(live, start_ref[e, k], height)
        return 0

    lax.fori_loop(0, exposures, point, 0, unroll=2)


def blur_kernel(
    height,
    pieces,
    batches_each,
    last,
    use_ref,
    move_ref,
    weight_ref,
    batch_ref,
    arrived_ref,
    bank_in_ref,
    seen_ref,
    *rest,
):
    if last:
        out_ref, residual_ref, rows_ref, bank_ref, result_ref, packed_ref, fwd_ref, bwd_ref, shift_ref, work_ref = rest
    else:
        out_ref, rows_ref, bank_ref, result_ref, packed_ref, fwd_ref, bwd_ref, shift_ref, work_ref = rest
    peers, rows_each, _ = out_ref.shape
    extra = bank_in_ref.shape[1]
    exposures = batch_ref.shape[0]
    each = LANES // height
    for o in range(peers):
        rows_ref[height + o * rows_each : height + (o + 1) * rows_each, :] = arrived_ref[o].astype(F32)
        bank_ref[o * extra : (o + 1) * extra, :] = bank_in_ref[o].astype(F32)
    place = lax.broadcasted_iota(I32, (height, LANES), 0)
    lane16 = lax.broadcasted_iota(I32, (height, LANES), 1)
    lane = lax.broadcasted_iota(I32, (LANES, LANES), 1)

    def fill_shifts(x):
        for i in range(TAPS):
            v = i - HALF
            if v == 0:
                moved = x
            else:
                moved = pltpu.roll(x, v % LANES, 1)
                moved = jnp.where((lane >= v) & (lane < LANES + v), moved, 0.0)
            shift_ref[i * LANES : (i + 1) * LANES, :] = moved.astype(BF16)

    def group(g, _):
        for n in range(each):
            e = g * each + n
            b = batch_ref[e]
            bank_row = lax.div(b, batches_each) * extra + lax.rem(b, batches_each) * TAPS
            own = (lane16 >= n * height) & (lane16 < (n + 1) * height)
            here = slice(n * height, (n + 1) * height)
            for i in range(TAPS):
                taps = jnp.broadcast_to(bank_ref[pl.ds(bank_row + i, 1), :], (height, LANES))
                there = slice(i * LANES, (i + 1) * LANES)
                f = pltpu.roll(taps, n * height, 1, stride=1, stride_axis=0)
                r = pltpu.roll(taps, (n * height + FLIP) % LANES, 1, stride=1, stride_axis=0)
                fwd_ref[here, there] = jnp.where(own, f, 0.0).astype(BF16)
                bwd_ref[here, there] = jnp.where(own, r, 0.0).astype(BF16)
            stamp = rows_ref[pl.ds(use_ref[0, e], height), :]
            for k in range(1, pieces):
                piece = rows_ref[pl.ds(use_ref[2 * k, e], height), :]
                stamp = jnp.where(place >= use_ref[2 * k + 1, e], piece, stamp)
            work_ref[here, :] = stamp
        fill_shifts(work_ref[...])
        predicted = jnp.dot(fwd_ref[...], shift_ref[...], preferred_element_type=F32)
        for n in range(each):
            e = g * each + n
            here = slice(n * height, (n + 1) * height)
            residual = weight_ref[e] * (predicted[here, :] - seen_ref[e].astype(F32))
            if last:
                residual_ref[e] = residual
            work_ref[here, :] = residual
        fill_shifts(work_ref[...])
        first = pl.multiple_of(g * LANES, LANES)
        result_ref[pl.ds(first, LANES), :] = jnp.dot(bwd_ref[...], shift_ref[...], preferred_element_type=F32)
        return 0

    lax.fori_loop(0, exposures // each, group, 0)

    def move(s, _):
        packed_ref[pl.ds(move_ref[1, s], height), :] = result_ref[pl.ds(move_ref[0, s], height), :]
        return 0

    lax.fori_loop(0, move_ref.shape[1], move, 0, unroll=16)
    for o in range(peers):
        out_ref[o, :, :] = packed_ref[o * rows_each : (o + 1) * rows_each, :].astype(BF16)


def body(
    model,
    exposures,
    inv_var,
    step_size,
    psf_taps,
    exp_batch,
    send_plane,
    send_row,
    send_cover,
    use_slot,
    use_start,
    use_stop,
    foot_lo,
    foot_hi,
):
    tile_count, bands, tile_rows, columns = model.shape
    count, height, _ = exposures.shape
    peers, capacity = send_plane.shape
    pieces = use_slot.shape[1]
    total = tile_count * bands * tile_rows
    rows_each = capacity * height // 2
    extra = aligned(psf_taps.shape[0] * TAPS)
    block = rows_each + extra
    assert columns == LANES and rows_each % extra == 0 and (count * height) % LANES == 0
    x = model.reshape(total, columns)

    def swap(a):
        return lax.all_to_all(a, "sky", split_axis=0, concat_axis=0, tiled=True)

    outbound = pl.pallas_call(
        functools.partial(first_send_kernel, tile_rows, height, rows_each),
        out_shape=jax.ShapeDtypeStruct((peers, block, columns), BF16),
        in_specs=[smem(), smem(), smem(), vmem(), hbm()],
        out_specs=vmem(),
        scratch_shapes=[
            pltpu.VMEM((total + height, columns), F32),
            pltpu.VMEM((peers * rows_each + height, columns), F32),
            pltpu.VMEM((extra, columns), F32),
            pltpu.SemaphoreType.DMA,
        ],
        compiler_params=params(),
        name="first_send",
    )(send_plane, send_row, send_cover, psf_taps, x)
    arrived = swap(outbound)
    use, move = pl.pallas_call(
        functools.partial(tables_kernel, capacity, height, rows_each),
        out_shape=(
            jax.ShapeDtypeStruct((2 * pieces, count), I32),
            jax.ShapeDtypeStruct((2, peers * capacity), I32),
        ),
        in_specs=[smem(), smem(), smem()],
        out_specs=(smem(), smem()),
        scratch_shapes=[pltpu.SMEM((peers * capacity,), I32)],
        cost_estimate=pl.CostEstimate(flops=4_000_000, bytes_accessed=8_000_000, transcendentals=0),
        name="tables",
    )(use_slot, use_start, use_stop)
    with_bank = arrived
    for sweep in range(ITERS):
        last = sweep == ITERS - 1
        rows_shape = jax.ShapeDtypeStruct((peers, rows_each, columns), BF16)
        outs = pl.pallas_call(
            functools.partial(blur_kernel, height, pieces, psf_taps.shape[0], last),
            grid=(1,),
            out_shape=(rows_shape, jax.ShapeDtypeStruct(exposures.shape, F32)) if last else rows_shape,
            in_specs=[
                smem(),
                smem(),
                smem(),
                smem(),
                pl.BlockSpec((peers, rows_each, columns), lambda i: (0, 0, 0)),
                pl.BlockSpec((peers, extra, columns), lambda i: (0, rows_each // extra, 0)),
                vmem(),
            ],
            out_specs=(vmem(), vmem()) if last else vmem(),
            scratch_shapes=[
                pltpu.VMEM((peers * rows_each + 2 * height, columns), F32),
                pltpu.VMEM((peers * extra, columns), F32),
                pltpu.VMEM((count * height + height, columns), F32),
                pltpu.VMEM((peers * rows_each + height, columns), F32),
                pltpu.VMEM((LANES, TAPS * LANES), BF16),
                pltpu.VMEM((LANES, TAPS * LANES), BF16),
                pltpu.VMEM((TAPS * LANES, columns), BF16),
                pltpu.VMEM((LANES, columns), F32),
            ],
            compiler_params=params(),
            name="blur",
        )(use, move, inv_var, exp_batch, arrived, with_bank, exposures)
        outgoing = outs[0] if last else outs
        returned = swap(outgoing)
        new_shape = jax.ShapeDtypeStruct((total, columns), F32)
        scratch = [
            pltpu.VMEM((total + height, columns), F32),
            pltpu.VMEM((peers * rows_each + height, columns), F32),
            pltpu.SMEM((tile_count * bands,), F32),
            pltpu.SemaphoreType.DMA,
        ]
        if not last:
            scratch.append(pltpu.VMEM((peers * rows_each + height, columns), F32))
        res = pl.pallas_call(
            functools.partial(update_kernel, bands, tile_rows, height, rows_each, last),
            out_shape=new_shape if last else (new_shape, rows_shape),
            in_specs=[smem()] * 6 + [vmem(), hbm()],
            out_specs=hbm() if last else (hbm(), vmem()),
            scratch_shapes=scratch,
            compiler_params=params(),
            name="update",
        )(send_plane, send_row, send_cover, step_size, foot_lo, foot_hi, returned, x)
        if last:
            x = res
        else:
            x, outbound = res
            arrived = swap(outbound)
    return (x.reshape(model.shape), outs[1])


def solution(mesh):
    both = ("groups", "sky")
    return jax.shard_map(
        body,
        mesh=mesh,
        in_specs=(
            P(both, None, None, None),
            P(both, None, None),
            P(both),
            P(),
            P(both, None),
            P(both),
            P(both, None),
            P(both, None),
            P(both, None),
            P(both, None),
            P(both, None),
            P(both, None),
            P(both),
            P(both),
        ),
        out_specs=(P(both, None, None, None), P(both, None, None)),
        check_vma=False,
    )
```

```python
import functools

import jax
import jax.numpy as jnp
from jax import lax
from jax.experimental import pallas as pl
from jax.experimental.pallas import tpu as pltpu
from jax.sharding import PartitionSpec as P

NPSF = 4
TAPS = 7
ITERS = 2
LANES = 128
HALF = TAPS // 2
FLIP = 64
F32 = jnp.float32
BF16 = jnp.bfloat16
I32 = jnp.int32
VMEM_BYTES = 60 * 1024 * 1024

smem = lambda: pl.BlockSpec(memory_space=pltpu.SMEM)
vmem = lambda: pl.BlockSpec(memory_space=pltpu.VMEM)
hbm = lambda: pl.BlockSpec(memory_space=pl.ANY)


def params():
    return pltpu.CompilerParams(vmem_limit_bytes=VMEM_BYTES)


def aligned(rows):
    return -(-rows // 16) * 16


def pack_slots(plane_ref, row_ref, cover_ref, tile_rows, height, rows_each, x_ref, packed_ref):
    peers, capacity = plane_ref.shape

    def peer(d, _):
        at = d * rows_each
        for c in range(capacity):
            first = jnp.maximum(plane_ref[d, c], 0) * tile_rows + row_ref[d, c]
            packed_ref[pl.ds(at, height), :] = x_ref[pl.ds(first, height), :]
            at = at + cover_ref[d, c]
        return 0

    lax.fori_loop(0, peers, peer, 0)


def bank_rows(taps):
    hp = lax.Precision.HIGHEST
    width = taps.shape[1]

    def grid(columns):
        return (
            lax.broadcasted_iota(I32, (width, columns), 0),
            lax.broadcasted_iota(I32, (width, columns), 1),
        )

    k, l = grid(width)
    total = jnp.dot(taps, (k // TAPS == l // TAPS).astype(F32), precision=hp, preferred_element_type=F32)
    unit = taps / total
    k, l = grid(NPSF * LANES)
    j, l = l // LANES, (l + HALF) % LANES
    wanted = jnp.where(l < TAPS, j * TAPS + TAPS - 1 - l, -1)
    wanted = jnp.where((l >= FLIP) & (l < FLIP + TAPS), j * TAPS + l - FLIP, wanted)
    row_part = jnp.dot(unit, (k == wanted).astype(F32), precision=hp, preferred_element_type=F32)
    k, l = grid(NPSF * TAPS * LANES)
    ji, l = l // LANES, (l + HALF) % LANES
    j, i = ji // TAPS, ji % TAPS
    wanted = NPSF * TAPS + j * TAPS + jnp.where(l < FLIP, i, TAPS - 1 - i)
    col_part = jnp.dot(unit, (k == wanted).astype(F32), precision=hp, preferred_element_type=F32)
    rows = []
    for i in range(TAPS):
        total = 0.0
        for j in range(NPSF):
            at = (j * TAPS + i) * LANES
            total = total + row_part[:, j * LANES : (j + 1) * LANES] * col_part[:, at : at + LANES]
        rows.append(total * (1.0 / NPSF))
    return rows


def first_send_kernel(
    tile_rows, height, rows_each, plane_ref, row_ref, cover_ref, taps_ref, model_ref, out_ref, x_ref, packed_ref, bank_ref, sem
):
    peers = plane_ref.shape[0]
    total = model_ref.shape[0]
    load = pltpu.make_async_copy(model_ref, x_ref.at[pl.ds(0, total), :], sem)
    load.start()
    bank_ref[...] = jnp.zeros(bank_ref.shape, F32)
    for i, row in enumerate(bank_rows(taps_ref[...])):
        for n in range(taps_ref.shape[0]):
            bank_ref[n * TAPS + i : n * TAPS + i + 1, :] = row[n : n + 1, :]
    bank = bank_ref[...].astype(BF16)
    load.wait()
    pack_slots(plane_ref, row_ref, cover_ref, tile_rows, height, rows_each, x_ref, packed_ref)
    for d in range(peers):
        out_ref[d, :rows_each, :] = packed_ref[d * rows_each : (d + 1) * rows_each, :].astype(BF16)
        out_ref[d, rows_each:, :] = bank


def update_kernel(
    bands,
    tile_rows,
    height,
    rows_each,
    last,
    plane_ref,
    row_ref,
    cover_ref,
    step_ref,
    lo_ref,
    hi_ref,
    returned_ref,
    model_ref,
    *rest,
):
    if last:
        new_ref, x_ref, back_ref, scale_ref, sem = rest
    else:
        new_ref, out_ref, x_ref, back_ref, scale_ref, sem, packed_ref = rest
    peers, capacity = plane_ref.shape
    total = model_ref.shape[0]
    planes = total // tile_rows
    load = pltpu.make_async_copy(model_ref, x_ref.at[pl.ds(0, total), :], sem)
    load.start()
    for p in range(planes):
        scale_ref[p] = step_ref[p % bands]
    for d in range(peers):
        back_ref[d * rows_each : (d + 1) * rows_each, :] = returned_ref[d].astype(F32)
    load.wait()
    place = lax.broadcasted_iota(I32, (height, LANES), 0)

    def peer(d, _):
        at = d * rows_each
        for c in range(capacity):
            p = jnp.maximum(plane_ref[d, c], 0)
            first = p * tile_rows + row_ref[d, c]
            cover = cover_ref[d, c]
            piece = jnp.where(place < cover, back_ref[pl.ds(at, height), :], 0.0)
            x_ref[pl.ds(first, height), :] = x_ref[pl.ds(first, height), :] - scale_ref[p] * piece
            at = at + cover
        return 0

    lax.fori_loop(0, peers, peer, 0)

    pos = lax.broadcasted_iota(I32, (tile_rows, LANES), 0)
    for p in range(planes):
        inside = (pos >= lo_ref[p // bands]) & (pos < hi_ref[p // bands])
        here = slice(p * tile_rows, (p + 1) * tile_rows)
        x_ref[here, :] = jnp.where(inside, jnp.maximum(x_ref[here, :], 0.0), 0.0)
    save = pltpu.make_async_copy(x_ref.at[pl.ds(0, total), :], new_ref, sem)
    save.start()
    if not last:
        pack_slots(plane_ref, row_ref, cover_ref, tile_rows, height, rows_each, x_ref, packed_ref)
        for d in range(peers):
            out_ref[d, :, :] = packed_ref[d * rows_each : (d + 1) * rows_each, :].astype(BF16)
    save.wait()


def tables_kernel(capacity, height, rows_each, slot_ref, start_ref, stop_ref, use_ref, move_ref, length_ref):
    exposures, pieces = slot_ref.shape
    slots = move_ref.shape[1]

    def clear(s, _):
        length_ref[s] = 0
        move_ref[0, s] = 0
        return 0

    lax.fori_loop(0, slots, clear, 0, unroll=8)

    def measure(e, _):
        for k in range(pieces):
            s = slot_ref[e, k]

            @pl.when(s >= 0)
            def _():
                length_ref[s] = stop_ref[e, k] - start_ref[e, k]
                move_ref[0, s] = e * height + start_ref[e, k]

        return 0

    lax.fori_loop(0, exposures, measure, 0, unroll=2)

    def lay(o, _):
        at = o * rows_each
        for c in range(capacity):
            s = o * capacity + c
            move_ref[1, s] = at
            at = at + length_ref[s]
        return 0

    lax.fori_loop(0, slots // capacity, lay, 0)

    def point(e, _):
        for k in range(pieces):
            s = slot_ref[e, k]
            live = s >= 0
            begin = move_ref[1, jnp.maximum(s, 0)]
            use_ref[2 * k, e] = jnp.where(live, height + begin - start_ref[e, k], 0)
            use_ref[2 * k + 1, e] = jnp.where(live, start_ref[e, k], height)
        return 0

    lax.fori_loop(0, exposures, point, 0, unroll=2)


def blur_kernel(
    height,
    pieces,
    batches_each,
    last,
    use_ref,
    move_ref,
    weight_ref,
    batch_ref,
    arrived_ref,
    bank_in_ref,
    seen_ref,
    *rest,
):
    if last:
        out_ref, residual_ref, rows_ref, bank_ref, result_ref, packed_ref, fwd_ref, bwd_ref, shift_ref, work_ref = rest
    else:
        out_ref, rows_ref, bank_ref, result_ref, packed_ref, fwd_ref, bwd_ref, shift_ref, work_ref = rest
    peers, rows_each, _ = out_ref.shape
    extra = bank_in_ref.shape[1]
    exposures = batch_ref.shape[0]
    each = LANES // height
    abreast = fwd_ref.shape[0]
    for o in range(peers):
        rows_ref[height + o * rows_each : height + (o + 1) * rows_each, :] = arrived_ref[o].astype(F32)
        bank_ref[o * extra : (o + 1) * extra, :] = bank_in_ref[o].astype(F32)
    place = lax.broadcasted_iota(I32, (height, LANES), 0)
    lane16 = lax.broadcasted_iota(I32, (height, LANES), 1)
    lane = lax.broadcasted_iota(I32, (LANES, LANES), 1)

    def fill_shifts(q, x):
        for i in range(TAPS):
            v = i - HALF
            if v == 0:
                moved = x
            else:
                moved = pltpu.roll(x, v % LANES, 1)
                moved = jnp.where((lane >= v) & (lane < LANES + v), moved, 0.0)
            shift_ref[q, i * LANES : (i + 1) * LANES, :] = moved.astype(BF16)

    def groups(step, _):
        for q in range(abreast):
            g = step * abreast + q
            for n in range(each):
                e = g * each + n
                b = batch_ref[e]
                bank_row = lax.div(b, batches_each) * extra + lax.rem(b, batches_each) * TAPS
                own = (lane16 >= n * height) & (lane16 < (n + 1) * height)
                here = slice(n * height, (n + 1) * height)
                for i in range(TAPS):
                    taps = jnp.broadcast_to(bank_ref[pl.ds(bank_row + i, 1), :], (height, LANES))
                    there = slice(i * LANES, (i + 1) * LANES)
                    f = pltpu.roll(taps, n * height, 1, stride=1, stride_axis=0)
                    r = pltpu.roll(taps, (n * height + FLIP) % LANES, 1, stride=1, stride_axis=0)
                    fwd_ref[q, here, there] = jnp.where(own, f, 0.0).astype(BF16)
                    bwd_ref[q, here, there] = jnp.where(own, r, 0.0).astype(BF16)
                stamp = rows_ref[pl.ds(use_ref[0, e], height), :]
                for k in range(1, pieces):
                    piece = rows_ref[pl.ds(use_ref[2 * k, e], height), :]
                    stamp = jnp.where(place >= use_ref[2 * k + 1, e], piece, stamp)
                work_ref[q, here, :] = stamp
        for q in range(abreast):
            fill_shifts(q, work_ref[q])
        predicted = [
            jnp.dot(fwd_ref[q], shift_ref[q], preferred_element_type=F32) for q in range(abreast)
        ]
        for q in range(abreast):
            for n in range(each):
                e = (step * abreast + q) * each + n
                here = slice(n * height, (n + 1) * height)
                residual = weight_ref[e] * (predicted[q][here, :] - seen_ref[e].astype(F32))
                if last:
                    residual_ref[e] = residual
                work_ref[q, here, :] = residual
        for q in range(abreast):
            fill_shifts(q, work_ref[q])
        for q in range(abreast):
            first = pl.multiple_of((step * abreast + q) * LANES, LANES)
            result_ref[pl.ds(first, LANES), :] = jnp.dot(bwd_ref[q], shift_ref[q], preferred_element_type=F32)
        return 0

    lax.fori_loop(0, exposures // (each * abreast), groups, 0)

    def move(s, _):
        packed_ref[pl.ds(move_ref[1, s], height), :] = result_ref[pl.ds(move_ref[0, s], height), :]
        return 0

    lax.fori_loop(0, move_ref.shape[1], move, 0, unroll=16)
    for o in range(peers):
        out_ref[o, :, :] = packed_ref[o * rows_each : (o + 1) * rows_each, :].astype(BF16)


def body(
    model,
    exposures,
    inv_var,
    step_size,
    psf_taps,
    exp_batch,
    send_plane,
    send_row,
    send_cover,
    use_slot,
    use_start,
    use_stop,
    foot_lo,
    foot_hi,
):
    tile_count, bands, tile_rows, columns = model.shape
    count, height, _ = exposures.shape
    peers, capacity = send_plane.shape
    pieces = use_slot.shape[1]
    total = tile_count * bands * tile_rows
    rows_each = capacity * height // 2
    extra = aligned(psf_taps.shape[0] * TAPS)
    block = rows_each + extra
    assert columns == LANES and rows_each % extra == 0 and (count * height) % LANES == 0
    group_count = count * height // LANES
    abreast = max(n for n in (1, 2, 4) if group_count % n == 0)
    x = model.reshape(total, columns)

    def swap(a):
        return lax.all_to_all(a, "sky", split_axis=0, concat_axis=0, tiled=True)

    outbound = pl.pallas_call(
        functools.partial(first_send_kernel, tile_rows, height, rows_each),
        out_shape=jax.ShapeDtypeStruct((peers, block, columns), BF16),
        in_specs=[smem(), smem(), smem(), vmem(), hbm()],
        out_specs=vmem(),
        scratch_shapes=[
            pltpu.VMEM((total + height, columns), F32),
            pltpu.VMEM((peers * rows_each + height, columns), F32),
            pltpu.VMEM((extra, columns), F32),
            pltpu.SemaphoreType.DMA,
        ],
        compiler_params=params(),
        name="first_send",
    )(send_plane, send_row, send_cover, psf_taps, x)
    arrived = swap(outbound)
    use, move = pl.pallas_call(
        functools.partial(tables_kernel, capacity, height, rows_each),
        out_shape=(
            jax.ShapeDtypeStruct((2 * pieces, count), I32),
            jax.ShapeDtypeStruct((2, peers * capacity), I32),
        ),
        in_specs=[smem(), smem(), smem()],
        out_specs=(smem(), smem()),
        scratch_shapes=[pltpu.SMEM((peers * capacity,), I32)],
        cost_estimate=pl.CostEstimate(flops=4_000_000, bytes_accessed=8_000_000, transcendentals=0),
        name="tables",
    )(use_slot, use_start, use_stop)
    with_bank = arrived
    for sweep in range(ITERS):
        last = sweep == ITERS - 1
        rows_shape = jax.ShapeDtypeStruct((peers, rows_each, columns), BF16)
        outs = pl.pallas_call(
            functools.partial(blur_kernel, height, pieces, psf_taps.shape[0], last),
            grid=(1,),
            out_shape=(rows_shape, jax.ShapeDtypeStruct(exposures.shape, F32)) if last else rows_shape,
            in_specs=[
                smem(),
                smem(),
                smem(),
                smem(),
                pl.BlockSpec((peers, rows_each, columns), lambda i: (0, 0, 0)),
                pl.BlockSpec((peers, extra, columns), lambda i: (0, rows_each // extra, 0)),
                vmem(),
            ],
            out_specs=(vmem(), vmem()) if last else vmem(),
            scratch_shapes=[
                pltpu.VMEM((peers * rows_each + 2 * height, columns), F32),
                pltpu.VMEM((peers * extra, columns), F32),
                pltpu.VMEM((count * height + height, columns), F32),
                pltpu.VMEM((peers * rows_each + height, columns), F32),
                pltpu.VMEM((abreast, LANES, TAPS * LANES), BF16),
                pltpu.VMEM((abreast, LANES, TAPS * LANES), BF16),
                pltpu.VMEM((abreast, TAPS * LANES, columns), BF16),
                pltpu.VMEM((abreast, LANES, columns), F32),
            ],
            compiler_params=params(),
            name="blur",
        )(use, move, inv_var, exp_batch, arrived, with_bank, exposures)
        outgoing = outs[0] if last else outs
        returned = swap(outgoing)
        new_shape = jax.ShapeDtypeStruct((total, columns), F32)
        scratch = [
            pltpu.VMEM((total + height, columns), F32),
            pltpu.VMEM((peers * rows_each + height, columns), F32),
            pltpu.SMEM((tile_count * bands,), F32),
            pltpu.SemaphoreType.DMA,
        ]
        if not last:
            scratch.append(pltpu.VMEM((peers * rows_each + height, columns), F32))
        res = pl.pallas_call(
            functools.partial(update_kernel, bands, tile_rows, height, rows_each, last),
            out_shape=new_shape if last else (new_shape, rows_shape),
            in_specs=[smem()] * 6 + [vmem(), hbm()],
            out_specs=hbm() if last else (hbm(), vmem()),
            scratch_shapes=scratch,
            compiler_params=params(),
            name="update",
        )(send_plane, send_row, send_cover, step_size, foot_lo, foot_hi, returned, x)
        if last:
            x = res
        else:
            x, outbound = res
            arrived = swap(outbound)
    return (x.reshape(model.shape), outs[1])


def solution(mesh):
    both = ("groups", "sky")
    return jax.shard_map(
        body,
        mesh=mesh,
        in_specs=(
            P(both, None, None, None),
            P(both, None, None),
            P(both),
            P(),
            P(both, None),
            P(both),
            P(both, None),
            P(both, None),
            P(both, None),
            P(both, None),
            P(both, None),
            P(both, None),
            P(both),
            P(both),
        ),
        out_specs=(P(both, None, None, None), P(both, None, None)),
        check_vma=False,
    )
```

```python
import functools

import jax
import jax.numpy as jnp
from jax import lax
from jax.experimental import pallas as pl
from jax.experimental.pallas import tpu as pltpu
from jax.sharding import PartitionSpec as P

NPSF = 4
TAPS = 7
ITERS = 2
LANES = 128
HALF = TAPS // 2
FLIP = 64
F32 = jnp.float32
BF16 = jnp.bfloat16
I32 = jnp.int32
VMEM_BYTES = 24 * 1024 * 1024

smem = lambda: pl.BlockSpec(memory_space=pltpu.SMEM)
vmem = lambda: pl.BlockSpec(memory_space=pltpu.VMEM)
hbm = lambda: pl.BlockSpec(memory_space=pl.ANY)


def params(share=1.0):
    return pltpu.CompilerParams(vmem_limit_bytes=int(share * VMEM_BYTES))


def each_peer(peers, refs):
    if len(refs) == 1:
        return [(o, refs[0].at[o]) for o in range(peers)]
    me = lax.axis_index("sky")
    return [(me ^ k, ref) for k, ref in enumerate(refs)]


def rows_of(o, count, offset=0):
    return pl.ds(pl.multiple_of(o * count + offset, 16), count)


def aligned(rows):
    return -(-rows // 16) * 16


def pack_slots(plane_ref, row_ref, cover_ref, tile_rows, height, rows_each, x_ref, packed_ref):
    peers, capacity = plane_ref.shape

    def peer(d, _):
        at = d * rows_each
        for c in range(capacity):
            first = jnp.maximum(plane_ref[d, c], 0) * tile_rows + row_ref[d, c]
            packed_ref[pl.ds(at, height), :] = x_ref[pl.ds(first, height), :]
            at = at + cover_ref[d, c]
        return 0

    lax.fori_loop(0, peers, peer, 0)


def bank_rows(taps):
    hp = lax.Precision.HIGHEST
    width = taps.shape[1]

    def grid(columns):
        return (
            lax.broadcasted_iota(I32, (width, columns), 0),
            lax.broadcasted_iota(I32, (width, columns), 1),
        )

    k, l = grid(width)
    total = jnp.dot(taps, (k // TAPS == l // TAPS).astype(F32), precision=hp, preferred_element_type=F32)
    unit = taps / total
    k, l = grid(NPSF * LANES)
    j, l = l // LANES, (l + HALF) % LANES
    wanted = jnp.where(l < TAPS, j * TAPS + TAPS - 1 - l, -1)
    wanted = jnp.where((l >= FLIP) & (l < FLIP + TAPS), j * TAPS + l - FLIP, wanted)
    row_part = jnp.dot(unit, (k == wanted).astype(F32), precision=hp, preferred_element_type=F32)
    k, l = grid(NPSF * TAPS * LANES)
    ji, l = l // LANES, (l + HALF) % LANES
    j, i = ji // TAPS, ji % TAPS
    wanted = NPSF * TAPS + j * TAPS + jnp.where(l < FLIP, i, TAPS - 1 - i)
    col_part = jnp.dot(unit, (k == wanted).astype(F32), precision=hp, preferred_element_type=F32)
    rows = []
    for i in range(TAPS):
        total = 0.0
        for j in range(NPSF):
            at = (j * TAPS + i) * LANES
            total = total + row_part[:, j * LANES : (j + 1) * LANES] * col_part[:, at : at + LANES]
        rows.append(total * (1.0 / NPSF))
    return rows


def first_send_kernel(
    tile_rows, height, rows_each, plane_ref, row_ref, cover_ref, taps_ref, model_ref, *rest
):
    *out_refs, x_ref, packed_ref, bank_ref, sem = rest
    peers = plane_ref.shape[0]
    total = model_ref.shape[0]
    load = pltpu.make_async_copy(model_ref, x_ref.at[pl.ds(0, total), :], sem)
    load.start()
    bank_ref[...] = jnp.zeros(bank_ref.shape, F32)
    for i, row in enumerate(bank_rows(taps_ref[...])):
        for n in range(taps_ref.shape[0]):
            bank_ref[n * TAPS + i : n * TAPS + i + 1, :] = row[n : n + 1, :]
    bank = bank_ref[...].astype(BF16)
    load.wait()
    pack_slots(plane_ref, row_ref, cover_ref, tile_rows, height, rows_each, x_ref, packed_ref)
    for d, out_ref in each_peer(peers, out_refs):
        out_ref[:rows_each, :] = packed_ref[rows_of(d, rows_each), :].astype(BF16)
        out_ref[rows_each:, :] = bank


def update_kernel(
    bands,
    tile_rows,
    height,
    rows_each,
    parts,
    last,
    plane_ref,
    row_ref,
    cover_ref,
    step_ref,
    lo_ref,
    hi_ref,
    model_ref,
    *rest,
):
    returned_refs, rest = rest[:parts], rest[parts:]
    if last:
        new_ref, x_ref, back_ref, scale_ref, sem = rest
    else:
        new_ref, *out_refs, x_ref, back_ref, scale_ref, sem, packed_ref = rest
    peers, capacity = plane_ref.shape
    total = model_ref.shape[0]
    planes = total // tile_rows
    load = pltpu.make_async_copy(model_ref, x_ref.at[pl.ds(0, total), :], sem)
    load.start()
    for p in range(planes):
        scale_ref[p] = step_ref[p % bands]
    for d, returned_ref in each_peer(peers, returned_refs):
        back_ref[rows_of(d, rows_each), :] = returned_ref[...].astype(F32)
    load.wait()
    place = lax.broadcasted_iota(I32, (height, LANES), 0)

    def peer(d, _):
        at = d * rows_each
        for c in range(capacity):
            p = jnp.maximum(plane_ref[d, c], 0)
            first = p * tile_rows + row_ref[d, c]
            cover = cover_ref[d, c]
            piece = jnp.where(place < cover, back_ref[pl.ds(at, height), :], 0.0)
            x_ref[pl.ds(first, height), :] = x_ref[pl.ds(first, height), :] - scale_ref[p] * piece
            at = at + cover
        return 0

    lax.fori_loop(0, peers, peer, 0)

    pos = lax.broadcasted_iota(I32, (tile_rows, LANES), 0)
    for p in range(planes):
        inside = (pos >= lo_ref[p // bands]) & (pos < hi_ref[p // bands])
        here = slice(p * tile_rows, (p + 1) * tile_rows)
        x_ref[here, :] = jnp.where(inside, jnp.maximum(x_ref[here, :], 0.0), 0.0)
    save = pltpu.make_async_copy(x_ref.at[pl.ds(0, total), :], new_ref, sem)
    save.start()
    if not last:
        pack_slots(plane_ref, row_ref, cover_ref, tile_rows, height, rows_each, x_ref, packed_ref)
        for d, out_ref in each_peer(peers, out_refs):
            out_ref[...] = packed_ref[rows_of(d, rows_each), :].astype(BF16)
    save.wait()


def tables_kernel(capacity, height, rows_each, slot_ref, start_ref, stop_ref, use_ref, move_ref, length_ref):
    exposures, pieces = slot_ref.shape
    slots = move_ref.shape[1]

    def clear(s, _):
        length_ref[s] = 0
        move_ref[0, s] = 0
        return 0

    lax.fori_loop(0, slots, clear, 0, unroll=8)

    def measure(e, _):
        for k in range(pieces):
            s = slot_ref[e, k]

            @pl.when(s >= 0)
            def _():
                length_ref[s] = stop_ref[e, k] - start_ref[e, k]
                move_ref[0, s] = e * height + start_ref[e, k]

        return 0

    lax.fori_loop(0, exposures, measure, 0, unroll=2)

    def lay(o, _):
        at = o * rows_each
        for c in range(capacity):
            s = o * capacity + c
            move_ref[1, s] = at
            at = at + length_ref[s]
        return 0

    lax.fori_loop(0, slots // capacity, lay, 0)

    def point(e, _):
        for k in range(pieces):
            s = slot_ref[e, k]
            live = s >= 0
            begin = move_ref[1, jnp.maximum(s, 0)]
            use_ref[2 * k, e] = jnp.where(live, height + begin - start_ref[e, k], 0)
            use_ref[2 * k + 1, e] = jnp.where(live, start_ref[e, k], height)
        return 0

    lax.fori_loop(0, exposures, point, 0, unroll=2)


def blur_kernel(
    height,
    pieces,
    batches_each,
    peers,
    parts,
    last,
    use_ref,
    move_ref,
    weight_ref,
    batch_ref,
    seen_ref,
    *rest,
):
    arrived_refs, bank_in_refs, out_refs, rest = rest[:parts], rest[parts : 2 * parts], rest[2 * parts : 3 * parts], rest[3 * parts :]
    if last:
        residual_ref, *rest = rest
    rows_ref, bank_ref, result_ref, packed_ref, fwd_ref, bwd_ref, shift_ref, work_ref = rest
    rows_each = out_refs[0].shape[-2]
    extra = bank_in_refs[0].shape[-2]
    exposures = batch_ref.shape[0]
    each = LANES // height
    abreast = fwd_ref.shape[0]
    for o, arrived_ref in each_peer(peers, arrived_refs):
        rows_ref[rows_of(o, rows_each, height), :] = arrived_ref[...].astype(F32)
    for o, bank_in_ref in each_peer(peers, bank_in_refs):
        bank_ref[rows_of(o, extra), :] = bank_in_ref[...].astype(F32)
    place = lax.broadcasted_iota(I32, (height, LANES), 0)
    lane16 = lax.broadcasted_iota(I32, (height, LANES), 1)
    lane = lax.broadcasted_iota(I32, (LANES, LANES), 1)

    def fill_shifts(q, x):
        for i in range(TAPS):
            v = i - HALF
            if v == 0:
                moved = x
            else:
                moved = pltpu.roll(x, v % LANES, 1)
                moved = jnp.where((lane >= v) & (lane < LANES + v), moved, 0.0)
            shift_ref[q, i * LANES : (i + 1) * LANES, :] = moved.astype(BF16)

    def groups(step, _):
        for q in range(abreast):
            g = step * abreast + q
            for n in range(each):
                e = g * each + n
                b = batch_ref[e]
                bank_row = lax.div(b, batches_each) * extra + lax.rem(b, batches_each) * TAPS
                own = (lane16 >= n * height) & (lane16 < (n + 1) * height)
                here = slice(n * height, (n + 1) * height)
                for i in range(TAPS):
                    taps = jnp.broadcast_to(bank_ref[pl.ds(bank_row + i, 1), :], (height, LANES))
                    there = slice(i * LANES, (i + 1) * LANES)
                    f = pltpu.roll(taps, n * height, 1, stride=1, stride_axis=0)
                    r = pltpu.roll(taps, (n * height + FLIP) % LANES, 1, stride=1, stride_axis=0)
                    fwd_ref[q, here, there] = jnp.where(own, f, 0.0).astype(BF16)
                    bwd_ref[q, here, there] = jnp.where(own, r, 0.0).astype(BF16)
                stamp = rows_ref[pl.ds(use_ref[0, e], height), :]
                for k in range(1, pieces):
                    piece = rows_ref[pl.ds(use_ref[2 * k, e], height), :]
                    stamp = jnp.where(place >= use_ref[2 * k + 1, e], piece, stamp)
                work_ref[q, here, :] = stamp
        for q in range(abreast):
            fill_shifts(q, work_ref[q])
        predicted = [
            jnp.dot(fwd_ref[q], shift_ref[q], preferred_element_type=F32) for q in range(abreast)
        ]
        for q in range(abreast):
            for n in range(each):
                e = (step * abreast + q) * each + n
                here = slice(n * height, (n + 1) * height)
                residual = weight_ref[e] * (predicted[q][here, :] - seen_ref[e].astype(F32))
                if last:
                    residual_ref[e] = residual
                work_ref[q, here, :] = residual
        for q in range(abreast):
            fill_shifts(q, work_ref[q])
        for q in range(abreast):
            first = pl.multiple_of((step * abreast + q) * LANES, LANES)
            result_ref[pl.ds(first, LANES), :] = jnp.dot(bwd_ref[q], shift_ref[q], preferred_element_type=F32)
        return 0

    lax.fori_loop(0, exposures // (each * abreast), groups, 0)

    def move(s, _):
        packed_ref[pl.ds(move_ref[1, s], height), :] = result_ref[pl.ds(move_ref[0, s], height), :]
        return 0

    lax.fori_loop(0, move_ref.shape[1], move, 0, unroll=16)
    for o, out_ref in each_peer(peers, out_refs):
        out_ref[...] = packed_ref[rows_of(o, rows_each), :].astype(BF16)


def body(
    model,
    exposures,
    inv_var,
    step_size,
    psf_taps,
    exp_batch,
    send_plane,
    send_row,
    send_cover,
    use_slot,
    use_start,
    use_stop,
    foot_lo,
    foot_hi,
):
    tile_count, bands, tile_rows, columns = model.shape
    count, height, _ = exposures.shape
    peers, capacity = send_plane.shape
    pieces = use_slot.shape[1]
    total = tile_count * bands * tile_rows
    rows_each = capacity * height // 2
    extra = aligned(psf_taps.shape[0] * TAPS)
    block = rows_each + extra
    assert columns == LANES and rows_each % extra == 0 and (count * height) % LANES == 0
    group_count = count * height // LANES
    abreast = max(n for n in (1, 2, 4) if group_count % n == 0)
    x = model.reshape(total, columns)

    paired = peers <= 16 and peers & (peers - 1) == 0
    parts = peers if paired else 1

    def part_shapes(rows):
        if paired:
            return [jax.ShapeDtypeStruct((rows, columns), BF16)] * parts
        return [jax.ShapeDtypeStruct((peers, rows, columns), BF16)]

    def part_specs(rows, at=0):
        if paired:
            return [pl.BlockSpec((rows, columns), lambda i: (at, 0))] * parts
        return [pl.BlockSpec((peers, rows, columns), lambda i: (0, at, 0))]

    def swap(blocks):
        if not paired:
            return [lax.all_to_all(blocks[0], "sky", split_axis=0, concat_axis=0, tiled=True)]
        moved = {0: blocks[0]}
        for k in range(peers - 1, 0, -1):
            moved[k] = lax.ppermute(blocks[k], "sky", [(i, i ^ k) for i in range(peers)])
        return [moved[k] for k in range(peers)]

    outbound = pl.pallas_call(
        functools.partial(first_send_kernel, tile_rows, height, rows_each),
        out_shape=part_shapes(block),
        in_specs=[smem(), smem(), smem(), vmem(), hbm()],
        out_specs=[vmem()] * parts,
        scratch_shapes=[
            pltpu.VMEM((total + height, columns), F32),
            pltpu.VMEM((peers * rows_each + height, columns), F32),
            pltpu.VMEM((extra, columns), F32),
            pltpu.SemaphoreType.DMA,
        ],
        compiler_params=params(2.5),
        name="first_send",
    )(send_plane, send_row, send_cover, psf_taps, x)
    arrived = swap(outbound)
    use, move = pl.pallas_call(
        functools.partial(tables_kernel, capacity, height, rows_each),
        out_shape=(
            jax.ShapeDtypeStruct((2 * pieces, count), I32),
            jax.ShapeDtypeStruct((2, peers * capacity), I32),
        ),
        in_specs=[smem(), smem(), smem()],
        out_specs=(smem(), smem()),
        scratch_shapes=[pltpu.SMEM((peers * capacity,), I32)],
        cost_estimate=pl.CostEstimate(flops=4_000_000, bytes_accessed=8_000_000, transcendentals=0),
        name="tables",
    )(use_slot, use_start, use_stop)
    with_bank = arrived
    for sweep in range(ITERS):
        last = sweep == ITERS - 1
        residual_shape = [jax.ShapeDtypeStruct(exposures.shape, F32)] if last else []
        outs = pl.pallas_call(
            functools.partial(blur_kernel, height, pieces, psf_taps.shape[0], peers, parts, last),
            grid=(1,),
            out_shape=part_shapes(rows_each) + residual_shape,
            in_specs=[smem()] * 4 + [vmem()] + part_specs(rows_each) + part_specs(extra, rows_each // extra),
            out_specs=[vmem()] * (parts + len(residual_shape)),
            scratch_shapes=[
                pltpu.VMEM((peers * rows_each + 2 * height, columns), F32),
                pltpu.VMEM((peers * extra, columns), F32),
                pltpu.VMEM((count * height + height, columns), F32),
                pltpu.VMEM((peers * rows_each + height, columns), F32),
                pltpu.VMEM((abreast, LANES, TAPS * LANES), BF16),
                pltpu.VMEM((abreast, LANES, TAPS * LANES), BF16),
                pltpu.VMEM((abreast, TAPS * LANES, columns), BF16),
                pltpu.VMEM((abreast, LANES, columns), F32),
            ],
            compiler_params=params(),
            name="blur",
        )(use, move, inv_var, exp_batch, exposures, *arrived, *with_bank)
        returned = swap(outs[:parts])
        scratch = [
            pltpu.VMEM((total + height, columns), F32),
            pltpu.VMEM((peers * rows_each + height, columns), F32),
            pltpu.SMEM((tile_count * bands,), F32),
            pltpu.SemaphoreType.DMA,
        ]
        sends = 0 if last else parts
        if not last:
            scratch.append(pltpu.VMEM((peers * rows_each + height, columns), F32))
        x, *outbound = pl.pallas_call(
            functools.partial(update_kernel, bands, tile_rows, height, rows_each, parts, last),
            out_shape=[jax.ShapeDtypeStruct((total, columns), F32)] + part_shapes(rows_each)[:sends],
            in_specs=[smem()] * 6 + [hbm()] + [vmem()] * parts,
            out_specs=[hbm()] + [vmem()] * sends,
            scratch_shapes=scratch,
            compiler_params=params(),
            name="update",
        )(send_plane, send_row, send_cover, step_size, foot_lo, foot_hi, x, *returned)
        if not last:
            arrived = swap(outbound)
    return (x.reshape(model.shape), outs[parts])


def solution(mesh):
    both = ("groups", "sky")
    return jax.shard_map(
        body,
        mesh=mesh,
        in_specs=(
            P(both, None, None, None),
            P(both, None, None),
            P(both),
            P(),
            P(both, None),
            P(both),
            P(both, None),
            P(both, None),
            P(both, None),
            P(both, None),
            P(both, None),
            P(both, None),
            P(both),
            P(both),
        ),
        out_specs=(P(both, None, None, None), P(both, None, None)),
        check_vma=False,
    )
```

```python
import functools

import jax
import jax.numpy as jnp
from jax import lax
from jax.experimental import pallas as pl
from jax.experimental.pallas import tpu as pltpu
from jax.sharding import PartitionSpec as P

NPSF = 4
TAPS = 7
ITERS = 2
LANES = 128
HALF = TAPS // 2
F32 = jnp.float32
BF16 = jnp.bfloat16
I32 = jnp.int32
VMEM_BYTES = 24 * 1024 * 1024

smem = lambda: pl.BlockSpec(memory_space=pltpu.SMEM)
vmem = lambda: pl.BlockSpec(memory_space=pltpu.VMEM)
hbm = lambda: pl.BlockSpec(memory_space=pl.ANY)


def params(share=1.0):
    return pltpu.CompilerParams(vmem_limit_bytes=int(share * VMEM_BYTES))


def aligned(rows):
    return -(-rows // 16) * 16


def pack_slots(plane_ref, row_ref, cover_ref, tile_rows, height, rows_each, x_ref, packed_ref):
    peers, capacity = plane_ref.shape

    def peer(d, _):
        at = d * rows_each
        for c in range(capacity):
            first = jnp.maximum(plane_ref[d, c], 0) * tile_rows + row_ref[d, c]
            packed_ref[pl.ds(at, height), :] = x_ref[pl.ds(first, height), :]
            at = at + cover_ref[d, c]
        return 0

    lax.fori_loop(0, peers, peer, 0)


def bank_rows(taps, height):
    hp = lax.Precision.HIGHEST
    width = taps.shape[1]

    def grid(columns):
        return (
            lax.broadcasted_iota(I32, (width, columns), 0),
            lax.broadcasted_iota(I32, (width, columns), 1),
        )

    k, l = grid(width)
    total = jnp.dot(taps, (k // TAPS == l // TAPS).astype(F32), precision=hp, preferred_element_type=F32)
    unit = taps / total
    k, l = grid(2 * NPSF * LANES)
    mirror, j, l = l // (NPSF * LANES), l // LANES % NPSF, (l + HALF) % LANES
    i, t = l // height, l % height
    valid = (i < TAPS) & (t < TAPS)
    row_tap = j * TAPS + jnp.where(mirror == 1, t, TAPS - 1 - t)
    col_tap = (NPSF + j) * TAPS + jnp.where(mirror == 1, TAPS - 1 - i, i)
    row_part = jnp.dot(unit, (valid & (k == row_tap)).astype(F32), precision=hp, preferred_element_type=F32)
    col_part = jnp.dot(unit, (valid & (k == col_tap)).astype(F32), precision=hp, preferred_element_type=F32)
    product = row_part * col_part * (1.0 / NPSF)
    return [
        sum(product[:, (m * NPSF + j) * LANES : (m * NPSF + j + 1) * LANES] for j in range(NPSF)) for m in range(2)
    ]


def first_send_kernel(
    tile_rows, height, rows_each, plane_ref, row_ref, cover_ref, taps_ref, model_ref, out_ref, x_ref, packed_ref, bank_ref, sem
):
    peers = plane_ref.shape[0]
    total = model_ref.shape[0]
    load = pltpu.make_async_copy(model_ref, x_ref.at[pl.ds(0, total), :], sem)
    load.start()
    bank_ref[...] = jnp.zeros(bank_ref.shape, F32)
    for m, row in enumerate(bank_rows(taps_ref[...], height)):
        for n in range(taps_ref.shape[0]):
            bank_ref[2 * n + m : 2 * n + m + 1, :] = row[n : n + 1, :]
    bank = bank_ref[...].astype(BF16)
    load.wait()
    pack_slots(plane_ref, row_ref, cover_ref, tile_rows, height, rows_each, x_ref, packed_ref)
    for d in range(peers):
        out_ref[d, :rows_each, :] = packed_ref[d * rows_each : (d + 1) * rows_each, :].astype(BF16)
        out_ref[d, rows_each:, :] = bank


def update_kernel(
    bands,
    tile_rows,
    height,
    rows_each,
    last,
    plane_ref,
    row_ref,
    cover_ref,
    step_ref,
    lo_ref,
    hi_ref,
    returned_ref,
    model_ref,
    *rest,
):
    if last:
        new_ref, x_ref, back_ref, scale_ref, sem = rest
    else:
        new_ref, out_ref, x_ref, back_ref, scale_ref, sem, packed_ref = rest
    peers, capacity = plane_ref.shape
    total = model_ref.shape[0]
    planes = total // tile_rows
    load = pltpu.make_async_copy(model_ref, x_ref.at[pl.ds(0, total), :], sem)
    load.start()
    for p in range(planes):
        scale_ref[p] = step_ref[p % bands]
    for d in range(peers):
        back_ref[d * rows_each : (d + 1) * rows_each, :] = returned_ref[d].astype(F32)
    load.wait()
    place = lax.broadcasted_iota(I32, (height, LANES), 0)

    def peer(d, _):
        at = d * rows_each
        for c in range(capacity):
            p = jnp.maximum(plane_ref[d, c], 0)
            first = p * tile_rows + row_ref[d, c]
            cover = cover_ref[d, c]
            piece = jnp.where(place < cover, back_ref[pl.ds(at, height), :], 0.0)
            x_ref[pl.ds(first, height), :] = x_ref[pl.ds(first, height), :] - scale_ref[p] * piece
            at = at + cover
        return 0

    lax.fori_loop(0, peers, peer, 0)

    pos = lax.broadcasted_iota(I32, (tile_rows, LANES), 0)
    for p in range(planes):
        inside = (pos >= lo_ref[p // bands]) & (pos < hi_ref[p // bands])
        here = slice(p * tile_rows, (p + 1) * tile_rows)
        x_ref[here, :] = jnp.where(inside, jnp.maximum(x_ref[here, :], 0.0), 0.0)
    save = pltpu.make_async_copy(x_ref.at[pl.ds(0, total), :], new_ref, sem)
    save.start()
    if not last:
        pack_slots(plane_ref, row_ref, cover_ref, tile_rows, height, rows_each, x_ref, packed_ref)
        for d in range(peers):
            out_ref[d, :, :] = packed_ref[d * rows_each : (d + 1) * rows_each, :].astype(BF16)
    save.wait()


def tables_kernel(capacity, height, rows_each, slot_ref, start_ref, stop_ref, table_ref, length_ref):
    exposures, pieces = slot_ref.shape
    slots = length_ref.shape[0]
    stamp_row, return_row = 2 * pieces, 2 * pieces + 1

    def clear(s, _):
        length_ref[s] = 0
        table_ref[stamp_row, s] = 0
        return 0

    lax.fori_loop(0, slots, clear, 0, unroll=8)

    def measure(e, _):
        for k in range(pieces):
            s = slot_ref[e, k]

            @pl.when(s >= 0)
            def _():
                length_ref[s] = stop_ref[e, k] - start_ref[e, k]
                table_ref[stamp_row, s] = e * height + start_ref[e, k]

        return 0

    lax.fori_loop(0, exposures, measure, 0, unroll=2)

    def lay(o, _):
        at = o * rows_each
        for c in range(capacity):
            s = o * capacity + c
            table_ref[return_row, s] = at
            at = at + length_ref[s]
        return 0

    lax.fori_loop(0, slots // capacity, lay, 0)

    def point(e, _):
        for k in range(pieces):
            s = slot_ref[e, k]
            live = s >= 0
            begin = table_ref[return_row, jnp.maximum(s, 0)]
            table_ref[2 * k, e] = jnp.where(live, height + begin - start_ref[e, k], 0)
            table_ref[2 * k + 1, e] = jnp.where(live, start_ref[e, k], height)
        return 0

    lax.fori_loop(0, exposures, point, 0, unroll=2)


def blur_kernel(
    height,
    pieces,
    batches_each,
    last,
    table_ref,
    weight_ref,
    batch_ref,
    arrived_ref,
    bank_in_ref,
    seen_ref,
    *rest,
):
    if last:
        out_ref, residual_ref, rows_ref, bank_ref, result_ref, packed_ref, blur_ref, back_ref = rest
    else:
        out_ref, rows_ref, bank_ref, result_ref, packed_ref, blur_ref, back_ref = rest
    peers, rows_each, _ = out_ref.shape
    extra = bank_in_ref.shape[1]
    exposures = batch_ref.shape[0]
    slots = peers * (2 * rows_each // height)
    abreast = max(n for n in (1, 2, 4, 8, 16) if exposures % n == 0)
    place = lax.broadcasted_iota(I32, (height, LANES), 0)
    lane = lax.broadcasted_iota(I32, (height, LANES), 1)
    for o in range(peers):
        rows_ref[height + o * rows_each : height + (o + 1) * rows_each, :] = arrived_ref[o].astype(F32)
        bank_ref[o * extra : (o + 1) * extra, :] = bank_in_ref[o].astype(F32)

    gap = lane % height - place
    near = (gap <= HALF) & (gap >= -HALF) & (lane < TAPS * height)

    def operators(o, _):
        for n in range(batches_each):
            for m, ref in enumerate((blur_ref, back_ref)):
                taps = jnp.broadcast_to(bank_ref[pl.ds(o * extra + 2 * n + m, 1), :], (height, LANES))
                ref[o * batches_each + n] = jnp.where(
                    near, pltpu.roll(taps, 0, 1, stride=1, stride_axis=0), 0.0
                ).astype(BF16)
        return 0

    lax.fori_loop(0, peers, operators, 0, unroll=4)

    def shifted(x):
        parts = []
        for v in range(-HALF, HALF + 1):
            moved = x if v == 0 else pltpu.roll(x, v % LANES, 1)
            parts.append(jnp.where((lane >= v) & (lane < LANES + v), moved, jnp.zeros((), BF16)))
        parts.append(jnp.zeros((LANES - TAPS * height, LANES), BF16))
        return jnp.concatenate(parts, axis=0)

    def step(s, _):
        for q in range(abreast):
            e = s * abreast + q
            b = batch_ref[e]
            stamp = rows_ref[pl.ds(table_ref[0, e], height), :]
            for k in range(1, pieces):
                piece = rows_ref[pl.ds(table_ref[2 * k, e], height), :]
                stamp = jnp.where(place >= table_ref[2 * k + 1, e], piece, stamp)
            predicted = jnp.dot(blur_ref[b], shifted(stamp.astype(BF16)), preferred_element_type=F32)
            residual = weight_ref[e] * (predicted - seen_ref[e].astype(F32))
            if last:
                residual_ref[e] = residual
            result_ref[pl.ds(pl.multiple_of(e * height, height), height), :] = jnp.dot(
                back_ref[b], shifted(residual.astype(BF16)), preferred_element_type=F32
            )
        return 0

    lax.fori_loop(0, exposures // abreast, step, 0)

    def move(s, _):
        packed_ref[pl.ds(table_ref[2 * pieces + 1, s], height), :] = result_ref[
            pl.ds(table_ref[2 * pieces, s], height), :
        ]
        return 0

    lax.fori_loop(0, slots, move, 0, unroll=16)
    for o in range(peers):
        out_ref[o, :, :] = packed_ref[o * rows_each : (o + 1) * rows_each, :].astype(BF16)


def body(
    model,
    exposures,
    inv_var,
    step_size,
    psf_taps,
    exp_batch,
    send_plane,
    send_row,
    send_cover,
    use_slot,
    use_start,
    use_stop,
    foot_lo,
    foot_hi,
):
    tile_count, bands, tile_rows, columns = model.shape
    count, height, _ = exposures.shape
    peers, capacity = send_plane.shape
    pieces = use_slot.shape[1]
    total = tile_count * bands * tile_rows
    rows_each = capacity * height // 2
    batches_each = psf_taps.shape[0]
    extra = aligned(batches_each * 2)
    block = rows_each + extra
    assert columns == LANES and rows_each % extra == 0 and TAPS * height <= LANES - HALF
    x = model.reshape(total, columns)

    def swap(a):
        return lax.all_to_all(a, "sky", split_axis=0, concat_axis=0, tiled=True)

    outbound = pl.pallas_call(
        functools.partial(first_send_kernel, tile_rows, height, rows_each),
        out_shape=jax.ShapeDtypeStruct((peers, block, columns), BF16),
        in_specs=[smem(), smem(), smem(), vmem(), hbm()],
        out_specs=vmem(),
        scratch_shapes=[
            pltpu.VMEM((total + height, columns), F32),
            pltpu.VMEM((peers * rows_each + height, columns), F32),
            pltpu.VMEM((extra, columns), F32),
            pltpu.SemaphoreType.DMA,
        ],
        compiler_params=params(2.5),
        name="first_send",
    )(send_plane, send_row, send_cover, psf_taps, x)
    arrived = swap(outbound)
    table = pl.pallas_call(
        functools.partial(tables_kernel, capacity, height, rows_each),
        out_shape=jax.ShapeDtypeStruct((2 * pieces + 2, max(count, peers * capacity)), I32),
        in_specs=[smem(), smem(), smem()],
        out_specs=smem(),
        scratch_shapes=[pltpu.SMEM((peers * capacity,), I32)],
        cost_estimate=pl.CostEstimate(flops=4_000_000, bytes_accessed=8_000_000, transcendentals=0),
        name="tables",
    )(use_slot, use_start, use_stop)
    with_bank = arrived
    for sweep in range(ITERS):
        last = sweep == ITERS - 1
        rows_shape = jax.ShapeDtypeStruct((peers, rows_each, columns), BF16)
        outs = pl.pallas_call(
            functools.partial(blur_kernel, height, pieces, batches_each, last),
            grid=(1,),
            out_shape=(rows_shape, jax.ShapeDtypeStruct(exposures.shape, F32)) if last else rows_shape,
            in_specs=[
                smem(),
                smem(),
                smem(),
                pl.BlockSpec((peers, rows_each, columns), lambda i: (0, 0, 0)),
                pl.BlockSpec((peers, extra, columns), lambda i: (0, rows_each // extra, 0)),
                vmem(),
            ],
            out_specs=(vmem(), vmem()) if last else vmem(),
            scratch_shapes=[
                pltpu.VMEM((peers * rows_each + 2 * height, columns), F32),
                pltpu.VMEM((peers * extra, columns), F32),
                pltpu.VMEM((count * height + height, columns), F32),
                pltpu.VMEM((peers * rows_each + height, columns), F32),
                pltpu.VMEM((peers * batches_each, height, LANES), BF16),
                pltpu.VMEM((peers * batches_each, height, LANES), BF16),
            ],
            compiler_params=params(),
            name="blur",
        )(table, inv_var, exp_batch, arrived, with_bank, exposures)
        outgoing = outs[0] if last else outs
        returned = swap(outgoing)
        new_shape = jax.ShapeDtypeStruct((total, columns), F32)
        scratch = [
            pltpu.VMEM((total + height, columns), F32),
            pltpu.VMEM((peers * rows_each + height, columns), F32),
            pltpu.SMEM((tile_count * bands,), F32),
            pltpu.SemaphoreType.DMA,
        ]
        if not last:
            scratch.append(pltpu.VMEM((peers * rows_each + height, columns), F32))
        res = pl.pallas_call(
            functools.partial(update_kernel, bands, tile_rows, height, rows_each, last),
            out_shape=new_shape if last else (new_shape, rows_shape),
            in_specs=[smem()] * 6 + [vmem(), hbm()],
            out_specs=hbm() if last else (hbm(), vmem()),
            scratch_shapes=scratch,
            compiler_params=params(),
            name="update",
        )(send_plane, send_row, send_cover, step_size, foot_lo, foot_hi, returned, x)
        if last:
            x = res
        else:
            x, outbound = res
            arrived = swap(outbound)
    return (x.reshape(model.shape), outs[1])


def solution(mesh):
    both = ("groups", "sky")
    return jax.shard_map(
        body,
        mesh=mesh,
        in_specs=(
            P(both, None, None, None),
            P(both, None, None),
            P(both),
            P(),
            P(both, None),
            P(both),
            P(both, None),
            P(both, None),
            P(both, None),
            P(both, None),
            P(both, None),
            P(both, None),
            P(both),
            P(both),
        ),
        out_specs=(P(both, None, None, None), P(both, None, None)),
        check_vma=False,
    )
```

```python
import functools

import jax
import jax.numpy as jnp
from jax import lax
from jax.experimental import pallas as pl
from jax.experimental.pallas import tpu as pltpu
from jax.sharding import PartitionSpec as P

NPSF = 4
TAPS = 7
ITERS = 2
LANES = 128
HALF = TAPS // 2
F32 = jnp.float32
BF16 = jnp.bfloat16
I32 = jnp.int32
VMEM_BYTES = 24 * 1024 * 1024

smem = lambda: pl.BlockSpec(memory_space=pltpu.SMEM)
vmem = lambda: pl.BlockSpec(memory_space=pltpu.VMEM)
hbm = lambda: pl.BlockSpec(memory_space=pl.ANY)


def params(share=1.0):
    return pltpu.CompilerParams(vmem_limit_bytes=int(share * VMEM_BYTES))


def aligned(rows):
    return -(-rows // 16) * 16


def exchange_order(peers):
    if peers % 2:
        return list(range(peers))
    return [p // 2 + p % 2 * (peers // 2) for p in range(peers)]


def pack_slots(plane_ref, row_ref, cover_ref, tile_rows, height, rows_each, x_ref, packed_ref):
    peers, capacity = plane_ref.shape

    def peer(d, _):
        at = d * rows_each
        for c in range(capacity):
            first = jnp.maximum(plane_ref[d, c], 0) * tile_rows + row_ref[d, c]
            packed_ref[pl.ds(at, height), :] = x_ref[pl.ds(first, height), :]
            at = at + cover_ref[d, c]
        return 0

    lax.fori_loop(0, peers, peer, 0)


def bank_rows(taps, height):
    hp = lax.Precision.HIGHEST
    width = taps.shape[1]

    def grid(columns):
        return (
            lax.broadcasted_iota(I32, (width, columns), 0),
            lax.broadcasted_iota(I32, (width, columns), 1),
        )

    k, l = grid(width)
    total = jnp.dot(taps, (k // TAPS == l // TAPS).astype(F32), precision=hp, preferred_element_type=F32)
    unit = taps / total
    k, l = grid(2 * NPSF * LANES)
    mirror, j, l = l // (NPSF * LANES), l // LANES % NPSF, (l + HALF) % LANES
    i, t = l // height, l % height
    valid = (i < TAPS) & (t < TAPS)
    row_tap = j * TAPS + jnp.where(mirror == 1, t, TAPS - 1 - t)
    col_tap = (NPSF + j) * TAPS + jnp.where(mirror == 1, TAPS - 1 - i, i)
    row_part = jnp.dot(unit, (valid & (k == row_tap)).astype(F32), precision=hp, preferred_element_type=F32)
    col_part = jnp.dot(unit, (valid & (k == col_tap)).astype(F32), precision=hp, preferred_element_type=F32)
    product = row_part * col_part * (1.0 / NPSF)
    return [
        sum(product[:, (m * NPSF + j) * LANES : (m * NPSF + j + 1) * LANES] for j in range(NPSF)) for m in range(2)
    ]


def first_send_kernel(
    tile_rows, height, rows_each, plane_ref, row_ref, cover_ref, taps_ref, model_ref, out_ref, x_ref, packed_ref, bank_ref, sem
):
    peers = plane_ref.shape[0]
    total = model_ref.shape[0]
    load = pltpu.make_async_copy(model_ref, x_ref.at[pl.ds(0, total), :], sem)
    load.start()
    bank_ref[...] = jnp.zeros(bank_ref.shape, F32)
    for m, row in enumerate(bank_rows(taps_ref[...], height)):
        for n in range(taps_ref.shape[0]):
            bank_ref[2 * n + m : 2 * n + m + 1, :] = row[n : n + 1, :]
    bank = bank_ref[...].astype(BF16)
    load.wait()
    pack_slots(plane_ref, row_ref, cover_ref, tile_rows, height, rows_each, x_ref, packed_ref)
    for p, d in enumerate(exchange_order(peers)):
        out_ref[p, :rows_each, :] = packed_ref[d * rows_each : (d + 1) * rows_each, :].astype(BF16)
        out_ref[p, rows_each:, :] = bank


def update_kernel(
    bands,
    tile_rows,
    height,
    rows_each,
    last,
    plane_ref,
    row_ref,
    cover_ref,
    step_ref,
    lo_ref,
    hi_ref,
    returned_ref,
    model_ref,
    *rest,
):
    if last:
        new_ref, x_ref, back_ref, scale_ref, sem = rest
    else:
        new_ref, out_ref, x_ref, back_ref, scale_ref, sem, packed_ref = rest
    peers, capacity = plane_ref.shape
    total = model_ref.shape[0]
    planes = total // tile_rows
    load = pltpu.make_async_copy(model_ref, x_ref.at[pl.ds(0, total), :], sem)
    load.start()
    for p in range(planes):
        scale_ref[p] = step_ref[p % bands]
    for p, d in enumerate(exchange_order(peers)):
        back_ref[d * rows_each : (d + 1) * rows_each, :] = returned_ref[p].astype(F32)
    load.wait()
    place = lax.broadcasted_iota(I32, (height, LANES), 0)

    def peer(d, _):
        at = d * rows_each
        for c in range(capacity):
            p = jnp.maximum(plane_ref[d, c], 0)
            first = p * tile_rows + row_ref[d, c]
            cover = cover_ref[d, c]
            piece = jnp.where(place < cover, back_ref[pl.ds(at, height), :], 0.0)
            x_ref[pl.ds(first, height), :] = x_ref[pl.ds(first, height), :] - scale_ref[p] * piece
            at = at + cover
        return 0

    lax.fori_loop(0, peers, peer, 0)

    pos = lax.broadcasted_iota(I32, (tile_rows, LANES), 0)
    for p in range(planes):
        inside = (pos >= lo_ref[p // bands]) & (pos < hi_ref[p // bands])
        here = slice(p * tile_rows, (p + 1) * tile_rows)
        x_ref[here, :] = jnp.where(inside, jnp.maximum(x_ref[here, :], 0.0), 0.0)
    save = pltpu.make_async_copy(x_ref.at[pl.ds(0, total), :], new_ref, sem)
    save.start()
    if not last:
        pack_slots(plane_ref, row_ref, cover_ref, tile_rows, height, rows_each, x_ref, packed_ref)
        for p, d in enumerate(exchange_order(peers)):
            out_ref[p, :, :] = packed_ref[d * rows_each : (d + 1) * rows_each, :].astype(BF16)
    save.wait()


def tables_kernel(capacity, height, rows_each, slot_ref, start_ref, stop_ref, table_ref, length_ref):
    exposures, pieces = slot_ref.shape
    slots = length_ref.shape[0]
    stamp_row, return_row = 2 * pieces, 2 * pieces + 1

    def clear(s, _):
        length_ref[s] = 0
        table_ref[stamp_row, s] = 0
        return 0

    lax.fori_loop(0, slots, clear, 0, unroll=8)

    def measure(e, _):
        for k in range(pieces):
            s = slot_ref[e, k]

            @pl.when(s >= 0)
            def _():
                length_ref[s] = stop_ref[e, k] - start_ref[e, k]
                table_ref[stamp_row, s] = e * height + start_ref[e, k]

        return 0

    lax.fori_loop(0, exposures, measure, 0, unroll=2)

    def lay(o, _):
        at = o * rows_each
        for c in range(capacity):
            s = o * capacity + c
            table_ref[return_row, s] = at
            at = at + length_ref[s]
        return 0

    lax.fori_loop(0, slots // capacity, lay, 0)

    def point(e, _):
        for k in range(pieces):
            s = slot_ref[e, k]
            live = s >= 0
            begin = table_ref[return_row, jnp.maximum(s, 0)]
            table_ref[2 * k, e] = jnp.where(live, height + begin - start_ref[e, k], 0)
            table_ref[2 * k + 1, e] = jnp.where(live, start_ref[e, k], height)
        return 0

    lax.fori_loop(0, exposures, point, 0, unroll=2)


def blur_kernel(
    height,
    pieces,
    batches_each,
    last,
    table_ref,
    weight_ref,
    batch_ref,
    arrived_ref,
    bank_in_ref,
    seen_ref,
    *rest,
):
    if last:
        out_ref, residual_ref, rows_ref, bank_ref, result_ref, packed_ref, held_ref, blur_ref, back_ref = rest
    else:
        out_ref, rows_ref, bank_ref, result_ref, packed_ref, held_ref, blur_ref, back_ref = rest
    peers, rows_each, _ = out_ref.shape
    extra = bank_in_ref.shape[1]
    exposures = batch_ref.shape[0]
    slots = peers * (2 * rows_each // height)
    abreast = max(n for n in (1, 2, 4, 8, 16) if exposures % n == 0)
    place = lax.broadcasted_iota(I32, (height, LANES), 0)
    lane = lax.broadcasted_iota(I32, (height, LANES), 1)
    for p, o in enumerate(exchange_order(peers)):
        rows_ref[height + o * rows_each : height + (o + 1) * rows_each, :] = arrived_ref[p].astype(F32)
        bank_ref[o * extra : (o + 1) * extra, :] = bank_in_ref[p].astype(F32)

    gap = lane % height - place
    near = (gap <= HALF) & (gap >= -HALF) & (lane < TAPS * height)

    def operators(o, _):
        for n in range(batches_each):
            for m, ref in enumerate((blur_ref, back_ref)):
                taps = jnp.broadcast_to(bank_ref[pl.ds(o * extra + 2 * n + m, 1), :], (height, LANES))
                ref[o * batches_each + n] = jnp.where(
                    near, pltpu.roll(taps, 0, 1, stride=1, stride_axis=0), 0.0
                ).astype(BF16)
        return 0

    lax.fori_loop(0, peers, operators, 0, unroll=4)

    def shifted(x):
        parts = []
        for v in range(-HALF, HALF + 1):
            moved = x if v == 0 else pltpu.roll(x, v % LANES, 1)
            parts.append(jnp.where((lane >= v) & (lane < LANES + v), moved, jnp.zeros((), BF16)))
        parts.append(jnp.zeros((LANES - TAPS * height, LANES), BF16))
        return jnp.concatenate(parts, axis=0)

    def correlate(s):
        for q in range(abreast):
            e = s * abreast + q
            here = pl.ds(pl.multiple_of(e * height, height), height)
            result_ref[here, :] = jnp.dot(
                back_ref[batch_ref[e]], shifted(held_ref[here, :]), preferred_element_type=F32
            )

    def blur(s):
        for q in range(abreast):
            e = s * abreast + q
            stamp = rows_ref[pl.ds(table_ref[0, e], height), :]
            for k in range(1, pieces):
                piece = rows_ref[pl.ds(table_ref[2 * k, e], height), :]
                stamp = jnp.where(place >= table_ref[2 * k + 1, e], piece, stamp)
            predicted = jnp.dot(
                blur_ref[batch_ref[e]], shifted(stamp.astype(BF16)), preferred_element_type=F32
            )
            residual = weight_ref[e] * (predicted - seen_ref[e].astype(F32))
            if last:
                residual_ref[e] = residual
            held_ref[pl.ds(pl.multiple_of(e * height, height), height), :] = residual.astype(BF16)

    def step(s, _):
        correlate(s - 1)
        blur(s)
        return 0

    steps = exposures // abreast
    blur(0)
    lax.fori_loop(1, steps, step, 0)
    correlate(steps - 1)

    def move(s, _):
        packed_ref[pl.ds(table_ref[2 * pieces + 1, s], height), :] = result_ref[
            pl.ds(table_ref[2 * pieces, s], height), :
        ]
        return 0

    lax.fori_loop(0, slots, move, 0, unroll=16)
    for p, o in enumerate(exchange_order(peers)):
        out_ref[p, :, :] = packed_ref[o * rows_each : (o + 1) * rows_each, :].astype(BF16)


def body(
    model,
    exposures,
    inv_var,
    step_size,
    psf_taps,
    exp_batch,
    send_plane,
    send_row,
    send_cover,
    use_slot,
    use_start,
    use_stop,
    foot_lo,
    foot_hi,
):
    tile_count, bands, tile_rows, columns = model.shape
    count, height, _ = exposures.shape
    peers, capacity = send_plane.shape
    pieces = use_slot.shape[1]
    total = tile_count * bands * tile_rows
    rows_each = capacity * height // 2
    batches_each = psf_taps.shape[0]
    extra = aligned(batches_each * 2)
    block = rows_each + extra
    assert columns == LANES and rows_each % extra == 0 and TAPS * height <= LANES - HALF
    x = model.reshape(total, columns)

    def swap(a):
        return lax.all_to_all(
            a, "sky", split_axis=0, concat_axis=0, tiled=True, axis_index_groups=[exchange_order(peers)]
        )

    outbound = pl.pallas_call(
        functools.partial(first_send_kernel, tile_rows, height, rows_each),
        out_shape=jax.ShapeDtypeStruct((peers, block, columns), BF16),
        in_specs=[smem(), smem(), smem(), vmem(), hbm()],
        out_specs=vmem(),
        scratch_shapes=[
            pltpu.VMEM((total + height, columns), F32),
            pltpu.VMEM((peers * rows_each + height, columns), F32),
            pltpu.VMEM((extra, columns), F32),
            pltpu.SemaphoreType.DMA,
        ],
        compiler_params=params(2.5),
        name="first_send",
    )(send_plane, send_row, send_cover, psf_taps, x)
    arrived = swap(outbound)
    table = pl.pallas_call(
        functools.partial(tables_kernel, capacity, height, rows_each),
        out_shape=jax.ShapeDtypeStruct((2 * pieces + 2, max(count, peers * capacity)), I32),
        in_specs=[smem(), smem(), smem()],
        out_specs=smem(),
        scratch_shapes=[pltpu.SMEM((peers * capacity,), I32)],
        cost_estimate=pl.CostEstimate(flops=4_000_000, bytes_accessed=8_000_000, transcendentals=0),
        name="tables",
    )(use_slot, use_start, use_stop)
    with_bank = arrived
    for sweep in range(ITERS):
        last = sweep == ITERS - 1
        rows_shape = jax.ShapeDtypeStruct((peers, rows_each, columns), BF16)
        outs = pl.pallas_call(
            functools.partial(blur_kernel, height, pieces, batches_each, last),
            grid=(1,),
            out_shape=(rows_shape, jax.ShapeDtypeStruct(exposures.shape, F32)) if last else rows_shape,
            in_specs=[
                smem(),
                smem(),
                smem(),
                pl.BlockSpec((peers, rows_each, columns), lambda i: (0, 0, 0)),
                pl.BlockSpec((peers, extra, columns), lambda i: (0, rows_each // extra, 0)),
                vmem(),
            ],
            out_specs=(vmem(), vmem()) if last else vmem(),
            scratch_shapes=[
                pltpu.VMEM((peers * rows_each + 2 * height, columns), F32),
                pltpu.VMEM((peers * extra, columns), F32),
                pltpu.VMEM((count * height + height, columns), F32),
                pltpu.VMEM((peers * rows_each + height, columns), F32),
                pltpu.VMEM((count * height, columns), BF16),
                pltpu.VMEM((peers * batches_each, height, LANES), BF16),
                pltpu.VMEM((peers * batches_each, height, LANES), BF16),
            ],
            compiler_params=params(),
            name="blur",
        )(table, inv_var, exp_batch, arrived, with_bank, exposures)
        outgoing = outs[0] if last else outs
        returned = swap(outgoing)
        new_shape = jax.ShapeDtypeStruct((total, columns), F32)
        scratch = [
            pltpu.VMEM((total + height, columns), F32),
            pltpu.VMEM((peers * rows_each + height, columns), F32),
            pltpu.SMEM((tile_count * bands,), F32),
            pltpu.SemaphoreType.DMA,
        ]
        if not last:
            scratch.append(pltpu.VMEM((peers * rows_each + height, columns), F32))
        res = pl.pallas_call(
            functools.partial(update_kernel, bands, tile_rows, height, rows_each, last),
            out_shape=new_shape if last else (new_shape, rows_shape),
            in_specs=[smem()] * 6 + [vmem(), hbm()],
            out_specs=hbm() if last else (hbm(), vmem()),
            scratch_shapes=scratch,
            compiler_params=params(),
            name="update",
        )(send_plane, send_row, send_cover, step_size, foot_lo, foot_hi, returned, x)
        if last:
            x = res
        else:
            x, outbound = res
            arrived = swap(outbound)
    return (x.reshape(model.shape), outs[1])


def solution(mesh):
    both = ("groups", "sky")
    return jax.shard_map(
        body,
        mesh=mesh,
        in_specs=(
            P(both, None, None, None),
            P(both, None, None),
            P(both),
            P(),
            P(both, None),
            P(both),
            P(both, None),
            P(both, None),
            P(both, None),
            P(both, None),
            P(both, None),
            P(both, None),
            P(both),
            P(both),
        ),
        out_specs=(P(both, None, None, None), P(both, None, None)),
        check_vma=False,
    )
```

```python
import functools

import jax
import jax.numpy as jnp
from jax import lax
from jax.experimental import pallas as pl
from jax.experimental.pallas import tpu as pltpu
from jax.sharding import PartitionSpec as P

NPSF = 4
TAPS = 7
ITERS = 2
LANES = 128
HALF = TAPS // 2
F32 = jnp.float32
BF16 = jnp.bfloat16
I32 = jnp.int32
VMEM_BYTES = 24 * 1024 * 1024

smem = lambda: pl.BlockSpec(memory_space=pltpu.SMEM)
vmem = lambda: pl.BlockSpec(memory_space=pltpu.VMEM)
hbm = lambda: pl.BlockSpec(memory_space=pl.ANY)


def params(share=1.0):
    return pltpu.CompilerParams(vmem_limit_bytes=int(share * VMEM_BYTES))


def aligned(rows):
    return -(-rows // 16) * 16


def fold(top, bottom, side):
    lane = lax.broadcasted_iota(I32, top.shape, 1)
    if side == 0:
        return jnp.where(lane < LANES // 2, top, pltpu.roll(bottom, LANES // 2, 1))
    return jnp.where(lane < LANES // 2, pltpu.roll(top, LANES // 2, 1), bottom)


def pack_slots(plane_ref, row_ref, cover_ref, tile_rows, height, rows_each, x_ref, packed_ref):
    peers, capacity = plane_ref.shape

    def peer(d, _):
        at = d * rows_each
        for c in range(capacity):
            first = jnp.maximum(plane_ref[d, c], 0) * tile_rows + row_ref[d, c]
            packed_ref[pl.ds(at, height), :] = x_ref[pl.ds(first, height), :]
            at = at + cover_ref[d, c]
        return 0

    lax.fori_loop(0, peers, peer, 0)


def bank_rows(taps, height):
    hp = lax.Precision.HIGHEST
    width = taps.shape[1]

    def grid(columns):
        return (
            lax.broadcasted_iota(I32, (width, columns), 0),
            lax.broadcasted_iota(I32, (width, columns), 1),
        )

    k, l = grid(width)
    total = jnp.dot(taps, (k // TAPS == l // TAPS).astype(F32), precision=hp, preferred_element_type=F32)
    unit = taps / total
    k, l = grid(2 * NPSF * LANES)
    mirror, j, l = l // (NPSF * LANES), l // LANES % NPSF, (l + HALF) % LANES
    i, t = l // height, l % height
    valid = (i < TAPS) & (t < TAPS)
    row_tap = j * TAPS + jnp.where(mirror == 1, t, TAPS - 1 - t)
    col_tap = (NPSF + j) * TAPS + jnp.where(mirror == 1, TAPS - 1 - i, i)
    row_part = jnp.dot(unit, (valid & (k == row_tap)).astype(F32), precision=hp, preferred_element_type=F32)
    col_part = jnp.dot(unit, (valid & (k == col_tap)).astype(F32), precision=hp, preferred_element_type=F32)
    product = row_part * col_part * (1.0 / NPSF)
    return [
        sum(product[:, (m * NPSF + j) * LANES : (m * NPSF + j + 1) * LANES] for j in range(NPSF)) for m in range(2)
    ]


def first_send_kernel(
    tile_rows, height, rows_each, plane_ref, row_ref, cover_ref, taps_ref, model_ref, out_ref, x_ref, packed_ref, bank_ref, sem
):
    peers = plane_ref.shape[0]
    total = model_ref.shape[0]
    load = pltpu.make_async_copy(model_ref, x_ref.at[pl.ds(0, total), :], sem)
    load.start()
    bank_ref[...] = jnp.zeros(bank_ref.shape, F32)
    for m, row in enumerate(bank_rows(taps_ref[...], height)):
        for n in range(taps_ref.shape[0]):
            bank_ref[2 * n + m : 2 * n + m + 1, :] = row[n : n + 1, :]
    bank = bank_ref[...].astype(BF16)
    load.wait()
    pack_slots(plane_ref, row_ref, cover_ref, tile_rows, height, rows_each, x_ref, packed_ref)
    for d in range(peers):
        out_ref[d, :rows_each, :] = packed_ref[d * rows_each : (d + 1) * rows_each, :].astype(BF16)
        out_ref[d, rows_each:, :] = bank


def update_kernel(
    bands,
    tile_rows,
    height,
    rows_each,
    side,
    last,
    plane_ref,
    row_ref,
    cover_ref,
    step_ref,
    lo_ref,
    hi_ref,
    returned_ref,
    model_ref,
    *rest,
):
    if last:
        new_ref, x_ref, back_ref, scale_ref, sem = rest
    else:
        new_ref, out_ref, x_ref, back_ref, scale_ref, sem, packed_ref = rest
    peers, capacity = plane_ref.shape
    total = model_ref.shape[0]
    planes = total // tile_rows
    half = rows_each // 2
    load = pltpu.make_async_copy(model_ref, x_ref.at[pl.ds(0, total), :], sem)
    load.start()
    for p in range(planes):
        scale_ref[p] = step_ref[p % bands]

    def on_side(lane):
        return (lane < LANES // 2) == (side == 0)

    for d in range(peers):
        at = d * rows_each
        rows = returned_ref[d].astype(F32)
        if side is None:
            back_ref[at : at + rows_each, :] = rows
        else:
            moved = pltpu.roll(rows, LANES // 2, 1)
            back_ref[at : at + half, :] = rows if side == 0 else moved
            back_ref[at + half : at + rows_each, :] = moved if side == 0 else rows
    load.wait()
    place = lax.broadcasted_iota(I32, (height, LANES), 0)
    if side is not None:
        place = jnp.where(on_side(lax.broadcasted_iota(I32, (height, LANES), 1)), place, height)

    def peer(d, _):
        at = d * rows_each
        for c in range(capacity):
            p = jnp.maximum(plane_ref[d, c], 0)
            first = p * tile_rows + row_ref[d, c]
            cover = cover_ref[d, c]
            piece = jnp.where(place < cover, back_ref[pl.ds(at, height), :], 0.0)
            x_ref[pl.ds(first, height), :] = x_ref[pl.ds(first, height), :] - scale_ref[p] * piece
            at = at + cover
        return 0

    lax.fori_loop(0, peers, peer, 0)

    pos = lax.broadcasted_iota(I32, (tile_rows, LANES), 0)
    for p in range(planes):
        inside = (pos >= lo_ref[p // bands]) & (pos < hi_ref[p // bands])
        here = slice(p * tile_rows, (p + 1) * tile_rows)
        old = x_ref[here, :]
        new = jnp.where(inside, jnp.maximum(old, 0.0), 0.0)
        if side is not None:
            new = jnp.where(on_side(lax.broadcasted_iota(I32, (tile_rows, LANES), 1)), new, old)
        x_ref[here, :] = new
    save = pltpu.make_async_copy(x_ref.at[pl.ds(0, total), :], new_ref, sem)
    save.start()
    if not last:
        pack_slots(plane_ref, row_ref, cover_ref, tile_rows, height, rows_each, x_ref, packed_ref)
        for d in range(peers):
            at = d * rows_each
            if side is None:
                out_ref[d] = packed_ref[at : at + rows_each, :].astype(BF16)
            else:
                top, bottom = packed_ref[at : at + half, :], packed_ref[at + half : at + rows_each, :]
                out_ref[d] = fold(top, bottom, side).astype(BF16)
    save.wait()


def tables_kernel(capacity, height, rows_each, slot_ref, start_ref, stop_ref, table_ref, length_ref):
    exposures, pieces = slot_ref.shape
    slots = length_ref.shape[0]
    stamp_row, return_row = 2 * pieces, 2 * pieces + 1

    def clear(s, _):
        length_ref[s] = 0
        table_ref[stamp_row, s] = 0
        return 0

    lax.fori_loop(0, slots, clear, 0, unroll=8)

    def measure(e, _):
        for k in range(pieces):
            s = slot_ref[e, k]

            @pl.when(s >= 0)
            def _():
                length_ref[s] = stop_ref[e, k] - start_ref[e, k]
                table_ref[stamp_row, s] = e * height + start_ref[e, k]

        return 0

    lax.fori_loop(0, exposures, measure, 0, unroll=2)

    def lay(o, _):
        at = o * rows_each
        for c in range(capacity):
            s = o * capacity + c
            table_ref[return_row, s] = at
            at = at + length_ref[s]
        return 0

    lax.fori_loop(0, slots // capacity, lay, 0)

    def point(e, _):
        for k in range(pieces):
            s = slot_ref[e, k]
            live = s >= 0
            begin = table_ref[return_row, jnp.maximum(s, 0)]
            table_ref[2 * k, e] = jnp.where(live, height + begin - start_ref[e, k], 0)
            table_ref[2 * k + 1, e] = jnp.where(live, start_ref[e, k], height)
        return 0

    lax.fori_loop(0, exposures, point, 0, unroll=2)


def blur_kernel(
    height,
    pieces,
    batches_each,
    sides_in,
    sides_out,
    last,
    table_ref,
    weight_ref,
    batch_ref,
    bank_in_ref,
    seen_ref,
    *rest,
):
    arrived_refs, out_refs, rest = rest[:sides_in], rest[sides_in : sides_in + sides_out], rest[sides_in + sides_out :]
    if last:
        residual_ref, rows_ref, bank_ref, result_ref, packed_ref, held_ref, blur_ref, back_ref = rest
    else:
        rows_ref, bank_ref, result_ref, packed_ref, held_ref, blur_ref, back_ref = rest
    peers = out_refs[0].shape[0]
    rows_each = out_refs[0].shape[1] * sides_out
    half = rows_each // 2
    extra = bank_in_ref.shape[1]
    exposures = batch_ref.shape[0]
    slots = peers * (2 * rows_each // height)
    abreast = max(n for n in (1, 2, 4, 8, 16) if exposures % n == 0)
    place = lax.broadcasted_iota(I32, (height, LANES), 0)
    lane = lax.broadcasted_iota(I32, (height, LANES), 1)
    for o in range(peers):
        at = height + o * rows_each
        parts = [ref[o].astype(F32) for ref in arrived_refs]
        if sides_in == 1:
            rows_ref[at : at + rows_each, :] = parts[0]
        else:
            rows_ref[at : at + half, :] = fold(*parts, 0)
            rows_ref[at + half : at + rows_each, :] = fold(*parts, 1)
        bank_ref[o * extra : (o + 1) * extra, :] = bank_in_ref[o].astype(F32)

    gap = lane % height - place
    near = (gap <= HALF) & (gap >= -HALF) & (lane < TAPS * height)

    def operators(o, _):
        for n in range(batches_each):
            for m, ref in enumerate((blur_ref, back_ref)):
                taps = jnp.broadcast_to(bank_ref[pl.ds(o * extra + 2 * n + m, 1), :], (height, LANES))
                ref[o * batches_each + n] = jnp.where(
                    near, pltpu.roll(taps, 0, 1, stride=1, stride_axis=0), 0.0
                ).astype(BF16)
        return 0

    lax.fori_loop(0, peers, operators, 0, unroll=4)

    def shifted(x):
        parts = []
        for v in range(-HALF, HALF + 1):
            moved = x if v == 0 else pltpu.roll(x, v % LANES, 1)
            parts.append(jnp.where((lane >= v) & (lane < LANES + v), moved, jnp.zeros((), BF16)))
        parts.append(jnp.zeros((LANES - TAPS * height, LANES), BF16))
        return jnp.concatenate(parts, axis=0)

    def correlate(s):
        for q in range(abreast):
            e = s * abreast + q
            here = pl.ds(pl.multiple_of(e * height, height), height)
            result_ref[here, :] = jnp.dot(
                back_ref[batch_ref[e]], shifted(held_ref[here, :]), preferred_element_type=F32
            )

    def blur(s):
        for q in range(abreast):
            e = s * abreast + q
            stamp = rows_ref[pl.ds(table_ref[0, e], height), :]
            for k in range(1, pieces):
                piece = rows_ref[pl.ds(table_ref[2 * k, e], height), :]
                stamp = jnp.where(place >= table_ref[2 * k + 1, e], piece, stamp)
            predicted = jnp.dot(
                blur_ref[batch_ref[e]], shifted(stamp.astype(BF16)), preferred_element_type=F32
            )
            residual = weight_ref[e] * (predicted - seen_ref[e].astype(F32))
            if last:
                residual_ref[e] = residual
            held_ref[pl.ds(pl.multiple_of(e * height, height), height), :] = residual.astype(BF16)

    def step(s, _):
        correlate(s - 1)
        blur(s)
        return 0

    steps = exposures // abreast
    blur(0)
    lax.fori_loop(1, steps, step, 0)
    correlate(steps - 1)

    def move(s, _):
        packed_ref[pl.ds(table_ref[2 * pieces + 1, s], height), :] = result_ref[
            pl.ds(table_ref[2 * pieces, s], height), :
        ]
        return 0

    lax.fori_loop(0, slots, move, 0, unroll=16)
    for o in range(peers):
        at = o * rows_each
        if sides_out == 1:
            out_refs[0][o] = packed_ref[at : at + rows_each, :].astype(BF16)
        else:
            top, bottom = packed_ref[at : at + half, :], packed_ref[at + half : at + rows_each, :]
            for side, out_ref in enumerate(out_refs):
                out_ref[o] = fold(top, bottom, side).astype(BF16)


def body(
    model,
    exposures,
    inv_var,
    step_size,
    psf_taps,
    exp_batch,
    send_plane,
    send_row,
    send_cover,
    use_slot,
    use_start,
    use_stop,
    foot_lo,
    foot_hi,
):
    tile_count, bands, tile_rows, columns = model.shape
    count, height, _ = exposures.shape
    peers, capacity = send_plane.shape
    pieces = use_slot.shape[1]
    total = tile_count * bands * tile_rows
    rows_each = capacity * height // 2
    batches_each = psf_taps.shape[0]
    extra = aligned(batches_each * 2)
    block = rows_each + extra
    assert columns == LANES and rows_each % extra == 0 and TAPS * height <= LANES - HALF
    x = model.reshape(total, columns)

    def swap(a):
        return lax.all_to_all(a, "sky", split_axis=0, concat_axis=0, tiled=True)

    outbound = pl.pallas_call(
        functools.partial(first_send_kernel, tile_rows, height, rows_each),
        out_shape=jax.ShapeDtypeStruct((peers, block, columns), BF16),
        in_specs=[smem(), smem(), smem(), vmem(), hbm()],
        out_specs=vmem(),
        scratch_shapes=[
            pltpu.VMEM((total + height, columns), F32),
            pltpu.VMEM((peers * rows_each + height, columns), F32),
            pltpu.VMEM((extra, columns), F32),
            pltpu.SemaphoreType.DMA,
        ],
        compiler_params=params(2.5),
        name="first_send",
    )(send_plane, send_row, send_cover, psf_taps, x)
    arrived = swap(outbound)
    table = pl.pallas_call(
        functools.partial(tables_kernel, capacity, height, rows_each),
        out_shape=jax.ShapeDtypeStruct((2 * pieces + 2, max(count, peers * capacity)), I32),
        in_specs=[smem(), smem(), smem()],
        out_specs=smem(),
        scratch_shapes=[pltpu.SMEM((peers * capacity,), I32)],
        cost_estimate=pl.CostEstimate(flops=4_000_000, bytes_accessed=8_000_000, transcendentals=0),
        name="tables",
    )(use_slot, use_start, use_stop)
    with_bank, arrived = arrived, [arrived]
    sides = 2 if rows_each % 32 == 0 else 1
    for sweep in range(ITERS):
        last = sweep == ITERS - 1
        sides_in, sides_out = len(arrived), 1 if last else sides
        residual_shape = [jax.ShapeDtypeStruct(exposures.shape, F32)] if last else []
        whole = pl.BlockSpec((peers, rows_each // sides_in, columns), lambda i: (0, 0, 0))
        outs = pl.pallas_call(
            functools.partial(blur_kernel, height, pieces, batches_each, sides_in, sides_out, last),
            grid=(1,),
            out_shape=[jax.ShapeDtypeStruct((peers, rows_each // sides_out, columns), BF16)] * sides_out
            + residual_shape,
            in_specs=[
                smem(),
                smem(),
                smem(),
                pl.BlockSpec((peers, extra, columns), lambda i: (0, rows_each // extra, 0)),
                vmem(),
            ]
            + [whole] * sides_in,
            out_specs=[vmem()] * (sides_out + len(residual_shape)),
            scratch_shapes=[
                pltpu.VMEM((peers * rows_each + 2 * height, columns), F32),
                pltpu.VMEM((peers * extra, columns), F32),
                pltpu.VMEM((count * height + height, columns), F32),
                pltpu.VMEM((peers * rows_each + height, columns), F32),
                pltpu.VMEM((count * height, columns), BF16),
                pltpu.VMEM((peers * batches_each, height, LANES), BF16),
                pltpu.VMEM((peers * batches_each, height, LANES), BF16),
            ],
            compiler_params=params(),
            name="blur",
        )(table, inv_var, exp_batch, with_bank, exposures, *arrived)
        returned = [swap(out) for out in outs[:sides_out]]
        arrived = []
        for side, back in enumerate(returned):
            scratch = [
                pltpu.VMEM((total + height, columns), F32),
                pltpu.VMEM((peers * rows_each + height, columns), F32),
                pltpu.SMEM((tile_count * bands,), F32),
                pltpu.SemaphoreType.DMA,
            ]
            if not last:
                scratch.append(pltpu.VMEM((peers * rows_each + height, columns), F32))
            sent = [] if last else [jax.ShapeDtypeStruct(back.shape, BF16)]
            x, *outbound = pl.pallas_call(
                functools.partial(
                    update_kernel,
                    bands,
                    tile_rows,
                    height,
                    rows_each,
                    side if sides_out == 2 else None,
                    last,
                ),
                out_shape=[jax.ShapeDtypeStruct((total, columns), F32)] + sent,
                in_specs=[smem()] * 6 + [vmem(), hbm()],
                out_specs=[hbm()] + [vmem()] * len(sent),
                scratch_shapes=scratch,
                compiler_params=params(),
                cost_estimate=pl.CostEstimate(flops=4_000_000, bytes_accessed=8_000_000, transcendentals=0),
                name="update",
            )(send_plane, send_row, send_cover, step_size, foot_lo, foot_hi, back, x)
            arrived += [swap(out) for out in outbound]
    return (x.reshape(model.shape), outs[1])


def solution(mesh):
    both = ("groups", "sky")
    return jax.shard_map(
        body,
        mesh=mesh,
        in_specs=(
            P(both, None, None, None),
            P(both, None, None),
            P(both),
            P(),
            P(both, None),
            P(both),
            P(both, None),
            P(both, None),
            P(both, None),
            P(both, None),
            P(both, None),
            P(both, None),
            P(both),
            P(both),
        ),
        out_specs=(P(both, None, None, None), P(both, None, None)),
        check_vma=False,
    )
```

```python
import functools

import jax
import jax.numpy as jnp
from jax import lax
from jax.experimental import pallas as pl
from jax.experimental.pallas import tpu as pltpu
from jax.sharding import PartitionSpec as P

NPSF = 4
TAPS = 7
ITERS = 2
LANES = 128
HALF = TAPS // 2
F32 = jnp.float32
BF16 = jnp.bfloat16
I32 = jnp.int32
VMEM_BYTES = 24 * 1024 * 1024

smem = lambda: pl.BlockSpec(memory_space=pltpu.SMEM)
vmem = lambda: pl.BlockSpec(memory_space=pltpu.VMEM)
hbm = lambda: pl.BlockSpec(memory_space=pl.ANY)


def params(share=1.0):
    return pltpu.CompilerParams(vmem_limit_bytes=int(share * VMEM_BYTES))


def aligned(rows):
    return -(-rows // 16) * 16


def pack_slots(plane_ref, row_ref, cover_ref, tile_rows, height, rows_each, x_ref, packed_ref):
    peers, capacity = plane_ref.shape

    def peer(d, _):
        at = d * rows_each
        for c in range(capacity):
            first = jnp.maximum(plane_ref[d, c], 0) * tile_rows + row_ref[d, c]
            packed_ref[pl.ds(at, height), :] = x_ref[pl.ds(first, height), :]
            at = at + cover_ref[d, c]
        return 0

    lax.fori_loop(0, peers, peer, 0, unroll=2)


def bank_rows(taps, height):
    count, width = taps.shape

    def grid(columns):
        return (
            lax.broadcasted_iota(I32, (width, columns), 0),
            lax.broadcasted_iota(I32, (width, columns), 1),
        )

    def select(x, mask):
        parts = []
        for _ in range(3):
            parts.append(x.astype(BF16).astype(F32))
            x = x - parts[-1]
        picked = jnp.dot(
            jnp.concatenate(parts, axis=0).astype(BF16), mask.astype(F32).astype(BF16), preferred_element_type=F32
        )
        return picked[:count] + picked[count : 2 * count] + picked[2 * count :]

    k, l = grid(width)
    unit = taps / select(taps, k // TAPS == l // TAPS)
    k, l = grid(2 * NPSF * LANES)
    mirror, j, l = l // (NPSF * LANES), l // LANES % NPSF, (l + HALF) % LANES
    i, t = l // height, l % height
    valid = (i < TAPS) & (t < TAPS)
    row_tap = j * TAPS + jnp.where(mirror == 1, t, TAPS - 1 - t)
    col_tap = (NPSF + j) * TAPS + jnp.where(mirror == 1, TAPS - 1 - i, i)
    row_part = select(unit, valid & (k == row_tap))
    col_part = select(unit, valid & (k == col_tap))
    product = row_part * col_part * (1.0 / NPSF)
    return [
        sum(product[:, (m * NPSF + j) * LANES : (m * NPSF + j + 1) * LANES] for j in range(NPSF)) for m in range(2)
    ]


def first_send_kernel(
    tile_rows, height, rows_each, plane_ref, row_ref, cover_ref, taps_ref, model_ref, out_ref, x_ref, packed_ref, bank_ref, sem
):
    peers = plane_ref.shape[0]
    total = model_ref.shape[0]
    load = pltpu.make_async_copy(model_ref, x_ref.at[pl.ds(0, total), :], sem)
    load.start()
    bank_ref[...] = jnp.zeros(bank_ref.shape, F32)
    for m, row in enumerate(bank_rows(taps_ref[...], height)):
        for n in range(taps_ref.shape[0]):
            bank_ref[2 * n + m : 2 * n + m + 1, :] = row[n : n + 1, :]
    bank = bank_ref[...].astype(BF16)
    load.wait()
    pack_slots(plane_ref, row_ref, cover_ref, tile_rows, height, rows_each, x_ref, packed_ref)
    for d in range(peers):
        out_ref[d, :rows_each, :] = packed_ref[d * rows_each : (d + 1) * rows_each, :].astype(BF16)
        out_ref[d, rows_each:, :] = bank


def update_kernel(
    bands,
    tile_rows,
    height,
    rows_each,
    last,
    plane_ref,
    row_ref,
    cover_ref,
    step_ref,
    lo_ref,
    hi_ref,
    returned_ref,
    model_ref,
    *rest,
):
    if last:
        new_ref, x_ref, back_ref, scale_ref, sem, saved, *more_refs = rest
    else:
        new_ref, out_ref, x_ref, back_ref, scale_ref, sem, saved, *more_refs, packed_ref = rest
    peers, capacity = plane_ref.shape
    total = model_ref.shape[0]
    planes = total // tile_rows
    load = pltpu.make_async_copy(model_ref, x_ref.at[pl.ds(0, total), :], sem)
    load.start()
    for p in range(planes):
        scale_ref[p] = step_ref[p % bands]
    for ref in more_refs:
        ref[...] = jnp.zeros(ref.shape, F32)
    for d in range(peers):
        back_ref[d * rows_each : (d + 1) * rows_each, :] = returned_ref[d].astype(F32)
    load.wait()
    place = lax.broadcasted_iota(I32, (height, LANES), 0)

    sums = [x_ref, *more_refs]

    def some_peers(step, _):
        at = [(step * len(sums) + n) * rows_each for n in range(len(sums))]
        for c in range(capacity):
            for n, ref in enumerate(sums):
                d = step * len(sums) + n
                p = jnp.maximum(plane_ref[d, c], 0)
                here = pl.ds(p * tile_rows + row_ref[d, c], height)
                cover = cover_ref[d, c]
                piece = jnp.where(place < cover, back_ref[pl.ds(at[n], height), :], 0.0)
                ref[here, :] = ref[here, :] - scale_ref[p] * piece
                at[n] = at[n] + cover
        return 0

    lax.fori_loop(0, peers // len(sums), some_peers, 0)

    pos = lax.broadcasted_iota(I32, (tile_rows, LANES), 0)
    saves = []
    for p in range(planes):
        inside = (pos >= lo_ref[p // bands]) & (pos < hi_ref[p // bands])
        here = slice(p * tile_rows, (p + 1) * tile_rows)
        new = sum((ref[here, :] for ref in more_refs), x_ref[here, :])
        x_ref[here, :] = jnp.where(inside, jnp.maximum(new, 0.0), 0.0)
        rows = pl.ds(p * tile_rows, tile_rows)
        saves.append(pltpu.make_async_copy(x_ref.at[rows, :], new_ref.at[rows, :], saved.at[p]))
        saves[-1].start()
    if not last:
        pack_slots(plane_ref, row_ref, cover_ref, tile_rows, height, rows_each, x_ref, packed_ref)
        for d in range(peers):
            out_ref[d, :, :] = packed_ref[d * rows_each : (d + 1) * rows_each, :].astype(BF16)
    for save in saves:
        save.wait()


def tables_kernel(capacity, height, rows_each, slot_ref, start_ref, stop_ref, table_ref, length_ref):
    exposures, pieces = slot_ref.shape
    slots = length_ref.shape[0]
    stamp_row, return_row = 2 * pieces, 2 * pieces + 1

    def clear(s, _):
        length_ref[s] = 0
        table_ref[stamp_row, s] = 0
        return 0

    lax.fori_loop(0, slots, clear, 0, unroll=8)

    def measure(e, _):
        for k in range(pieces):
            s = slot_ref[e, k]

            @pl.when(s >= 0)
            def _():
                length_ref[s] = stop_ref[e, k] - start_ref[e, k]
                table_ref[stamp_row, s] = e * height + start_ref[e, k]

        return 0

    lax.fori_loop(0, exposures, measure, 0, unroll=2)

    def lay(o, _):
        at = o * rows_each
        for c in range(capacity):
            s = o * capacity + c
            table_ref[return_row, s] = at
            at = at + length_ref[s]
        return 0

    lax.fori_loop(0, slots // capacity, lay, 0)

    def point(e, _):
        for k in range(pieces):
            s = slot_ref[e, k]
            live = s >= 0
            begin = table_ref[return_row, jnp.maximum(s, 0)]
            table_ref[2 * k, e] = jnp.where(live, height + begin - start_ref[e, k], 0)
            table_ref[2 * k + 1, e] = jnp.where(live, start_ref[e, k], height)
        return 0

    lax.fori_loop(0, exposures, point, 0, unroll=2)


def blur_kernel(
    height,
    pieces,
    batches_each,
    last,
    table_in_ref,
    weight_ref,
    batch_ref,
    arrived_ref,
    bank_in_ref,
    seen_ref,
    *rest,
):
    if last:
        out_ref, residual_out_ref, *rest = rest
        *rest, residual_ref, sent = rest
    else:
        out_ref, *rest = rest
    table_ref, sem, rows_ref, bank_ref, result_ref, packed_ref, held_ref, blur_ref, back_ref = rest
    load = pltpu.make_async_copy(table_in_ref, table_ref, sem)
    load.start()
    peers, rows_each, _ = out_ref.shape
    extra = bank_in_ref.shape[1]
    exposures = batch_ref.shape[0]
    slots = peers * (2 * rows_each // height)
    abreast = max(n for n in (1, 2, 4, 8, 16, 32) if exposures % n == 0)
    place = lax.broadcasted_iota(I32, (height, LANES), 0)
    lane = lax.broadcasted_iota(I32, (height, LANES), 1)
    for o in range(peers):
        rows_ref[height + o * rows_each : height + (o + 1) * rows_each, :] = arrived_ref[o].astype(F32)
        bank_ref[o * extra : (o + 1) * extra, :] = bank_in_ref[o].astype(F32)

    gap = lane % height - place
    near = (gap <= HALF) & (gap >= -HALF) & (lane < TAPS * height)

    def operators(o, _):
        for n in range(batches_each):
            for m, ref in enumerate((blur_ref, back_ref)):
                taps = jnp.broadcast_to(bank_ref[pl.ds(o * extra + 2 * n + m, 1), :], (height, LANES))
                ref[o * batches_each + n] = jnp.where(
                    near, pltpu.roll(taps, 0, 1, stride=1, stride_axis=0), 0.0
                ).astype(BF16)
        return 0

    lax.fori_loop(0, peers, operators, 0, unroll=4)

    def shifted(x):
        parts = []
        for v in range(-HALF, HALF + 1):
            moved = x if v == 0 else pltpu.roll(x, v % LANES, 1)
            parts.append(jnp.where((lane >= v) & (lane < LANES + v), moved, jnp.zeros((), BF16)))
        parts.append(jnp.zeros((LANES - TAPS * height, LANES), BF16))
        return jnp.concatenate(parts, axis=0)

    def correlate(s):
        for q in range(abreast):
            e = s * abreast + q
            here = pl.ds(e * height, height)
            result_ref[here, :] = jnp.dot(
                back_ref[batch_ref[e]], shifted(held_ref[here, :]), preferred_element_type=F32
            )

    def blur(s):
        for q in range(abreast):
            e = s * abreast + q
            stamp = rows_ref[pl.ds(table_ref[0, e], height), :]
            for k in range(1, pieces):
                piece = rows_ref[pl.ds(table_ref[2 * k, e], height), :]
                stamp = jnp.where(place >= table_ref[2 * k + 1, e], piece, stamp)
            predicted = jnp.dot(
                blur_ref[batch_ref[e]], shifted(stamp.astype(BF16)), preferred_element_type=F32
            )
            residual = weight_ref[e] * (predicted - seen_ref[e].astype(F32))
            if last:
                residual_ref[e] = residual
            held_ref[pl.ds(e * height, height), :] = residual.astype(BF16)

    steps = exposures // abreast

    def send(s):
        some = pl.ds(s * abreast, abreast)
        return pltpu.make_async_copy(residual_ref.at[some], residual_out_ref.at[some], sent.at[s])

    load.wait()
    for s in range(steps + 1):
        if s > 0:
            correlate(s - 1)
        if s < steps:
            blur(s)
            if last:
                send(s).start()

    def move(s, _):
        packed_ref[pl.ds(table_ref[2 * pieces + 1, s], height), :] = result_ref[
            pl.ds(table_ref[2 * pieces, s], height), :
        ]
        return 0

    lax.fori_loop(0, slots, move, 0, unroll=16)
    for o in range(peers):
        out_ref[o, :, :] = packed_ref[o * rows_each : (o + 1) * rows_each, :].astype(BF16)
    if last:
        for s in range(steps):
            send(s).wait()


def body(
    model,
    exposures,
    inv_var,
    step_size,
    psf_taps,
    exp_batch,
    send_plane,
    send_row,
    send_cover,
    use_slot,
    use_start,
    use_stop,
    foot_lo,
    foot_hi,
):
    tile_count, bands, tile_rows, columns = model.shape
    count, height, _ = exposures.shape
    peers, capacity = send_plane.shape
    pieces = use_slot.shape[1]
    total = tile_count * bands * tile_rows
    rows_each = capacity * height // 2
    batches_each = psf_taps.shape[0]
    extra = aligned(batches_each * 2)
    block = rows_each + extra
    assert columns == LANES and rows_each % extra == 0 and TAPS * height <= LANES - HALF
    x = model.reshape(total, columns)

    def swap(a):
        return lax.all_to_all(a, "sky", split_axis=0, concat_axis=0, tiled=True)

    outbound = pl.pallas_call(
        functools.partial(first_send_kernel, tile_rows, height, rows_each),
        out_shape=jax.ShapeDtypeStruct((peers, block, columns), BF16),
        in_specs=[smem(), smem(), smem(), vmem(), hbm()],
        out_specs=vmem(),
        scratch_shapes=[
            pltpu.VMEM((total + height, columns), F32),
            pltpu.VMEM((peers * rows_each + height, columns), F32),
            pltpu.VMEM((extra, columns), F32),
            pltpu.SemaphoreType.DMA,
        ],
        compiler_params=params(2.5),
        name="first_send",
    )(send_plane, send_row, send_cover, psf_taps, x)
    arrived = swap(outbound)
    table = pl.pallas_call(
        functools.partial(tables_kernel, capacity, height, rows_each),
        out_shape=jax.ShapeDtypeStruct((2 * pieces + 2, max(count, peers * capacity)), I32),
        in_specs=[smem(), smem(), smem()],
        out_specs=smem(),
        scratch_shapes=[pltpu.SMEM((peers * capacity,), I32)],
        cost_estimate=pl.CostEstimate(flops=4_000_000, bytes_accessed=8_000_000, transcendentals=0),
        name="tables",
    )(use_slot, use_start, use_stop)
    with_bank = arrived
    for sweep in range(ITERS):
        last = sweep == ITERS - 1
        rows_shape = jax.ShapeDtypeStruct((peers, rows_each, columns), BF16)
        outs = pl.pallas_call(
            functools.partial(blur_kernel, height, pieces, batches_each, last),
            grid=(1,),
            out_shape=(rows_shape, jax.ShapeDtypeStruct(exposures.shape, F32)) if last else rows_shape,
            in_specs=[
                hbm(),
                smem(),
                smem(),
                pl.BlockSpec((peers, rows_each, columns), lambda i: (0, 0, 0)),
                pl.BlockSpec((peers, extra, columns), lambda i: (0, rows_each // extra, 0)),
                vmem(),
            ],
            out_specs=(vmem(), hbm()) if last else vmem(),
            scratch_shapes=[
                pltpu.SMEM(table.shape, I32),
                pltpu.SemaphoreType.DMA,
                pltpu.VMEM((peers * rows_each + 2 * height, columns), F32),
                pltpu.VMEM((peers * extra, columns), F32),
                pltpu.VMEM((count * height + height, columns), F32),
                pltpu.VMEM((peers * rows_each + height, columns), F32),
                pltpu.VMEM((count * height, columns), BF16),
                pltpu.VMEM((peers * batches_each, height, LANES), BF16),
                pltpu.VMEM((peers * batches_each, height, LANES), BF16),
            ]
            + [pltpu.VMEM(exposures.shape, F32), pltpu.SemaphoreType.DMA((count,))] * last,
            compiler_params=params(),
            name="blur",
        )(table, inv_var, exp_batch, arrived, with_bank, exposures)
        outgoing = outs[0] if last else outs
        returned = swap(outgoing)
        new_shape = jax.ShapeDtypeStruct((total, columns), F32)
        scratch = [
            pltpu.VMEM((total + height, columns), F32),
            pltpu.VMEM((peers * rows_each + height, columns), F32),
            pltpu.SMEM((tile_count * bands,), F32),
            pltpu.SemaphoreType.DMA,
            pltpu.SemaphoreType.DMA((tile_count * bands,)),
        ]
        sums = max(n for n in (1, 2, 4) if peers % n == 0)
        scratch += [pltpu.VMEM((total + height, columns), F32)] * (sums - 1)
        if not last:
            scratch.append(pltpu.VMEM((peers * rows_each + height, columns), F32))
        res = pl.pallas_call(
            functools.partial(update_kernel, bands, tile_rows, height, rows_each, last),
            out_shape=new_shape if last else (new_shape, rows_shape),
            in_specs=[smem()] * 6 + [vmem(), hbm()],
            out_specs=hbm() if last else (hbm(), vmem()),
            scratch_shapes=scratch,
            compiler_params=params(),
            name="update",
        )(send_plane, send_row, send_cover, step_size, foot_lo, foot_hi, returned, x)
        if last:
            x = res
        else:
            x, outbound = res
            arrived = swap(outbound)
    return (x.reshape(model.shape), outs[1])


def solution(mesh):
    both = ("groups", "sky")
    return jax.shard_map(
        body,
        mesh=mesh,
        in_specs=(
            P(both, None, None, None),
            P(both, None, None),
            P(both),
            P(),
            P(both, None),
            P(both),
            P(both, None),
            P(both, None),
            P(both, None),
            P(both, None),
            P(both, None),
            P(both, None),
            P(both),
            P(both),
        ),
        out_specs=(P(both, None, None, None), P(both, None, None)),
        check_vma=False,
    )
```

```python
import functools

import jax
import jax.numpy as jnp
from jax import lax
from jax.experimental import pallas as pl
from jax.experimental.pallas import tpu as pltpu
from jax.sharding import PartitionSpec as P

NPSF = 4
TAPS = 7
ITERS = 2
LANES = 128
HALF = TAPS // 2
F32 = jnp.float32
BF16 = jnp.bfloat16
I32 = jnp.int32
VMEM_BYTES = 24 * 1024 * 1024

smem = lambda: pl.BlockSpec(memory_space=pltpu.SMEM)
vmem = lambda: pl.BlockSpec(memory_space=pltpu.VMEM)
hbm = lambda: pl.BlockSpec(memory_space=pltpu.HBM)


def params():
    return pltpu.CompilerParams(vmem_limit_bytes=VMEM_BYTES)


def aligned(rows):
    return -(-rows // 16) * 16


def pack_slots(plane_ref, row_ref, cover_ref, tile_rows, height, rows_each, x_ref, packed_ref):
    peers, capacity = plane_ref.shape

    def peer(d, _):
        at = d * rows_each
        for c in range(capacity):
            first = jnp.maximum(plane_ref[d, c], 0) * tile_rows + row_ref[d, c]
            packed_ref[pl.ds(at, height), :] = x_ref[pl.ds(first, height), :]
            at = at + cover_ref[d, c]
        return 0

    lax.fori_loop(0, peers, peer, 0, unroll=2)


def bank_rows(taps, height):
    count, width = taps.shape

    def grid(columns):
        return (
            lax.broadcasted_iota(I32, (width, columns), 0),
            lax.broadcasted_iota(I32, (width, columns), 1),
        )

    def select(x, mask):
        parts = []
        for _ in range(3):
            parts.append(x.astype(BF16).astype(F32))
            x = x - parts[-1]
        picked = jnp.dot(
            jnp.concatenate(parts, axis=0).astype(BF16), mask.astype(F32).astype(BF16), preferred_element_type=F32
        )
        return picked[:count] + picked[count : 2 * count] + picked[2 * count :]

    k, l = grid(width)
    unit = taps / select(taps, k // TAPS == l // TAPS)
    k, l = grid(2 * NPSF * LANES)
    mirror, j, l = l // (NPSF * LANES), l // LANES % NPSF, (l + HALF) % LANES
    i, t = l // height, l % height
    valid = (i < TAPS) & (t < TAPS)
    row_tap = j * TAPS + jnp.where(mirror == 1, t, TAPS - 1 - t)
    col_tap = (NPSF + j) * TAPS + jnp.where(mirror == 1, TAPS - 1 - i, i)
    row_part = select(unit, valid & (k == row_tap))
    col_part = select(unit, valid & (k == col_tap))
    product = row_part * col_part * (1.0 / NPSF)
    return [
        sum(product[:, (m * NPSF + j) * LANES : (m * NPSF + j + 1) * LANES] for j in range(NPSF)) for m in range(2)
    ]


def first_send_kernel(
    tile_rows,
    height,
    rows_each,
    plane_in_ref,
    row_in_ref,
    cover_in_ref,
    taps_in_ref,
    model_ref,
    out_ref,
    plane_ref,
    row_ref,
    cover_ref,
    taps_ref,
    x_ref,
    packed_ref,
    bank_ref,
    sems,
):
    peers = plane_ref.shape[0]
    pairs = (
        (taps_in_ref, taps_ref),
        (model_ref, x_ref.at[pl.ds(0, model_ref.shape[0]), :]),
        (plane_in_ref, plane_ref),
        (row_in_ref, row_ref),
        (cover_in_ref, cover_ref),
    )
    loads = [pltpu.make_async_copy(*pair, sems.at[n]) for n, pair in enumerate(pairs)]
    for load in loads:
        load.start()
    bank_ref[...] = jnp.zeros(bank_ref.shape, F32)
    loads[0].wait()
    for m, row in enumerate(bank_rows(taps_ref[...], height)):
        for n in range(taps_ref.shape[0]):
            bank_ref[2 * n + m : 2 * n + m + 1, :] = row[n : n + 1, :]
    bank = bank_ref[...].astype(BF16)
    for load in loads[1:]:
        load.wait()
    pack_slots(plane_ref, row_ref, cover_ref, tile_rows, height, rows_each, x_ref, packed_ref)
    for d in range(peers):
        out_ref[d, :rows_each, :] = packed_ref[d * rows_each : (d + 1) * rows_each, :].astype(BF16)
        out_ref[d, rows_each:, :] = bank


def update_kernel(
    bands,
    tile_rows,
    height,
    rows_each,
    last,
    plane_ref,
    row_ref,
    cover_ref,
    step_ref,
    lo_ref,
    hi_ref,
    returned_ref,
    model_ref,
    *rest,
):
    if last:
        new_ref, back_ref, scale_ref, x_ref, saved, *more_refs = rest
    else:
        x_ref, out_ref, back_ref, scale_ref, packed_ref, *more_refs = rest
    peers, capacity = plane_ref.shape
    total = x_ref.shape[0] - height
    planes = total // tile_rows
    for p in range(planes):
        scale_ref[p] = step_ref[p % bands]
    x_ref[:total, :] = model_ref[:total, :]
    for ref in more_refs:
        ref[...] = jnp.zeros(ref.shape, F32)
    for d in range(peers):
        back_ref[d * rows_each : (d + 1) * rows_each, :] = returned_ref[d].astype(F32)
    place = lax.broadcasted_iota(I32, (height, LANES), 0)

    sums = [x_ref, *more_refs]

    def some_peers(step, _):
        at = [(step * len(sums) + n) * rows_each for n in range(len(sums))]
        for c in range(capacity):
            for n, ref in enumerate(sums):
                d = step * len(sums) + n
                p = jnp.maximum(plane_ref[d, c], 0)
                here = pl.ds(p * tile_rows + row_ref[d, c], height)
                cover = cover_ref[d, c]
                piece = jnp.where(place < cover, back_ref[pl.ds(at[n], height), :], 0.0)
                ref[here, :] = ref[here, :] - scale_ref[p] * piece
                at[n] = at[n] + cover
        return 0

    lax.fori_loop(0, peers // len(sums), some_peers, 0)

    pos = lax.broadcasted_iota(I32, (tile_rows, LANES), 0)
    saves = []
    for p in range(planes):
        inside = (pos >= lo_ref[p // bands]) & (pos < hi_ref[p // bands])
        here = slice(p * tile_rows, (p + 1) * tile_rows)
        new = sum((ref[here, :] for ref in more_refs), x_ref[here, :])
        x_ref[here, :] = jnp.where(inside, jnp.maximum(new, 0.0), 0.0)
        if last:
            rows = pl.ds(p * tile_rows, tile_rows)
            saves.append(pltpu.make_async_copy(x_ref.at[rows, :], new_ref.at[rows, :], saved.at[p]))
            saves[-1].start()
    if not last:
        pack_slots(plane_ref, row_ref, cover_ref, tile_rows, height, rows_each, x_ref, packed_ref)
        for d in range(peers):
            out_ref[d, :, :] = packed_ref[d * rows_each : (d + 1) * rows_each, :].astype(BF16)
    for save in saves:
        save.wait()


def tables_kernel(capacity, height, rows_each, slot_ref, start_ref, stop_ref, table_ref, length_ref):
    exposures, pieces = slot_ref.shape
    slots = length_ref.shape[0]
    stamp_row, return_row = 2 * pieces, 2 * pieces + 1

    def clear(s, _):
        length_ref[s] = 0
        table_ref[stamp_row, s] = 0
        return 0

    lax.fori_loop(0, slots, clear, 0, unroll=8)

    def measure(e, _):
        for k in range(pieces):
            s = slot_ref[e, k]

            @pl.when(s >= 0)
            def _():
                length_ref[s] = stop_ref[e, k] - start_ref[e, k]
                table_ref[stamp_row, s] = e * height + start_ref[e, k]

        return 0

    lax.fori_loop(0, exposures, measure, 0, unroll=2)

    def lay(o, _):
        at = o * rows_each
        for c in range(capacity):
            s = o * capacity + c
            table_ref[return_row, s] = at
            at = at + length_ref[s]
        return 0

    lax.fori_loop(0, slots // capacity, lay, 0)

    def point(e, _):
        for k in range(pieces):
            s = slot_ref[e, k]
            live = s >= 0
            begin = table_ref[return_row, jnp.maximum(s, 0)]
            table_ref[2 * k, e] = jnp.where(live, height + begin - start_ref[e, k], 0)
            table_ref[2 * k + 1, e] = jnp.where(live, start_ref[e, k], height)
        return 0

    lax.fori_loop(0, exposures, point, 0, unroll=2)


def blur_kernel(
    height,
    pieces,
    batches_each,
    last,
    table_in_ref,
    weight_ref,
    batch_ref,
    arrived_ref,
    bank_in_ref,
    seen_ref,
    *rest,
):
    if last:
        out_ref, residual_out_ref, *rest = rest
        *rest, residual_ref, sent = rest
        send = pltpu.make_async_copy(residual_ref, residual_out_ref, sent)
    else:
        out_ref, *rest = rest
    table_ref, sem, rows_ref, bank_ref, result_ref, packed_ref, held_ref, blur_ref, back_ref = rest
    load = pltpu.make_async_copy(table_in_ref, table_ref, sem)
    load.start()
    peers, rows_each, _ = out_ref.shape
    extra = bank_in_ref.shape[1] - rows_each
    exposures = batch_ref.shape[0]
    slots = peers * (2 * rows_each // height)
    abreast = max(n for n in (1, 2, 4, 8, 16, 32) if exposures % n == 0)
    place = lax.broadcasted_iota(I32, (height, LANES), 0)
    lane = lax.broadcasted_iota(I32, (height, LANES), 1)
    for o in range(peers):
        rows_ref[height + o * rows_each : height + (o + 1) * rows_each, :] = arrived_ref[o, :rows_each, :].astype(F32)
        bank_ref[o * extra : (o + 1) * extra, :] = bank_in_ref[o, rows_each:, :].astype(F32)

    gap = lane % height - place
    near = (gap <= HALF) & (gap >= -HALF) & (lane < TAPS * height)

    def operators(o, _):
        for n in range(batches_each):
            for m, ref in enumerate((blur_ref, back_ref)):
                taps = jnp.broadcast_to(bank_ref[pl.ds(o * extra + 2 * n + m, 1), :], (height, LANES))
                ref[o * batches_each + n] = jnp.where(
                    near, pltpu.roll(taps, 0, 1, stride=1, stride_axis=0), 0.0
                ).astype(BF16)
        return 0

    lax.fori_loop(0, peers, operators, 0, unroll=4)

    def shifted(x):
        parts = []
        for v in range(-HALF, HALF + 1):
            moved = x if v == 0 else pltpu.roll(x, v % LANES, 1)
            parts.append(jnp.where((lane >= v) & (lane < LANES + v), moved, jnp.zeros((), BF16)))
        parts.append(jnp.zeros((LANES - TAPS * height, LANES), BF16))
        return jnp.concatenate(parts, axis=0)

    def correlate(s):
        for q in range(abreast):
            e = s * abreast + q
            here = pl.ds(e * height, height)
            result_ref[here, :] = jnp.dot(
                back_ref[batch_ref[e]], shifted(held_ref[here, :]), preferred_element_type=F32
            )

    def blur(s):
        for q in range(abreast):
            e = s * abreast + q
            stamp = rows_ref[pl.ds(table_ref[0, e], height), :]
            for k in range(1, pieces):
                piece = rows_ref[pl.ds(table_ref[2 * k, e], height), :]
                stamp = jnp.where(place >= table_ref[2 * k + 1, e], piece, stamp)
            predicted = jnp.dot(
                blur_ref[batch_ref[e]], shifted(stamp.astype(BF16)), preferred_element_type=F32
            )
            residual = weight_ref[e] * (predicted - seen_ref[e].astype(F32))
            if last:
                residual_ref[e] = residual
            held_ref[pl.ds(e * height, height), :] = residual.astype(BF16)

    steps = exposures // abreast

    load.wait()
    for s in range(steps + 1):
        if s > 0:
            correlate(s - 1)
        if s < steps:
            blur(s)
    if last:
        send.start()

    def move(s, _):
        packed_ref[pl.ds(table_ref[2 * pieces + 1, s], height), :] = result_ref[
            pl.ds(table_ref[2 * pieces, s], height), :
        ]
        return 0

    lax.fori_loop(0, slots, move, 0, unroll=16)
    for o in range(peers):
        out_ref[o, :, :] = packed_ref[o * rows_each : (o + 1) * rows_each, :].astype(BF16)
    if last:
        send.wait()


def body(
    model,
    exposures,
    inv_var,
    step_size,
    psf_taps,
    exp_batch,
    send_plane,
    send_row,
    send_cover,
    use_slot,
    use_start,
    use_stop,
    foot_lo,
    foot_hi,
):
    tile_count, bands, tile_rows, columns = model.shape
    count, height, _ = exposures.shape
    peers, capacity = send_plane.shape
    pieces = use_slot.shape[1]
    total = tile_count * bands * tile_rows
    rows_each = capacity * height // 2
    batches_each = psf_taps.shape[0]
    extra = aligned(batches_each * 2)
    block = rows_each + extra
    assert columns == LANES and rows_each % extra == 0 and TAPS * height <= LANES - HALF
    x = model.reshape(total, columns)

    def swap(a):
        return lax.all_to_all(a, "sky", split_axis=0, concat_axis=0, tiled=True)

    outbound = pl.pallas_call(
        functools.partial(first_send_kernel, tile_rows, height, rows_each),
        out_shape=jax.ShapeDtypeStruct((peers, block, columns), BF16),
        in_specs=[hbm()] * 5,
        out_specs=vmem(),
        scratch_shapes=[
            pltpu.SMEM(send_plane.shape, I32),
            pltpu.SMEM(send_row.shape, I32),
            pltpu.SMEM(send_cover.shape, I32),
            pltpu.VMEM(psf_taps.shape, F32),
            pltpu.VMEM((total + height, columns), F32),
            pltpu.VMEM((peers * rows_each + height, columns), F32),
            pltpu.VMEM((extra, columns), F32),
            pltpu.SemaphoreType.DMA((5,)),
        ],
        compiler_params=params(),
        name="first_send",
    )(send_plane, send_row, send_cover, psf_taps, x)
    arrived = swap(outbound)
    table = pl.pallas_call(
        functools.partial(tables_kernel, capacity, height, rows_each),
        out_shape=jax.ShapeDtypeStruct((2 * pieces + 2, max(count, peers * capacity)), I32),
        in_specs=[smem(), smem(), smem()],
        out_specs=smem(),
        scratch_shapes=[pltpu.SMEM((peers * capacity,), I32)],
        cost_estimate=pl.CostEstimate(flops=4_000_000, bytes_accessed=8_000_000, transcendentals=0),
        name="tables",
    )(use_slot, use_start, use_stop)
    with_bank = arrived
    for sweep in range(ITERS):
        last = sweep == ITERS - 1
        rows_shape = jax.ShapeDtypeStruct((peers, rows_each, columns), BF16)
        outs = pl.pallas_call(
            functools.partial(blur_kernel, height, pieces, batches_each, last),
            out_shape=(rows_shape, jax.ShapeDtypeStruct(exposures.shape, F32)) if last else rows_shape,
            in_specs=[
                hbm(),
                smem(),
                smem(),
                vmem(),
                vmem(),
                vmem(),
            ],
            out_specs=(vmem(), hbm()) if last else vmem(),
            scratch_shapes=[
                pltpu.SMEM(table.shape, I32),
                pltpu.SemaphoreType.DMA,
                pltpu.VMEM((peers * rows_each + 2 * height, columns), F32),
                pltpu.VMEM((peers * extra, columns), F32),
                pltpu.VMEM((count * height + height, columns), F32),
                pltpu.VMEM((peers * rows_each + height, columns), F32),
                pltpu.VMEM((count * height, columns), BF16),
                pltpu.VMEM((peers * batches_each, height, LANES), BF16),
                pltpu.VMEM((peers * batches_each, height, LANES), BF16),
            ]
            + [pltpu.VMEM(exposures.shape, F32), pltpu.SemaphoreType.DMA] * last,
            compiler_params=params(),
            name="blur",
        )(table, inv_var, exp_batch, arrived, with_bank, exposures)
        outgoing = outs[0] if last else outs
        returned = swap(outgoing)
        new_shape = jax.ShapeDtypeStruct((total, columns), F32)
        padded = (total + height, columns)
        scratch = [pltpu.VMEM((peers * rows_each + height, columns), F32), pltpu.SMEM((tile_count * bands,), F32)]
        if last:
            scratch += [pltpu.VMEM(padded, F32), pltpu.SemaphoreType.DMA((tile_count * bands,))]
        else:
            scratch.append(pltpu.VMEM((peers * rows_each + height, columns), F32))
        sums = max(n for n in (1, 2, 4) if peers % n == 0)
        res = pl.pallas_call(
            functools.partial(update_kernel, bands, tile_rows, height, rows_each, last),
            out_shape=jax.ShapeDtypeStruct((total, columns), F32)
            if last
            else (jax.ShapeDtypeStruct(padded, F32), rows_shape),
            in_specs=[smem()] * 6 + [vmem(), vmem()],
            out_specs=hbm() if last else (vmem(), vmem()),
            scratch_shapes=scratch + [pltpu.VMEM(padded, F32)] * (sums - 1),
            compiler_params=params(),
            name="update",
        )(send_plane, send_row, send_cover, step_size, foot_lo, foot_hi, returned, x)
        if last:
            x = res
        else:
            x, outbound = res
            arrived = swap(outbound)
    return (x.reshape(model.shape), outs[1])


def solution(mesh):
    both = ("groups", "sky")
    return jax.shard_map(
        body,
        mesh=mesh,
        in_specs=(
            P(both, None, None, None),
            P(both, None, None),
            P(both),
            P(),
            P(both, None),
            P(both),
            P(both, None),
            P(both, None),
            P(both, None),
            P(both, None),
            P(both, None),
            P(both, None),
            P(both),
            P(both),
        ),
        out_specs=(P(both, None, None, None), P(both, None, None)),
        check_vma=False,
    )
```

```python
import functools

import jax
import jax.numpy as jnp
from jax import lax
from jax.experimental import pallas as pl
from jax.experimental.pallas import tpu as pltpu
from jax.sharding import PartitionSpec as P

NPSF = 4
TAPS = 7
ITERS = 2
LANES = 128
HALF = TAPS // 2
F32 = jnp.float32
BF16 = jnp.bfloat16
I32 = jnp.int32
VMEM_BYTES = 24 * 1024 * 1024

smem = lambda: pl.BlockSpec(memory_space=pltpu.SMEM)
vmem = lambda: pl.BlockSpec(memory_space=pltpu.VMEM)
hbm = lambda: pl.BlockSpec(memory_space=pltpu.HBM)


def params(share=1.0):
    return pltpu.CompilerParams(vmem_limit_bytes=int(share * VMEM_BYTES))


def table_rows(pieces):
    return range(2 * pieces, 2 * pieces + 7)


def aligned(rows):
    return -(-rows // 16) * 16


def pack_slots(plane_ref, row_ref, cover_ref, tile_rows, height, rows_each, x_ref, packed_ref):
    peers, capacity = plane_ref.shape

    def peer(d, _):
        at = d * rows_each
        for c in range(capacity):
            first = jnp.maximum(plane_ref[d, c], 0) * tile_rows + row_ref[d, c]
            packed_ref[pl.ds(at, height), :] = x_ref[pl.ds(first, height), :]
            at = at + cover_ref[d, c]
        return 0

    lax.fori_loop(0, peers, peer, 0, unroll=2)


def bank_rows(taps, height):
    count, width = taps.shape

    def grid(columns):
        return (
            lax.broadcasted_iota(I32, (width, columns), 0),
            lax.broadcasted_iota(I32, (width, columns), 1),
        )

    def select(x, mask):
        parts = []
        for _ in range(3):
            parts.append(x.astype(BF16).astype(F32))
            x = x - parts[-1]
        picked = jnp.dot(
            jnp.concatenate(parts, axis=0).astype(BF16), mask.astype(F32).astype(BF16), preferred_element_type=F32
        )
        return picked[:count] + picked[count : 2 * count] + picked[2 * count :]

    k, l = grid(width)
    unit = taps / select(taps, k // TAPS == l // TAPS)
    k, l = grid(2 * NPSF * LANES)
    mirror, j, l = l // (NPSF * LANES), l // LANES % NPSF, (l + HALF) % LANES
    i, t = l // height, l % height
    valid = (i < TAPS) & (t < TAPS)
    row_tap = j * TAPS + jnp.where(mirror == 1, t, TAPS - 1 - t)
    col_tap = (NPSF + j) * TAPS + jnp.where(mirror == 1, TAPS - 1 - i, i)
    row_part = select(unit, valid & (k == row_tap))
    col_part = select(unit, valid & (k == col_tap))
    product = row_part * col_part * (1.0 / NPSF)
    return [
        sum(product[:, (m * NPSF + j) * LANES : (m * NPSF + j + 1) * LANES] for j in range(NPSF)) for m in range(2)
    ]


def first_send_kernel(
    tile_rows,
    height,
    rows_each,
    plane_in_ref,
    row_in_ref,
    cover_in_ref,
    taps_in_ref,
    model_ref,
    out_ref,
    plane_ref,
    row_ref,
    cover_ref,
    taps_ref,
    x_ref,
    packed_ref,
    bank_ref,
    sems,
):
    peers = plane_ref.shape[0]
    pairs = (
        (taps_in_ref, taps_ref),
        (model_ref, x_ref.at[pl.ds(0, model_ref.shape[0]), :]),
        (plane_in_ref, plane_ref),
        (row_in_ref, row_ref),
        (cover_in_ref, cover_ref),
    )
    loads = [pltpu.make_async_copy(*pair, sems.at[n]) for n, pair in enumerate(pairs)]
    for load in loads:
        load.start()
    bank_ref[...] = jnp.zeros(bank_ref.shape, F32)
    loads[0].wait()
    for m, row in enumerate(bank_rows(taps_ref[...], height)):
        for n in range(taps_ref.shape[0]):
            bank_ref[2 * n + m : 2 * n + m + 1, :] = row[n : n + 1, :]
    bank = bank_ref[...].astype(BF16)
    for load in loads[1:]:
        load.wait()
    pack_slots(plane_ref, row_ref, cover_ref, tile_rows, height, rows_each, x_ref, packed_ref)
    for d in range(peers):
        out_ref[d, :rows_each, :] = packed_ref[d * rows_each : (d + 1) * rows_each, :].astype(BF16)
        out_ref[d, rows_each:, :] = bank


def update_kernel(pieces, bands, tile_rows, height, last, table_ref, factor_ref, returned_ref, model_ref, *rest):
    if last:
        new_ref, back_ref, x_ref, saved, *more_refs = rest
    else:
        x_ref, out_ref, back_ref, packed_ref, *more_refs = rest
    _, _, _, first_row, cover_row, sent_row, foot_row = table_rows(pieces)
    peers, rows_each, _ = returned_ref.shape
    capacity = 2 * rows_each // height
    total = x_ref.shape[0] - height
    planes = total // tile_rows
    tiles = planes // bands
    x_ref[:total, :] = model_ref[:total, :]
    for ref in more_refs:
        ref[...] = jnp.zeros(ref.shape, F32)
    for d in range(peers):
        back_ref[d * rows_each : (d + 1) * rows_each, :] = returned_ref[d].astype(F32)
    place = lax.broadcasted_iota(I32, (height, LANES), 0)

    sums = [x_ref, *more_refs]

    def some_peers(step, _):
        for c in range(capacity):
            for n, ref in enumerate(sums):
                slot = (step * len(sums) + n) * capacity + c
                here = pl.ds(table_ref[first_row, slot], height)
                piece = back_ref[pl.ds(table_ref[sent_row, slot], height), :]
                piece = jnp.where(place < table_ref[cover_row, slot], piece, 0.0)
                ref[here, :] = ref[here, :] - factor_ref[1, slot] * piece
        return 0

    lax.fori_loop(0, peers // len(sums), some_peers, 0)

    pos = lax.broadcasted_iota(I32, (tile_rows, LANES), 0)
    saves = []
    for p in range(planes):
        inside = (pos >= table_ref[foot_row, p // bands]) & (pos < table_ref[foot_row, tiles + p // bands])
        here = slice(p * tile_rows, (p + 1) * tile_rows)
        new = sum((ref[here, :] for ref in more_refs), x_ref[here, :])
        x_ref[here, :] = jnp.where(inside, jnp.maximum(new, 0.0), 0.0)
        if last:
            rows = pl.ds(p * tile_rows, tile_rows)
            saves.append(pltpu.make_async_copy(x_ref.at[rows, :], new_ref.at[rows, :], saved.at[p]))
            saves[-1].start()
    if not last:

        def pack(slot, _):
            piece = x_ref[pl.ds(table_ref[first_row, slot], height), :]
            packed_ref[pl.ds(table_ref[sent_row, slot], height), :] = piece
            return 0

        lax.fori_loop(0, peers * capacity, pack, 0, unroll=16)
        for d in range(peers):
            out_ref[d, :, :] = packed_ref[d * rows_each : (d + 1) * rows_each, :].astype(BF16)
    for save in saves:
        save.wait()


def tables_kernel(
    tile_rows,
    bands,
    height,
    rows_each,
    slot_ref,
    start_ref,
    stop_ref,
    batch_ref,
    weight_ref,
    plane_ref,
    row_ref,
    cover_ref,
    step_ref,
    lo_ref,
    hi_ref,
    table_ref,
    factor_ref,
    length_ref,
    scale_ref,
):
    pieces, exposures = slot_ref.shape
    peers, capacity = plane_ref.shape
    slots = peers * capacity
    batch_row, stamp_row, return_row, first_row, cover_row, sent_row, foot_row = table_rows(pieces)

    def clear(s, _):
        length_ref[s] = 0
        table_ref[stamp_row, s] = 0
        return 0

    lax.fori_loop(0, slots, clear, 0, unroll=16)
    for p in range(scale_ref.shape[0]):
        scale_ref[p] = step_ref[p % bands]
    tiles = lo_ref.shape[0]
    for t in range(tiles):
        table_ref[foot_row, t] = lo_ref[t]
        table_ref[foot_row, tiles + t] = hi_ref[t]

    def measure(e, _):
        for k in range(pieces):
            s = slot_ref[k, e]
            s = jnp.where(s >= 0, s, slots)
            length_ref[s] = stop_ref[k, e] - start_ref[k, e]
            table_ref[stamp_row, s] = e * height + start_ref[k, e]
        table_ref[batch_row, e] = batch_ref[e]
        factor_ref[0, e] = weight_ref[e]
        return 0

    lax.fori_loop(0, exposures, measure, 0, unroll=8)

    def lay(o, _):
        at = sent = o * rows_each
        for c in range(capacity):
            s = o * capacity + c
            table_ref[return_row, s] = at
            at = at + length_ref[s]
            p = jnp.maximum(plane_ref[o, c], 0)
            table_ref[first_row, s] = p * tile_rows + row_ref[o, c]
            factor_ref[1, s] = scale_ref[p]
            cover = cover_ref[o, c]
            table_ref[cover_row, s] = cover
            table_ref[sent_row, s] = sent
            sent = sent + cover
        return 0

    lax.fori_loop(0, peers, lay, 0)

    def point(e, _):
        for k in range(pieces):
            s = slot_ref[k, e]
            live = s >= 0
            begin = table_ref[return_row, jnp.maximum(s, 0)]
            start = start_ref[k, e]
            table_ref[2 * k, e] = jnp.where(live, height + begin - start, 0)
            table_ref[2 * k + 1, e] = jnp.where(live, start, height)
        return 0

    lax.fori_loop(0, exposures, point, 0, unroll=8)


def blur_kernel(
    height,
    pieces,
    batches_each,
    last,
    table_ref,
    factor_ref,
    arrived_ref,
    bank_in_ref,
    seen_ref,
    *rest,
):
    if last:
        out_ref, residual_out_ref, *rest = rest
        *rest, residual_ref, sent = rest
        send = pltpu.make_async_copy(residual_ref, residual_out_ref, sent)
    else:
        out_ref, *rest = rest
    rows_ref, bank_ref, result_ref, packed_ref, held_ref, blur_ref, back_ref = rest
    batch_row, stamp_row, return_row = table_rows(pieces)[:3]
    peers, rows_each, _ = out_ref.shape
    extra = bank_in_ref.shape[1] - rows_each
    exposures = seen_ref.shape[0]
    slots = peers * (2 * rows_each // height)
    abreast = max(n for n in (1, 2, 4, 8, 16, 32) if exposures % n == 0)
    place = lax.broadcasted_iota(I32, (height, LANES), 0)
    lane = lax.broadcasted_iota(I32, (height, LANES), 1)
    for o in range(peers):
        rows_ref[height + o * rows_each : height + (o + 1) * rows_each, :] = arrived_ref[o, :rows_each, :].astype(F32)
        bank_ref[o * extra : (o + 1) * extra, :] = bank_in_ref[o, rows_each:, :].astype(F32)

    gap = lane % height - place
    near = (gap <= HALF) & (gap >= -HALF) & (lane < TAPS * height)

    def operators(o, _):
        for n in range(batches_each):
            for m, ref in enumerate((blur_ref, back_ref)):
                taps = jnp.broadcast_to(bank_ref[pl.ds(o * extra + 2 * n + m, 1), :], (height, LANES))
                ref[o * batches_each + n] = jnp.where(
                    near, pltpu.roll(taps, 0, 1, stride=1, stride_axis=0), 0.0
                ).astype(BF16)
        return 0

    lax.fori_loop(0, peers, operators, 0, unroll=4)

    def shifted(x):
        parts = []
        for v in range(-HALF, HALF + 1):
            moved = x if v == 0 else pltpu.roll(x, v % LANES, 1)
            parts.append(jnp.where((lane >= v) & (lane < LANES + v), moved, jnp.zeros((), BF16)))
        parts.append(jnp.zeros((LANES - TAPS * height, LANES), BF16))
        return jnp.concatenate(parts, axis=0)

    def correlate(s):
        for q in range(abreast):
            e = s * abreast + q
            here = pl.ds(e * height, height)
            result_ref[here, :] = jnp.dot(
                back_ref[table_ref[batch_row, e]], shifted(held_ref[here, :]), preferred_element_type=F32
            )

    def blur(s):
        for q in range(abreast):
            e = s * abreast + q
            stamp = rows_ref[pl.ds(table_ref[0, e], height), :]
            for k in range(1, pieces):
                piece = rows_ref[pl.ds(table_ref[2 * k, e], height), :]
                stamp = jnp.where(place >= table_ref[2 * k + 1, e], piece, stamp)
            predicted = jnp.dot(
                blur_ref[table_ref[batch_row, e]], shifted(stamp.astype(BF16)), preferred_element_type=F32
            )
            residual = factor_ref[0, e] * (predicted - seen_ref[e].astype(F32))
            if last:
                residual_ref[e] = residual
            held_ref[pl.ds(e * height, height), :] = residual.astype(BF16)

    steps = exposures // abreast

    for s in range(steps + 1):
        if s > 0:
            correlate(s - 1)
        if s < steps:
            blur(s)
    if last:
        send.start()

    def move(s, _):
        packed_ref[pl.ds(table_ref[return_row, s], height), :] = result_ref[pl.ds(table_ref[stamp_row, s], height), :]
        return 0

    lax.fori_loop(0, slots, move, 0, unroll=16)
    for o in range(peers):
        out_ref[o, :, :] = packed_ref[o * rows_each : (o + 1) * rows_each, :].astype(BF16)
    if last:
        send.wait()


def body(
    model,
    exposures,
    inv_var,
    step_size,
    psf_taps,
    exp_batch,
    send_plane,
    send_row,
    send_cover,
    use_slot,
    use_start,
    use_stop,
    foot_lo,
    foot_hi,
):
    tile_count, bands, tile_rows, columns = model.shape
    count, height, _ = exposures.shape
    peers, capacity = send_plane.shape
    pieces = use_slot.shape[1]
    total = tile_count * bands * tile_rows
    rows_each = capacity * height // 2
    batches_each = psf_taps.shape[0]
    extra = aligned(batches_each * 2)
    block = rows_each + extra
    assert columns == LANES and rows_each % extra == 0 and TAPS * height <= LANES - HALF
    x = model.reshape(total, columns)

    def swap(a):
        return lax.all_to_all(a, "sky", split_axis=0, concat_axis=0, tiled=True)

    outbound = pl.pallas_call(
        functools.partial(first_send_kernel, tile_rows, height, rows_each),
        out_shape=jax.ShapeDtypeStruct((peers, block, columns), BF16),
        in_specs=[hbm()] * 5,
        out_specs=vmem(),
        scratch_shapes=[
            pltpu.SMEM(send_plane.shape, I32),
            pltpu.SMEM(send_row.shape, I32),
            pltpu.SMEM(send_cover.shape, I32),
            pltpu.VMEM(psf_taps.shape, F32),
            pltpu.VMEM((total + height, columns), F32),
            pltpu.VMEM((peers * rows_each + height, columns), F32),
            pltpu.VMEM((extra, columns), F32),
            pltpu.SemaphoreType.DMA((5,)),
        ],
        compiler_params=params(2.5),
        name="first_send",
    )(send_plane, send_row, send_cover, psf_taps, x)
    arrived = swap(outbound)
    slots = peers * capacity
    wide = max(count, slots + 1)
    table, factors = pl.pallas_call(
        functools.partial(tables_kernel, tile_rows, bands, height, rows_each),
        out_shape=(
            jax.ShapeDtypeStruct((table_rows(pieces).stop, wide), I32),
            jax.ShapeDtypeStruct((2, wide), F32),
        ),
        in_specs=[smem()] * 11,
        out_specs=(smem(), smem()),
        scratch_shapes=[pltpu.SMEM((slots + 1,), I32), pltpu.SMEM((tile_count * bands,), F32)],
        compiler_params=params(),
        cost_estimate=pl.CostEstimate(flops=4_000_000, bytes_accessed=8_000_000, transcendentals=0),
        name="tables",
    )(
        use_slot.T,
        use_start.T,
        use_stop.T,
        exp_batch,
        inv_var,
        send_plane,
        send_row,
        send_cover,
        step_size,
        foot_lo,
        foot_hi,
    )
    with_bank = arrived
    for sweep in range(ITERS):
        last = sweep == ITERS - 1
        rows_shape = jax.ShapeDtypeStruct((peers, rows_each, columns), BF16)
        outs = pl.pallas_call(
            functools.partial(blur_kernel, height, pieces, batches_each, last),
            out_shape=(rows_shape, jax.ShapeDtypeStruct(exposures.shape, F32)) if last else rows_shape,
            in_specs=[smem()] * 2 + [vmem()] * 3,
            out_specs=(vmem(), hbm()) if last else vmem(),
            scratch_shapes=[
                pltpu.VMEM((peers * rows_each + 2 * height, columns), F32),
                pltpu.VMEM((peers * extra, columns), F32),
                pltpu.VMEM((count * height + height, columns), F32),
                pltpu.VMEM((peers * rows_each + height, columns), F32),
                pltpu.VMEM((count * height, columns), BF16),
                pltpu.VMEM((peers * batches_each, height, LANES), BF16),
                pltpu.VMEM((peers * batches_each, height, LANES), BF16),
            ]
            + [pltpu.VMEM(exposures.shape, F32), pltpu.SemaphoreType.DMA] * last,
            compiler_params=params(),
            name="blur",
        )(table, factors, arrived, with_bank, exposures)
        outgoing = outs[0] if last else outs
        returned = swap(outgoing)
        new_shape = jax.ShapeDtypeStruct((total, columns), F32)
        padded = (total + height, columns)
        scratch = [pltpu.VMEM((peers * rows_each + height, columns), F32)]
        if last:
            scratch += [pltpu.VMEM(padded, F32), pltpu.SemaphoreType.DMA((tile_count * bands,))]
        else:
            scratch.append(pltpu.VMEM((peers * rows_each + height, columns), F32))
        sums = max(n for n in (1, 2, 4) if peers % n == 0)
        res = pl.pallas_call(
            functools.partial(update_kernel, pieces, bands, tile_rows, height, last),
            out_shape=jax.ShapeDtypeStruct((total, columns), F32)
            if last
            else (jax.ShapeDtypeStruct(padded, F32), rows_shape),
            in_specs=[smem()] * 2 + [vmem(), vmem()],
            out_specs=hbm() if last else (vmem(), vmem()),
            scratch_shapes=scratch + [pltpu.VMEM(padded, F32)] * (sums - 1),
            compiler_params=params(),
            name="update",
        )(table, factors, returned, x)
        if last:
            x = res
        else:
            x, outbound = res
            arrived = swap(outbound)
    return (x.reshape(model.shape), outs[1])


def solution(mesh):
    both = ("groups", "sky")
    return jax.shard_map(
        body,
        mesh=mesh,
        in_specs=(
            P(both, None, None, None),
            P(both, None, None),
            P(both),
            P(),
            P(both, None),
            P(both),
            P(both, None),
            P(both, None),
            P(both, None),
            P(both, None),
            P(both, None),
            P(both, None),
            P(both),
            P(both),
        ),
        out_specs=(P(both, None, None, None), P(both, None, None)),
        check_vma=False,
    )
```

```python
import functools

import jax
import jax.numpy as jnp
from jax import lax
from jax.experimental import pallas as pl
from jax.experimental.pallas import tpu as pltpu
from jax.sharding import PartitionSpec as P

NPSF = 4
TAPS = 7
ITERS = 2
LANES = 128
HALF = TAPS // 2
F32 = jnp.float32
BF16 = jnp.bfloat16
I32 = jnp.int32
VMEM_BYTES = 24 * 1024 * 1024

smem = lambda: pl.BlockSpec(memory_space=pltpu.SMEM)
vmem = lambda: pl.BlockSpec(memory_space=pltpu.VMEM)
hbm = lambda: pl.BlockSpec(memory_space=pltpu.HBM)


def params(share=1.0):
    return pltpu.CompilerParams(vmem_limit_bytes=int(share * VMEM_BYTES))


SHIFT = 16
PLACE = 13


def low(word):
    return word & ((1 << SHIFT) - 1)


def high(word):
    return lax.shift_right_logical(word, SHIFT)


def aligned(rows):
    return -(-rows // 16) * 16


def first_and_sent(word):
    mask = (1 << PLACE) - 1
    return word & mask, lax.shift_right_logical(word, PLACE) & mask


def pack_slots(plane_ref, row_ref, cover_ref, tile_rows, height, rows_each, x_ref, packed_ref):
    peers, capacity = plane_ref.shape

    def peer(d, _):
        at = d * rows_each
        for c in range(capacity):
            first = jnp.maximum(plane_ref[d, c], 0) * tile_rows + row_ref[d, c]
            packed_ref[pl.ds(at, height), :] = x_ref[pl.ds(first, height), :]
            at = at + cover_ref[d, c]
        return 0

    lax.fori_loop(0, peers, peer, 0, unroll=2)


def bank_rows(taps, height):
    count, width = taps.shape

    def grid(columns):
        return (
            lax.broadcasted_iota(I32, (width, columns), 0),
            lax.broadcasted_iota(I32, (width, columns), 1),
        )

    def select(x, mask):
        parts = []
        for _ in range(3):
            parts.append(x.astype(BF16).astype(F32))
            x = x - parts[-1]
        picked = jnp.dot(
            jnp.concatenate(parts, axis=0).astype(BF16), mask.astype(F32).astype(BF16), preferred_element_type=F32
        )
        return picked[:count] + picked[count : 2 * count] + picked[2 * count :]

    k, l = grid(width)
    unit = taps / select(taps, k // TAPS == l // TAPS)
    k, l = grid(2 * NPSF * LANES)
    mirror, j, l = l // (NPSF * LANES), l // LANES % NPSF, (l + HALF) % LANES
    i, t = l // height, l % height
    valid = (i < TAPS) & (t < TAPS)
    row_tap = j * TAPS + jnp.where(mirror == 1, t, TAPS - 1 - t)
    col_tap = (NPSF + j) * TAPS + jnp.where(mirror == 1, TAPS - 1 - i, i)
    row_part = select(unit, valid & (k == row_tap))
    col_part = select(unit, valid & (k == col_tap))
    product = row_part * col_part * (1.0 / NPSF)
    return [
        sum(product[:, (m * NPSF + j) * LANES : (m * NPSF + j + 1) * LANES] for j in range(NPSF)) for m in range(2)
    ]


def first_send_kernel(
    tile_rows,
    height,
    rows_each,
    plane_in_ref,
    row_in_ref,
    cover_in_ref,
    taps_in_ref,
    model_ref,
    out_ref,
    plane_ref,
    row_ref,
    cover_ref,
    taps_ref,
    x_ref,
    packed_ref,
    bank_ref,
    sems,
):
    peers = plane_ref.shape[0]
    pairs = (
        (taps_in_ref, taps_ref),
        (model_ref, x_ref.at[pl.ds(0, model_ref.shape[0]), :]),
        (plane_in_ref, plane_ref),
        (row_in_ref, row_ref),
        (cover_in_ref, cover_ref),
    )
    loads = [pltpu.make_async_copy(*pair, sems.at[n]) for n, pair in enumerate(pairs)]
    for load in loads:
        load.start()
    bank_ref[...] = jnp.zeros(bank_ref.shape, F32)
    loads[0].wait()
    for m, row in enumerate(bank_rows(taps_ref[...], height)):
        for n in range(taps_ref.shape[0]):
            bank_ref[2 * n + m : 2 * n + m + 1, :] = row[n : n + 1, :]
    bank = bank_ref[...].astype(BF16)
    for load in loads[1:]:
        load.wait()
    pack_slots(plane_ref, row_ref, cover_ref, tile_rows, height, rows_each, x_ref, packed_ref)
    for d in range(peers):
        out_ref[d, :rows_each, :] = packed_ref[d * rows_each : (d + 1) * rows_each, :].astype(BF16)
        out_ref[d, rows_each:, :] = bank


def update_kernel(bands, tile_rows, height, last, table_ref, factor_ref, returned_ref, model_ref, *rest):
    if last:
        new_ref, back_ref, x_ref, saved, *more_refs = rest
    else:
        x_ref, out_ref, back_ref, packed_ref, *more_refs = rest
    peers, rows_each, _ = returned_ref.shape
    capacity = 2 * rows_each // height
    slots = peers * capacity
    total = x_ref.shape[0] - height
    planes = total // tile_rows
    tiles = planes // bands
    x_ref[:total, :] = model_ref[:total, :]
    for ref in more_refs:
        ref[...] = jnp.zeros(ref.shape, F32)
    for d in range(peers):
        back_ref[d * rows_each : (d + 1) * rows_each, :] = returned_ref[d].astype(F32)
    place = lax.broadcasted_iota(I32, (height, LANES), 0)

    sums = [x_ref, *more_refs]

    def some_peers(step, _):
        for c in range(capacity):
            for n, ref in enumerate(sums):
                slot = (step * len(sums) + n) * capacity + c
                word = table_ref[slot]
                first, sent = first_and_sent(word)
                here = pl.ds(first, height)
                cover = lax.shift_right_logical(word, 2 * PLACE)
                piece = jnp.where(place < cover, back_ref[pl.ds(sent, height), :], 0.0)
                ref[here, :] = ref[here, :] - factor_ref[slot] * piece
        return 0

    lax.fori_loop(0, peers // len(sums), some_peers, 0)

    pos = lax.broadcasted_iota(I32, (tile_rows, LANES), 0)
    saves = []
    for p in range(planes):
        inside = (pos >= table_ref[slots + p // bands]) & (pos < table_ref[slots + tiles + p // bands])
        here = slice(p * tile_rows, (p + 1) * tile_rows)
        new = sum((ref[here, :] for ref in more_refs), x_ref[here, :])
        x_ref[here, :] = jnp.where(inside, jnp.maximum(new, 0.0), 0.0)
        if last:
            rows = pl.ds(p * tile_rows, tile_rows)
            saves.append(pltpu.make_async_copy(x_ref.at[rows, :], new_ref.at[rows, :], saved.at[p]))
            saves[-1].start()
    if not last:

        def pack(slot, _):
            first, sent = first_and_sent(table_ref[slot])
            packed_ref[pl.ds(sent, height), :] = x_ref[pl.ds(first, height), :]
            return 0

        lax.fori_loop(0, slots, pack, 0, unroll=16)
        for d in range(peers):
            out_ref[d, :, :] = packed_ref[d * rows_each : (d + 1) * rows_each, :].astype(BF16)
    for save in saves:
        save.wait()


def tables_kernel(
    tile_rows,
    bands,
    height,
    rows_each,
    slot_ref,
    start_ref,
    stop_ref,
    batch_ref,
    plane_ref,
    row_ref,
    cover_ref,
    step_ref,
    lo_ref,
    hi_ref,
    blur_ref,
    update_ref,
    factor_ref,
    length_ref,
    stamp_ref,
    begin_ref,
    scale_ref,
):
    pieces, exposures = slot_ref.shape
    peers, capacity = plane_ref.shape
    slots = peers * capacity

    def clear(s, _):
        length_ref[s] = 0
        stamp_ref[s] = 0
        return 0

    lax.fori_loop(0, slots, clear, 0, unroll=16)
    for p in range(scale_ref.shape[0]):
        scale_ref[p] = step_ref[p % bands]
    tiles = lo_ref.shape[0]
    for t in range(tiles):
        update_ref[slots + t] = lo_ref[t]
        update_ref[slots + tiles + t] = hi_ref[t]

    def measure(e, _):
        for k in range(pieces):
            s = slot_ref[k, e]
            s = jnp.where(s >= 0, s, slots)
            length_ref[s] = stop_ref[k, e] - start_ref[k, e]
            stamp_ref[s] = e * height + start_ref[k, e]
        return 0

    lax.fori_loop(0, exposures, measure, 0, unroll=8)

    def lay(o, _):
        at = sent = o * rows_each
        for c in range(capacity):
            s = o * capacity + c
            begin_ref[s] = at
            blur_ref[pieces * exposures + s] = stamp_ref[s] | (at << SHIFT)
            at = at + length_ref[s]
            p = jnp.maximum(plane_ref[o, c], 0)
            cover = cover_ref[o, c]
            update_ref[s] = (p * tile_rows + row_ref[o, c]) | (sent << PLACE) | (cover << 2 * PLACE)
            factor_ref[s] = scale_ref[p]
            sent = sent + cover
        return 0

    lax.fori_loop(0, peers, lay, 0)

    def point(e, _):
        for k in range(pieces):
            s = slot_ref[k, e]
            live = s >= 0
            start = start_ref[k, e]
            begin = jnp.where(live, height + begin_ref[jnp.maximum(s, 0)] - start, 0)
            above = batch_ref[e] if k == 0 else jnp.where(live, start, height)
            blur_ref[k * exposures + e] = begin | (above << SHIFT)
        return 0

    lax.fori_loop(0, exposures, point, 0, unroll=8)


def blur_kernel(
    height,
    pieces,
    batches_each,
    last,
    table_ref,
    weight_ref,
    arrived_ref,
    bank_in_ref,
    seen_ref,
    *rest,
):
    if last:
        out_ref, residual_out_ref, *rest = rest
        *rest, residual_ref, sent = rest
        send = pltpu.make_async_copy(residual_ref, residual_out_ref, sent)
    else:
        out_ref, *rest = rest
    rows_ref, bank_ref, result_ref, packed_ref, held_ref, blur_ref, back_ref = rest
    peers, rows_each, _ = out_ref.shape
    extra = bank_in_ref.shape[1] - rows_each
    exposures = seen_ref.shape[0]
    slots = peers * (2 * rows_each // height)
    abreast = max(n for n in (1, 2, 4, 8, 16, 32) if exposures % n == 0)
    place = lax.broadcasted_iota(I32, (height, LANES), 0)
    lane = lax.broadcasted_iota(I32, (height, LANES), 1)
    for o in range(peers):
        rows_ref[height + o * rows_each : height + (o + 1) * rows_each, :] = arrived_ref[o, :rows_each, :].astype(F32)
        bank_ref[o * extra : (o + 1) * extra, :] = bank_in_ref[o, rows_each:, :].astype(F32)

    gap = lane % height - place
    near = (gap <= HALF) & (gap >= -HALF) & (lane < TAPS * height)

    def operators(o, _):
        for n in range(batches_each):
            for m, ref in enumerate((blur_ref, back_ref)):
                taps = jnp.broadcast_to(bank_ref[pl.ds(o * extra + 2 * n + m, 1), :], (height, LANES))
                ref[o * batches_each + n] = jnp.where(
                    near, pltpu.roll(taps, 0, 1, stride=1, stride_axis=0), 0.0
                ).astype(BF16)
        return 0

    lax.fori_loop(0, peers, operators, 0, unroll=4)

    def shifted(x):
        parts = []
        for v in range(-HALF, HALF + 1):
            moved = x if v == 0 else pltpu.roll(x, v % LANES, 1)
            parts.append(jnp.where((lane >= v) & (lane < LANES + v), moved, jnp.zeros((), BF16)))
        parts.append(jnp.zeros((LANES - TAPS * height, LANES), BF16))
        return jnp.concatenate(parts, axis=0)

    def correlate(s):
        for q in range(abreast):
            e = s * abreast + q
            here = pl.ds(e * height, height)
            result_ref[here, :] = jnp.dot(
                back_ref[high(table_ref[e])], shifted(held_ref[here, :]), preferred_element_type=F32
            )

    def blur(s):
        for q in range(abreast):
            e = s * abreast + q
            stamp = rows_ref[pl.ds(low(table_ref[e]), height), :]
            for k in range(1, pieces):
                word = table_ref[k * exposures + e]
                stamp = jnp.where(place >= high(word), rows_ref[pl.ds(low(word), height), :], stamp)
            predicted = jnp.dot(
                blur_ref[high(table_ref[e])], shifted(stamp.astype(BF16)), preferred_element_type=F32
            )
            residual = weight_ref[e] * (predicted - seen_ref[e].astype(F32))
            if last:
                residual_ref[e] = residual
            held_ref[pl.ds(e * height, height), :] = residual.astype(BF16)

    steps = exposures // abreast

    for s in range(steps + 1):
        if s > 0:
            correlate(s - 1)
        if s < steps:
            blur(s)
    if last:
        send.start()

    def move(s, _):
        word = table_ref[pieces * exposures + s]
        packed_ref[pl.ds(high(word), height), :] = result_ref[pl.ds(low(word), height), :]
        return 0

    lax.fori_loop(0, slots, move, 0, unroll=16)
    for o in range(peers):
        out_ref[o, :, :] = packed_ref[o * rows_each : (o + 1) * rows_each, :].astype(BF16)
    if last:
        send.wait()


def body(
    model,
    exposures,
    inv_var,
    step_size,
    psf_taps,
    exp_batch,
    send_plane,
    send_row,
    send_cover,
    use_slot,
    use_start,
    use_stop,
    foot_lo,
    foot_hi,
):
    tile_count, bands, tile_rows, columns = model.shape
    count, height, _ = exposures.shape
    peers, capacity = send_plane.shape
    pieces = use_slot.shape[1]
    total = tile_count * bands * tile_rows
    rows_each = capacity * height // 2
    batches_each = psf_taps.shape[0]
    extra = aligned(batches_each * 2)
    block = rows_each + extra
    assert columns == LANES and rows_each % extra == 0 and TAPS * height <= LANES - HALF
    x = model.reshape(total, columns)

    def swap(a):
        return lax.all_to_all(a, "sky", split_axis=0, concat_axis=0, tiled=True)

    outbound = pl.pallas_call(
        functools.partial(first_send_kernel, tile_rows, height, rows_each),
        out_shape=jax.ShapeDtypeStruct((peers, block, columns), BF16),
        in_specs=[hbm()] * 5,
        out_specs=vmem(),
        scratch_shapes=[
            pltpu.SMEM(send_plane.shape, I32),
            pltpu.SMEM(send_row.shape, I32),
            pltpu.SMEM(send_cover.shape, I32),
            pltpu.VMEM(psf_taps.shape, F32),
            pltpu.VMEM((total + height, columns), F32),
            pltpu.VMEM((peers * rows_each + height, columns), F32),
            pltpu.VMEM((extra, columns), F32),
            pltpu.SemaphoreType.DMA((5,)),
        ],
        compiler_params=params(2.5),
        name="first_send",
    )(send_plane, send_row, send_cover, psf_taps, x)
    arrived = swap(outbound)
    slots = peers * capacity
    assert max(total, peers * rows_each) < 1 << PLACE and height < 1 << (31 - 2 * PLACE)
    assert max(count, peers * capacity + 2) * height < 1 << (SHIFT - 1)
    blur_table, update_table, factors = pl.pallas_call(
        functools.partial(tables_kernel, tile_rows, bands, height, rows_each),
        out_shape=(
            jax.ShapeDtypeStruct((pieces * count + slots,), I32),
            jax.ShapeDtypeStruct((slots + 2 * tile_count,), I32),
            jax.ShapeDtypeStruct((slots,), F32),
        ),
        in_specs=[smem()] * 10,
        out_specs=(smem(), smem(), smem()),
        scratch_shapes=[
            pltpu.SMEM((slots + 1,), I32),
            pltpu.SMEM((slots + 1,), I32),
            pltpu.SMEM((slots,), I32),
            pltpu.SMEM((tile_count * bands,), F32),
        ],
        compiler_params=params(),
        cost_estimate=pl.CostEstimate(flops=4_000_000, bytes_accessed=8_000_000, transcendentals=0),
        name="tables",
    )(
        use_slot.T,
        use_start.T,
        use_stop.T,
        exp_batch,
        send_plane,
        send_row,
        send_cover,
        step_size,
        foot_lo,
        foot_hi,
    )
    with_bank = arrived
    for sweep in range(ITERS):
        last = sweep == ITERS - 1
        rows_shape = jax.ShapeDtypeStruct((peers, rows_each, columns), BF16)
        outs = pl.pallas_call(
            functools.partial(blur_kernel, height, pieces, batches_each, last),
            out_shape=(rows_shape, jax.ShapeDtypeStruct(exposures.shape, F32)) if last else rows_shape,
            in_specs=[smem()] * 2 + [vmem()] * 3,
            out_specs=(vmem(), hbm()) if last else vmem(),
            scratch_shapes=[
                pltpu.VMEM((peers * rows_each + 2 * height, columns), F32),
                pltpu.VMEM((peers * extra, columns), F32),
                pltpu.VMEM((count * height + height, columns), F32),
                pltpu.VMEM((peers * rows_each + height, columns), F32),
                pltpu.VMEM((count * height, columns), BF16),
                pltpu.VMEM((peers * batches_each, height, LANES), BF16),
                pltpu.VMEM((peers * batches_each, height, LANES), BF16),
            ]
            + [pltpu.VMEM(exposures.shape, F32), pltpu.SemaphoreType.DMA] * last,
            compiler_params=params(),
            name="blur",
        )(blur_table, inv_var, arrived, with_bank, exposures)
        outgoing = outs[0] if last else outs
        returned = swap(outgoing)
        new_shape = jax.ShapeDtypeStruct((total, columns), F32)
        padded = (total + height, columns)
        scratch = [pltpu.VMEM((peers * rows_each + height, columns), F32)]
        if last:
            scratch += [pltpu.VMEM(padded, F32), pltpu.SemaphoreType.DMA((tile_count * bands,))]
        else:
            scratch.append(pltpu.VMEM((peers * rows_each + height, columns), F32))
        sums = max(n for n in (1, 2, 4 if last else 2) if peers % n == 0)
        res = pl.pallas_call(
            functools.partial(update_kernel, bands, tile_rows, height, last),
            out_shape=jax.ShapeDtypeStruct((total, columns), F32)
            if last
            else (jax.ShapeDtypeStruct(padded, F32), rows_shape),
            in_specs=[smem()] * 2 + [vmem(), vmem()],
            out_specs=hbm() if last else (vmem(), vmem()),
            scratch_shapes=scratch + [pltpu.VMEM(padded, F32)] * (sums - 1),
            compiler_params=params(),
            name="update",
        )(update_table, factors, returned, x)
        if last:
            x = res
        else:
            x, outbound = res
            arrived = swap(outbound)
    return (x.reshape(model.shape), outs[1])


def solution(mesh):
    both = ("groups", "sky")
    return jax.shard_map(
        body,
        mesh=mesh,
        in_specs=(
            P(both, None, None, None),
            P(both, None, None),
            P(both),
            P(),
            P(both, None),
            P(both),
            P(both, None),
            P(both, None),
            P(both, None),
            P(both, None),
            P(both, None),
            P(both, None),
            P(both),
            P(both),
        ),
        out_specs=(P(both, None, None, None), P(both, None, None)),
        check_vma=False,
    )
```

```python
import functools

import jax
import jax.numpy as jnp
from jax import lax
from jax.experimental import pallas as pl
from jax.experimental.pallas import tpu as pltpu
from jax.sharding import PartitionSpec as P

NPSF = 4
TAPS = 7
ITERS = 2
LANES = 128
HALF = TAPS // 2
F32 = jnp.float32
BF16 = jnp.bfloat16
I32 = jnp.int32
VMEM_BYTES = 24 * 1024 * 1024

smem = lambda: pl.BlockSpec(memory_space=pltpu.SMEM)
vmem = lambda: pl.BlockSpec(memory_space=pltpu.VMEM)
hbm = lambda: pl.BlockSpec(memory_space=pltpu.HBM)


def params(share=1.0):
    return pltpu.CompilerParams(vmem_limit_bytes=int(share * VMEM_BYTES))


SHIFT = 16
PLACE = 13


def low(word):
    return word & ((1 << SHIFT) - 1)


def high(word):
    return lax.shift_right_logical(word, SHIFT)


def aligned(rows):
    return -(-rows // 16) * 16


def first_and_sent(word):
    mask = (1 << PLACE) - 1
    return word & mask, lax.shift_right_logical(word, PLACE) & mask


def pack_slots(begin, count, plane_ref, row_ref, cover_ref, tile_rows, height, rows_each, x_ref, packed_ref):
    capacity = plane_ref.shape[1]

    def peer(d, _):
        at = d * rows_each
        for c in range(capacity):
            first = jnp.maximum(plane_ref[d, c], 0) * tile_rows + row_ref[d, c]
            packed_ref[pl.ds(at, height), :] = x_ref[pl.ds(first, height), :]
            at = at + cover_ref[d, c]
        return 0

    lax.fori_loop(begin, begin + count, peer, 0, unroll=2)


def bank_rows(taps, height):
    count, width = taps.shape

    def grid(columns):
        return (
            lax.broadcasted_iota(I32, (width, columns), 0),
            lax.broadcasted_iota(I32, (width, columns), 1),
        )

    def select(x, mask):
        parts = []
        for _ in range(3):
            parts.append(x.astype(BF16).astype(F32))
            x = x - parts[-1]
        picked = jnp.dot(
            jnp.concatenate(parts, axis=0).astype(BF16), mask.astype(F32).astype(BF16), preferred_element_type=F32
        )
        return picked[:count] + picked[count : 2 * count] + picked[2 * count :]

    k, l = grid(width)
    unit = taps / select(taps, k // TAPS == l // TAPS)
    k, l = grid(2 * NPSF * LANES)
    mirror, j, l = l // (NPSF * LANES), l // LANES % NPSF, (l + HALF) % LANES
    i, t = l // height, l % height
    valid = (i < TAPS) & (t < TAPS)
    row_tap = j * TAPS + jnp.where(mirror == 1, t, TAPS - 1 - t)
    col_tap = (NPSF + j) * TAPS + jnp.where(mirror == 1, TAPS - 1 - i, i)
    row_part = select(unit, valid & (k == row_tap))
    col_part = select(unit, valid & (k == col_tap))
    product = row_part * col_part * (1.0 / NPSF)
    return [
        sum(product[:, (m * NPSF + j) * LANES : (m * NPSF + j + 1) * LANES] for j in range(NPSF)) for m in range(2)
    ]


def first_send_kernel(
    tile_rows,
    height,
    rows_each,
    plane_in_ref,
    row_in_ref,
    cover_in_ref,
    taps_in_ref,
    model_ref,
    out_ref,
    plane_ref,
    row_ref,
    cover_ref,
    taps_ref,
    x_ref,
    packed_ref,
    bank_ref,
    block_ref,
    sems,
):
    peers = plane_ref.shape[0]
    pairs = (
        (taps_in_ref, taps_ref),
        (model_ref, x_ref.at[pl.ds(0, model_ref.shape[0]), :]),
        (plane_in_ref, plane_ref),
        (row_in_ref, row_ref),
        (cover_in_ref, cover_ref),
    )
    loads = [pltpu.make_async_copy(*pair, sems.at[n]) for n, pair in enumerate(pairs)]
    for load in loads:
        load.start()
    bank_ref[...] = jnp.zeros(bank_ref.shape, F32)
    loads[0].wait()
    for m, row in enumerate(bank_rows(taps_ref[...], height)):
        for n in range(taps_ref.shape[0]):
            bank_ref[2 * n + m : 2 * n + m + 1, :] = row[n : n + 1, :]
    bank = bank_ref[...].astype(BF16)
    for load in loads[1:]:
        load.wait()
    parts = max(n for n in (1, 2, 4) if peers % n == 0)
    some = peers // parts
    sends = []
    for part in range(parts):
        here = pl.ds(part * some, some)
        pack_slots(part * some, some, plane_ref, row_ref, cover_ref, tile_rows, height, rows_each, x_ref, packed_ref)
        for d in range(part * some, (part + 1) * some):
            block_ref[d, :rows_each, :] = packed_ref[d * rows_each : (d + 1) * rows_each, :].astype(BF16)
            block_ref[d, rows_each:, :] = bank
        sends.append(pltpu.make_async_copy(block_ref.at[here], out_ref.at[here], sems.at[len(loads) + part]))
        sends[-1].start()
    for send in sends:
        send.wait()


def update_kernel(bands, tile_rows, height, last, table_ref, factor_ref, returned_ref, model_ref, *rest):
    if last:
        new_ref, back_ref, x_ref, saved, *more_refs = rest
    else:
        x_ref, out_ref, back_ref, packed_ref, *more_refs = rest
    peers, rows_each, _ = returned_ref.shape
    capacity = 2 * rows_each // height
    slots = peers * capacity
    total = x_ref.shape[0] - height
    planes = total // tile_rows
    tiles = planes // bands
    x_ref[:total, :] = model_ref[:total, :]
    for ref in more_refs:
        ref[...] = jnp.zeros(ref.shape, F32)
    for d in range(peers):
        back_ref[d * rows_each : (d + 1) * rows_each, :] = returned_ref[d].astype(F32)
    place = lax.broadcasted_iota(I32, (height, LANES), 0)

    sums = [x_ref, *more_refs]

    def some_peers(step, _):
        for c in range(capacity):
            for n, ref in enumerate(sums):
                slot = (step * len(sums) + n) * capacity + c
                word = table_ref[slot]
                first, sent = first_and_sent(word)
                here = pl.ds(first, height)
                cover = lax.shift_right_logical(word, 2 * PLACE)
                piece = jnp.where(place < cover, back_ref[pl.ds(sent, height), :], 0.0)
                ref[here, :] = ref[here, :] - factor_ref[slot] * piece
        return 0

    lax.fori_loop(0, peers // len(sums), some_peers, 0)

    pos = lax.broadcasted_iota(I32, (tile_rows, LANES), 0)
    saves = []
    for p in range(planes):
        inside = (pos >= table_ref[slots + p // bands]) & (pos < table_ref[slots + tiles + p // bands])
        here = slice(p * tile_rows, (p + 1) * tile_rows)
        new = sum((ref[here, :] for ref in more_refs), x_ref[here, :])
        x_ref[here, :] = jnp.where(inside, jnp.maximum(new, 0.0), 0.0)
        if last:
            rows = pl.ds(p * tile_rows, tile_rows)
            saves.append(pltpu.make_async_copy(x_ref.at[rows, :], new_ref.at[rows, :], saved.at[p]))
            saves[-1].start()
    if not last:

        def pack(slot, _):
            first, sent = first_and_sent(table_ref[slot])
            packed_ref[pl.ds(sent, height), :] = x_ref[pl.ds(first, height), :]
            return 0

        lax.fori_loop(0, slots, pack, 0, unroll=16)
        for d in range(peers):
            out_ref[d, :, :] = packed_ref[d * rows_each : (d + 1) * rows_each, :].astype(BF16)
    for save in saves:
        save.wait()


def tables_kernel(
    tile_rows,
    bands,
    height,
    rows_each,
    slot_ref,
    start_ref,
    stop_ref,
    batch_ref,
    plane_ref,
    row_ref,
    cover_ref,
    step_ref,
    lo_ref,
    hi_ref,
    blur_ref,
    update_ref,
    factor_ref,
    length_ref,
    begin_ref,
    scale_ref,
):
    pieces, exposures = slot_ref.shape
    peers, capacity = plane_ref.shape
    slots = peers * capacity

    def clear(s, _):
        length_ref[s] = 0
        return 0

    lax.fori_loop(0, slots, clear, 0, unroll=16)
    for p in range(scale_ref.shape[0]):
        scale_ref[p] = step_ref[p % bands]
    tiles = lo_ref.shape[0]
    for t in range(tiles):
        update_ref[slots + t] = lo_ref[t]
        update_ref[slots + tiles + t] = hi_ref[t]

    def measure(e, _):
        for k in range(pieces):
            s = slot_ref[k, e]
            s = jnp.where(s >= 0, s, slots)
            length_ref[s] = stop_ref[k, e] - start_ref[k, e]
        return 0

    lax.fori_loop(0, exposures, measure, 0, unroll=8)

    def lay(o, _):
        at = sent = o * rows_each
        for c in range(capacity):
            s = o * capacity + c
            begin_ref[s] = at
            at = at + length_ref[s]
            p = jnp.maximum(plane_ref[o, c], 0)
            cover = cover_ref[o, c]
            update_ref[s] = (p * tile_rows + row_ref[o, c]) | (sent << PLACE) | (cover << 2 * PLACE)
            factor_ref[s] = scale_ref[p]
            sent = sent + cover
        return 0

    lax.fori_loop(0, peers, lay, 0)

    def point(e, _):
        for k in range(pieces):
            s = slot_ref[k, e]
            live = s >= 0
            start = start_ref[k, e]
            begin = jnp.where(live, height + begin_ref[jnp.maximum(s, 0)] - start, 0)
            above = batch_ref[e] if k == 0 else jnp.where(live, start, height)
            blur_ref[k * exposures + e] = begin | (above << SHIFT)
        return 0

    lax.fori_loop(0, exposures, point, 0, unroll=8)


def blur_kernel(
    height,
    pieces,
    batches_each,
    last,
    table_ref,
    weight_ref,
    arrived_ref,
    bank_in_ref,
    seen_ref,
    *rest,
):
    if last:
        out_ref, residual_out_ref, *rest = rest
        *rest, residual_ref, sent = rest
        send = pltpu.make_async_copy(residual_ref, residual_out_ref, sent)
    else:
        out_ref, *rest = rest
    rows_ref, bank_ref, packed_ref, held_ref, blur_ref, back_ref = rest
    peers, rows_each, _ = out_ref.shape
    extra = bank_in_ref.shape[1] - rows_each
    exposures = seen_ref.shape[0]
    abreast = max(n for n in (1, 2, 4, 8, 16, 32) if exposures % n == 0)
    place = lax.broadcasted_iota(I32, (height, LANES), 0)
    lane = lax.broadcasted_iota(I32, (height, LANES), 1)
    for o in range(peers):
        rows_ref[height + o * rows_each : height + (o + 1) * rows_each, :] = arrived_ref[o, :rows_each, :].astype(F32)
        bank_ref[o * extra : (o + 1) * extra, :] = bank_in_ref[o, rows_each:, :].astype(F32)

    gap = lane % height - place
    near = (gap <= HALF) & (gap >= -HALF) & (lane < TAPS * height)

    def operators(o, _):
        for n in range(batches_each):
            for m, ref in enumerate((blur_ref, back_ref)):
                taps = jnp.broadcast_to(bank_ref[pl.ds(o * extra + 2 * n + m, 1), :], (height, LANES))
                ref[o * batches_each + n] = jnp.where(
                    near, pltpu.roll(taps, 0, 1, stride=1, stride_axis=0), 0.0
                ).astype(BF16)
        return 0

    lax.fori_loop(0, peers, operators, 0, unroll=4)

    def shifted(x):
        parts = []
        for v in range(-HALF, HALF + 1):
            moved = x if v == 0 else pltpu.roll(x, v % LANES, 1)
            parts.append(jnp.where((lane >= v) & (lane < LANES + v), moved, jnp.zeros((), BF16)))
        parts.append(jnp.zeros((LANES - TAPS * height, LANES), BF16))
        return jnp.concatenate(parts, axis=0)

    def correlate(s):
        for q in range(abreast):
            e = s * abreast + q
            result = jnp.dot(
                back_ref[high(table_ref[e])],
                shifted(held_ref[e * height : (e + 1) * height, :]),
                preferred_element_type=F32,
            )
            words = [table_ref[k * exposures + e] for k in range(pieces)]
            for k, word in enumerate(words):
                mask = place >= high(word) if k else None
                if k + 1 < pieces:
                    before = place < high(words[k + 1])
                    mask = before if mask is None else mask & before
                pltpu.store(packed_ref.at[pl.ds(low(word), height), :], result, mask=mask)

    def blur(s):
        for q in range(abreast):
            e = s * abreast + q
            stamp = rows_ref[pl.ds(low(table_ref[e]), height), :]
            for k in range(1, pieces):
                word = table_ref[k * exposures + e]
                stamp = jnp.where(place >= high(word), rows_ref[pl.ds(low(word), height), :], stamp)
            predicted = jnp.dot(
                blur_ref[high(table_ref[e])], shifted(stamp.astype(BF16)), preferred_element_type=F32
            )
            residual = weight_ref[e] * (predicted - seen_ref[e].astype(F32))
            if last:
                residual_ref[e] = residual
            held_ref[pl.ds(e * height, height), :] = residual.astype(BF16)

    steps = exposures // abreast

    for s in range(steps + 1):
        if s > 0:
            correlate(s - 1)
        if s < steps:
            blur(s)
    if last:
        send.start()

    for o in range(peers):
        at = height + o * rows_each
        out_ref[o, :, :] = packed_ref[at : at + rows_each, :].astype(BF16)
    if last:
        send.wait()


def body(
    model,
    exposures,
    inv_var,
    step_size,
    psf_taps,
    exp_batch,
    send_plane,
    send_row,
    send_cover,
    use_slot,
    use_start,
    use_stop,
    foot_lo,
    foot_hi,
):
    tile_count, bands, tile_rows, columns = model.shape
    count, height, _ = exposures.shape
    peers, capacity = send_plane.shape
    pieces = use_slot.shape[1]
    total = tile_count * bands * tile_rows
    rows_each = capacity * height // 2
    batches_each = psf_taps.shape[0]
    extra = aligned(batches_each * 2)
    block = rows_each + extra
    assert columns == LANES and rows_each % extra == 0 and TAPS * height <= LANES - HALF
    x = model.reshape(total, columns)

    def swap(a):
        return lax.all_to_all(a, "sky", split_axis=0, concat_axis=0, tiled=True)

    outbound = pl.pallas_call(
        functools.partial(first_send_kernel, tile_rows, height, rows_each),
        out_shape=jax.ShapeDtypeStruct((peers, block, columns), BF16),
        in_specs=[hbm()] * 5,
        out_specs=hbm(),
        scratch_shapes=[
            pltpu.SMEM(send_plane.shape, I32),
            pltpu.SMEM(send_row.shape, I32),
            pltpu.SMEM(send_cover.shape, I32),
            pltpu.VMEM(psf_taps.shape, F32),
            pltpu.VMEM((total + height, columns), F32),
            pltpu.VMEM((peers * rows_each + height, columns), F32),
            pltpu.VMEM((extra, columns), F32),
            pltpu.VMEM((peers, block, columns), BF16),
            pltpu.SemaphoreType.DMA((9,)),
        ],
        compiler_params=params(2.5),
        name="first_send",
    )(send_plane, send_row, send_cover, psf_taps, x)
    arrived = swap(outbound)
    slots = peers * capacity
    assert max(total, peers * rows_each) < 1 << PLACE and height < 1 << (31 - 2 * PLACE)
    assert max(peers * rows_each + 2 * height, psf_taps.shape[0] * peers) < 1 << (SHIFT - 1)
    blur_table, update_table, factors = pl.pallas_call(
        functools.partial(tables_kernel, tile_rows, bands, height, rows_each),
        out_shape=(
            jax.ShapeDtypeStruct((pieces * count,), I32),
            jax.ShapeDtypeStruct((slots + 2 * tile_count,), I32),
            jax.ShapeDtypeStruct((slots,), F32),
        ),
        in_specs=[smem()] * 10,
        out_specs=(smem(), smem(), smem()),
        scratch_shapes=[
            pltpu.SMEM((slots + 1,), I32),
            pltpu.SMEM((slots,), I32),
            pltpu.SMEM((tile_count * bands,), F32),
        ],
        compiler_params=params(),
        cost_estimate=pl.CostEstimate(flops=4_000_000, bytes_accessed=8_000_000, transcendentals=0),
        name="tables",
    )(
        use_slot.T,
        use_start.T,
        use_stop.T,
        exp_batch,
        send_plane,
        send_row,
        send_cover,
        step_size,
        foot_lo,
        foot_hi,
    )
    with_bank = arrived
    for sweep in range(ITERS):
        last = sweep == ITERS - 1
        rows_shape = jax.ShapeDtypeStruct((peers, rows_each, columns), BF16)
        outs = pl.pallas_call(
            functools.partial(blur_kernel, height, pieces, batches_each, last),
            out_shape=(rows_shape, jax.ShapeDtypeStruct(exposures.shape, F32)) if last else rows_shape,
            in_specs=[smem()] * 2 + [vmem()] * 3,
            out_specs=(vmem(), hbm()) if last else vmem(),
            scratch_shapes=[
                pltpu.VMEM((peers * rows_each + 2 * height, columns), F32),
                pltpu.VMEM((peers * extra, columns), F32),
                pltpu.VMEM((peers * rows_each + 2 * height, columns), F32),
                pltpu.VMEM((count * height, columns), BF16),
                pltpu.VMEM((peers * batches_each, height, LANES), BF16),
                pltpu.VMEM((peers * batches_each, height, LANES), BF16),
            ]
            + [pltpu.VMEM(exposures.shape, F32), pltpu.SemaphoreType.DMA] * last,
            compiler_params=params(),
            name="blur",
        )(blur_table, inv_var, arrived, with_bank, exposures)
        outgoing = outs[0] if last else outs
        returned = swap(outgoing)
        new_shape = jax.ShapeDtypeStruct((total, columns), F32)
        padded = (total + height, columns)
        scratch = [pltpu.VMEM((peers * rows_each + height, columns), F32)]
        if last:
            scratch += [pltpu.VMEM(padded, F32), pltpu.SemaphoreType.DMA((tile_count * bands,))]
        else:
            scratch.append(pltpu.VMEM((peers * rows_each + height, columns), F32))
        sums = max(n for n in (1, 2) if peers % n == 0)
        res = pl.pallas_call(
            functools.partial(update_kernel, bands, tile_rows, height, last),
            out_shape=jax.ShapeDtypeStruct((total, columns), F32)
            if last
            else (jax.ShapeDtypeStruct(padded, F32), rows_shape),
            in_specs=[smem()] * 2 + [vmem(), vmem()],
            out_specs=hbm() if last else (vmem(), vmem()),
            scratch_shapes=scratch + [pltpu.VMEM(padded, F32)] * (sums - 1),
            compiler_params=params(),
            name="update",
        )(update_table, factors, returned, x)
        if last:
            x = res
        else:
            x, outbound = res
            arrived = swap(outbound)
    return (x.reshape(model.shape), outs[1])


def solution(mesh):
    both = ("groups", "sky")
    return jax.shard_map(
        body,
        mesh=mesh,
        in_specs=(
            P(both, None, None, None),
            P(both, None, None),
            P(both),
            P(),
            P(both, None),
            P(both),
            P(both, None),
            P(both, None),
            P(both, None),
            P(both, None),
            P(both, None),
            P(both, None),
            P(both),
            P(both),
        ),
        out_specs=(P(both, None, None, None), P(both, None, None)),
        check_vma=False,
    )
```

```python
import functools

import jax
import jax.numpy as jnp
from jax import lax
from jax.experimental import pallas as pl
from jax.experimental.pallas import tpu as pltpu
from jax.sharding import PartitionSpec as P

NPSF = 4
TAPS = 7
ITERS = 2
LANES = 128
HALF = TAPS // 2
F32 = jnp.float32
BF16 = jnp.bfloat16
I32 = jnp.int32
VMEM_BYTES = 24 * 1024 * 1024

smem = lambda: pl.BlockSpec(memory_space=pltpu.SMEM)
vmem = lambda: pl.BlockSpec(memory_space=pltpu.VMEM)
hbm = lambda: pl.BlockSpec(memory_space=pltpu.HBM)


def params(share=1.0):
    return pltpu.CompilerParams(vmem_limit_bytes=int(share * VMEM_BYTES))


SHIFT = 16
PLACE = 13


def low(word):
    return word & ((1 << SHIFT) - 1)


def high(word):
    return lax.shift_right_logical(word, SHIFT)


def aligned(rows):
    return -(-rows // 16) * 16


def first_and_sent(word):
    mask = (1 << PLACE) - 1
    return word & mask, lax.shift_right_logical(word, PLACE) & mask


def pack_slots(begin, count, plane_ref, row_ref, cover_ref, tile_rows, height, rows_each, x_ref, packed_ref):
    capacity = plane_ref.shape[1]

    def peer(d, _):
        at = d * rows_each
        for c in range(capacity):
            first = jnp.maximum(plane_ref[d, c], 0) * tile_rows + row_ref[d, c]
            packed_ref[pl.ds(at, height), :] = x_ref[pl.ds(first, height), :]
            at = at + cover_ref[d, c]
        return 0

    lax.fori_loop(begin, begin + count, peer, 0, unroll=2)


def bank_rows(taps, height):
    count, width = taps.shape

    def grid(columns):
        return (
            lax.broadcasted_iota(I32, (width, columns), 0),
            lax.broadcasted_iota(I32, (width, columns), 1),
        )

    def select(x, mask):
        parts = []
        for _ in range(3):
            parts.append(x.astype(BF16).astype(F32))
            x = x - parts[-1]
        picked = jnp.dot(
            jnp.concatenate(parts, axis=0).astype(BF16), mask.astype(F32).astype(BF16), preferred_element_type=F32
        )
        return picked[:count] + picked[count : 2 * count] + picked[2 * count :]

    k, l = grid(width)
    unit = taps / select(taps, k // TAPS == l // TAPS)
    k, l = grid(2 * NPSF * LANES)
    mirror, j, l = l // (NPSF * LANES), l // LANES % NPSF, (l + HALF) % LANES
    i, t = l // height, l % height
    valid = (i < TAPS) & (t < TAPS)
    row_tap = j * TAPS + jnp.where(mirror == 1, t, TAPS - 1 - t)
    col_tap = (NPSF + j) * TAPS + jnp.where(mirror == 1, TAPS - 1 - i, i)
    row_part = select(unit, valid & (k == row_tap))
    col_part = select(unit, valid & (k == col_tap))
    product = row_part * col_part * (1.0 / NPSF)
    return [
        sum(product[:, (m * NPSF + j) * LANES : (m * NPSF + j + 1) * LANES] for j in range(NPSF)) for m in range(2)
    ]


def first_send_kernel(
    tile_rows,
    height,
    rows_each,
    plane_in_ref,
    row_in_ref,
    cover_in_ref,
    taps_in_ref,
    model_ref,
    out_ref,
    plane_ref,
    row_ref,
    cover_ref,
    taps_ref,
    x_ref,
    packed_ref,
    bank_ref,
    block_ref,
    sems,
):
    peers = plane_ref.shape[0]
    total = model_ref.shape[0]
    cuts = max(n for n in (1, 2, 4) if total % (16 * n) == 0)
    pairs = [(plane_in_ref, plane_ref), (row_in_ref, row_ref), (cover_in_ref, cover_ref), (taps_in_ref, taps_ref)]
    for n in range(cuts):
        here = pl.ds(n * (total // cuts), total // cuts)
        pairs.append((model_ref.at[here, :], x_ref.at[here, :]))
    loads = [pltpu.make_async_copy(*pair, sems.at[n]) for n, pair in enumerate(pairs)]
    for load in loads:
        load.start()
    bank_ref[...] = jnp.zeros(bank_ref.shape, F32)
    taps_load = loads.pop(3)
    taps_load.wait()
    for m, row in enumerate(bank_rows(taps_ref[...], height)):
        for n in range(taps_ref.shape[0]):
            bank_ref[2 * n + m : 2 * n + m + 1, :] = row[n : n + 1, :]
    bank = bank_ref[...].astype(BF16)
    for load in loads:
        load.wait()
    parts = max(n for n in (1, 2, 4) if peers % n == 0)
    some = peers // parts
    sends = []
    for part in range(parts):
        here = pl.ds(part * some, some)
        pack_slots(part * some, some, plane_ref, row_ref, cover_ref, tile_rows, height, rows_each, x_ref, packed_ref)
        for d in range(part * some, (part + 1) * some):
            block_ref[d, :rows_each, :] = packed_ref[d * rows_each : (d + 1) * rows_each, :].astype(BF16)
            block_ref[d, rows_each:, :] = bank
        sends.append(pltpu.make_async_copy(block_ref.at[here], out_ref.at[here], sems.at[len(pairs) + part]))
        sends[-1].start()
    for send in sends:
        send.wait()


def update_kernel(bands, tile_rows, height, last, table_ref, factor_ref, returned_ref, model_ref, *rest):
    if last:
        new_ref, back_ref, x_ref, saved, *more_refs = rest
    else:
        x_ref, out_ref, back_ref, packed_ref, *more_refs = rest
    peers, rows_each, _ = returned_ref.shape
    capacity = 2 * rows_each // height
    slots = peers * capacity
    total = x_ref.shape[0] - height
    planes = total // tile_rows
    tiles = planes // bands
    x_ref[:total, :] = model_ref[:total, :]
    for ref in more_refs:
        ref[...] = jnp.zeros(ref.shape, F32)
    for d in range(peers):
        back_ref[d * rows_each : (d + 1) * rows_each, :] = returned_ref[d].astype(F32)
    place = lax.broadcasted_iota(I32, (height, LANES), 0)

    sums = [x_ref, *more_refs]

    def some_peers(step, _):
        for c in range(capacity):
            for n, ref in enumerate(sums):
                slot = (step * len(sums) + n) * capacity + c
                word = table_ref[slot]
                first, sent = first_and_sent(word)
                here = pl.ds(first, height)
                cover = lax.shift_right_logical(word, 2 * PLACE)
                piece = jnp.where(place < cover, back_ref[pl.ds(sent, height), :], 0.0)
                ref[here, :] = ref[here, :] - factor_ref[slot] * piece
        return 0

    lax.fori_loop(0, peers // len(sums), some_peers, 0)

    pos = lax.broadcasted_iota(I32, (tile_rows, LANES), 0)
    saves = []
    for p in range(planes):
        inside = (pos >= table_ref[slots + p // bands]) & (pos < table_ref[slots + tiles + p // bands])
        here = slice(p * tile_rows, (p + 1) * tile_rows)
        new = sum((ref[here, :] for ref in more_refs), x_ref[here, :])
        x_ref[here, :] = jnp.where(inside, jnp.maximum(new, 0.0), 0.0)
        if last:
            rows = pl.ds(p * tile_rows, tile_rows)
            saves.append(pltpu.make_async_copy(x_ref.at[rows, :], new_ref.at[rows, :], saved.at[p]))
            saves[-1].start()
    if not last:

        def pack(slot, _):
            first, sent = first_and_sent(table_ref[slot])
            packed_ref[pl.ds(sent, height), :] = x_ref[pl.ds(first, height), :]
            return 0

        lax.fori_loop(0, slots, pack, 0, unroll=16)
        for d in range(peers):
            out_ref[d, :, :] = packed_ref[d * rows_each : (d + 1) * rows_each, :].astype(BF16)
    for save in saves:
        save.wait()


def tables_kernel(
    tile_rows,
    bands,
    height,
    rows_each,
    slot_ref,
    start_ref,
    stop_ref,
    batch_ref,
    plane_ref,
    row_ref,
    cover_ref,
    step_ref,
    lo_ref,
    hi_ref,
    blur_ref,
    update_ref,
    factor_ref,
    length_ref,
    begin_ref,
    scale_ref,
):
    pieces, exposures = slot_ref.shape
    peers, capacity = plane_ref.shape
    slots = peers * capacity

    def clear(s, _):
        length_ref[s] = 0
        return 0

    lax.fori_loop(0, slots, clear, 0, unroll=16)
    for p in range(scale_ref.shape[0]):
        scale_ref[p] = step_ref[p % bands]
    tiles = lo_ref.shape[0]
    for t in range(tiles):
        update_ref[slots + t] = lo_ref[t]
        update_ref[slots + tiles + t] = hi_ref[t]

    def measure(e, _):
        for k in range(pieces):
            s = slot_ref[k, e]
            s = jnp.where(s >= 0, s, slots)
            length_ref[s] = stop_ref[k, e] - start_ref[k, e]
        return 0

    lax.fori_loop(0, exposures, measure, 0, unroll=8)

    def lay(o, _):
        at = sent = o * rows_each
        for c in range(capacity):
            s = o * capacity + c
            begin_ref[s] = at
            at = at + length_ref[s]
            p = jnp.maximum(plane_ref[o, c], 0)
            cover = cover_ref[o, c]
            update_ref[s] = (p * tile_rows + row_ref[o, c]) | (sent << PLACE) | (cover << 2 * PLACE)
            factor_ref[s] = scale_ref[p]
            sent = sent + cover
        return 0

    lax.fori_loop(0, peers, lay, 0)

    def point(e, _):
        for k in range(pieces):
            s = slot_ref[k, e]
            live = s >= 0
            start = start_ref[k, e]
            begin = jnp.where(live, height + begin_ref[jnp.maximum(s, 0)] - start, 0)
            above = batch_ref[e] if k == 0 else jnp.where(live, start, height)
            blur_ref[k * exposures + e] = begin | (above << SHIFT)
        return 0

    lax.fori_loop(0, exposures, point, 0, unroll=8)


def blur_kernel(
    height,
    pieces,
    batches_each,
    last,
    table_ref,
    weight_ref,
    arrived_ref,
    seen_ref,
    *rest,
):
    if last:
        blur_ref, back_ref, out_ref, residual_out_ref, rows_ref, packed_ref, held_ref, residual_ref, sent = rest
    else:
        out_ref, blur_ref, back_ref, rows_ref, packed_ref, held_ref, bank_ref = rest
    peers, rows_each, _ = out_ref.shape
    exposures = seen_ref.shape[0]
    place = lax.broadcasted_iota(I32, (height, LANES), 0)
    lane = lax.broadcasted_iota(I32, (height, LANES), 1)
    for o in range(peers):
        at = height + o * rows_each
        rows_ref[at : at + rows_each, :] = arrived_ref[o, :rows_each, :].astype(F32)
    if not last:
        extra = arrived_ref.shape[1] - rows_each
        for o in range(peers):
            bank_ref[o * extra : (o + 1) * extra, :] = arrived_ref[o, rows_each:, :].astype(F32)
        gap = lane % height - place
        near = (gap <= HALF) & (gap >= -HALF) & (lane < TAPS * height)

        def operators(o, _):
            for n in range(batches_each):
                for m, ref in enumerate((blur_ref, back_ref)):
                    taps = jnp.broadcast_to(bank_ref[pl.ds(o * extra + 2 * n + m, 1), :], (height, LANES))
                    ref[o * batches_each + n] = jnp.where(
                        near, pltpu.roll(taps, 0, 1, stride=1, stride_axis=0), 0.0
                    ).astype(BF16)
            return 0

        lax.fori_loop(0, peers, operators, 0, unroll=4)

    def shifted(x):
        parts = []
        for v in range(-HALF, HALF + 1):
            moved = x if v == 0 else pltpu.roll(x, v % LANES, 1)
            parts.append(jnp.where((lane >= v) & (lane < LANES + v), moved, jnp.zeros((), BF16)))
        parts.append(jnp.zeros((LANES - TAPS * height, LANES), BF16))
        return jnp.concatenate(parts, axis=0)

    def blur(e):
        stamp = rows_ref[pl.ds(low(table_ref[e]), height), :]
        for k in range(1, pieces):
            word = table_ref[k * exposures + e]
            stamp = jnp.where(place >= high(word), rows_ref[pl.ds(low(word), height), :], stamp)
        predicted = jnp.dot(
            blur_ref[high(table_ref[e])], shifted(stamp.astype(BF16)), preferred_element_type=F32
        )
        residual = weight_ref[e] * (predicted - seen_ref[e].astype(F32))
        if last:
            residual_ref[e] = residual
        held_ref[e * height : (e + 1) * height, :] = residual.astype(BF16)

    def correlate(e):
        result = jnp.dot(
            back_ref[high(table_ref[e])],
            shifted(held_ref[e * height : (e + 1) * height, :]),
            preferred_element_type=F32,
        )
        words = [table_ref[k * exposures + e] for k in range(pieces)]
        for k, word in enumerate(words):
            mask = place >= high(word) if k else None
            if k + 1 < pieces:
                before = place < high(words[k + 1])
                mask = before if mask is None else mask & before
            pltpu.store(packed_ref.at[pl.ds(low(word), height), :], result, mask=mask)

    for e in range(exposures):
        blur(e)
    if last:
        send = pltpu.make_async_copy(residual_ref, residual_out_ref, sent)
        send.start()
    for e in range(exposures):
        correlate(e)
    for o in range(peers):
        at = height + o * rows_each
        out_ref[o, :, :] = packed_ref[at : at + rows_each, :].astype(BF16)
    if last:
        send.wait()


def body(
    model,
    exposures,
    inv_var,
    step_size,
    psf_taps,
    exp_batch,
    send_plane,
    send_row,
    send_cover,
    use_slot,
    use_start,
    use_stop,
    foot_lo,
    foot_hi,
):
    tile_count, bands, tile_rows, columns = model.shape
    count, height, _ = exposures.shape
    peers, capacity = send_plane.shape
    pieces = use_slot.shape[1]
    total = tile_count * bands * tile_rows
    rows_each = capacity * height // 2
    batches_each = psf_taps.shape[0]
    extra = aligned(batches_each * 2)
    block = rows_each + extra
    assert columns == LANES and rows_each % extra == 0 and TAPS * height <= LANES - HALF
    x = model.reshape(total, columns)

    def swap(a):
        return lax.all_to_all(a, "sky", split_axis=0, concat_axis=0, tiled=True)

    outbound = pl.pallas_call(
        functools.partial(first_send_kernel, tile_rows, height, rows_each),
        out_shape=jax.ShapeDtypeStruct((peers, block, columns), BF16),
        in_specs=[hbm()] * 5,
        out_specs=hbm(),
        scratch_shapes=[
            pltpu.SMEM(send_plane.shape, I32),
            pltpu.SMEM(send_row.shape, I32),
            pltpu.SMEM(send_cover.shape, I32),
            pltpu.VMEM(psf_taps.shape, F32),
            pltpu.VMEM((total + height, columns), F32),
            pltpu.VMEM((peers * rows_each + height, columns), F32),
            pltpu.VMEM((extra, columns), F32),
            pltpu.VMEM((peers, block, columns), BF16),
            pltpu.SemaphoreType.DMA((12,)),
        ],
        compiler_params=params(2.5),
        name="first_send",
    )(send_plane, send_row, send_cover, psf_taps, x)
    arrived = swap(outbound)
    slots = peers * capacity
    assert max(total, peers * rows_each) < 1 << PLACE and height < 1 << (31 - 2 * PLACE)
    assert max(peers * rows_each + 2 * height, psf_taps.shape[0] * peers) < 1 << (SHIFT - 1)
    blur_table, update_table, factors = pl.pallas_call(
        functools.partial(tables_kernel, tile_rows, bands, height, rows_each),
        out_shape=(
            jax.ShapeDtypeStruct((pieces * count,), I32),
            jax.ShapeDtypeStruct((slots + 2 * tile_count,), I32),
            jax.ShapeDtypeStruct((slots,), F32),
        ),
        in_specs=[smem()] * 10,
        out_specs=(smem(), smem(), smem()),
        scratch_shapes=[
            pltpu.SMEM((slots + 1,), I32),
            pltpu.SMEM((slots,), I32),
            pltpu.SMEM((tile_count * bands,), F32),
        ],
        compiler_params=params(),
        cost_estimate=pl.CostEstimate(flops=4_000_000, bytes_accessed=8_000_000, transcendentals=0),
        name="tables",
    )(
        use_slot.T,
        use_start.T,
        use_stop.T,
        exp_batch,
        send_plane,
        send_row,
        send_cover,
        step_size,
        foot_lo,
        foot_hi,
    )
    operators = []
    for sweep in range(ITERS):
        last = sweep == ITERS - 1
        rows_shape = jax.ShapeDtypeStruct((peers, rows_each, columns), BF16)
        scratch = [
            pltpu.VMEM((peers * rows_each + 2 * height, columns), F32),
            pltpu.VMEM((peers * rows_each + 2 * height, columns), F32),
            pltpu.VMEM((count * height, columns), BF16),
        ]
        if last:
            scratch += [pltpu.VMEM(exposures.shape, F32), pltpu.SemaphoreType.DMA]
            out_shape, out_specs = (rows_shape, jax.ShapeDtypeStruct(exposures.shape, F32)), (vmem(), hbm())
        else:
            scratch.append(pltpu.VMEM((peers * extra, columns), F32))
            operator_shape = jax.ShapeDtypeStruct((peers * batches_each, height, columns), BF16)
            out_shape, out_specs = (rows_shape, operator_shape, operator_shape), (vmem(),) * 3
        outgoing, *others = pl.pallas_call(
            functools.partial(blur_kernel, height, pieces, batches_each, last),
            out_shape=out_shape,
            in_specs=[smem()] * 2 + [vmem()] * (4 if last else 2),
            out_specs=out_specs,
            scratch_shapes=scratch,
            compiler_params=params(),
            name="blur",
        )(blur_table, inv_var, arrived, exposures, *operators)
        operators = [] if last else others
        returned = swap(outgoing)
        new_shape = jax.ShapeDtypeStruct((total, columns), F32)
        padded = (total + height, columns)
        scratch = [pltpu.VMEM((peers * rows_each + height, columns), F32)]
        if last:
            scratch += [pltpu.VMEM(padded, F32), pltpu.SemaphoreType.DMA((tile_count * bands,))]
        else:
            scratch.append(pltpu.VMEM((peers * rows_each + height, columns), F32))
        sums = max(n for n in (1, 2) if peers % n == 0)
        res = pl.pallas_call(
            functools.partial(update_kernel, bands, tile_rows, height, last),
            out_shape=jax.ShapeDtypeStruct((total, columns), F32)
            if last
            else (jax.ShapeDtypeStruct(padded, F32), rows_shape),
            in_specs=[smem()] * 2 + [vmem(), vmem()],
            out_specs=hbm() if last else (vmem(), vmem()),
            scratch_shapes=scratch + [pltpu.VMEM(padded, F32)] * (sums - 1),
            compiler_params=params(),
            name="update",
        )(update_table, factors, returned, x)
        if last:
            x = res
        else:
            x, outbound = res
            arrived = swap(outbound)
    return (x.reshape(model.shape), others[0])


def solution(mesh):
    both = ("groups", "sky")
    return jax.shard_map(
        body,
        mesh=mesh,
        in_specs=(
            P(both, None, None, None),
            P(both, None, None),
            P(both),
            P(),
            P(both, None),
            P(both),
            P(both, None),
            P(both, None),
            P(both, None),
            P(both, None),
            P(both, None),
            P(both, None),
            P(both),
            P(both),
        ),
        out_specs=(P(both, None, None, None), P(both, None, None)),
        check_vma=False,
    )
```

```python
import functools

import jax
import jax.numpy as jnp
from jax import lax
from jax.experimental import pallas as pl
from jax.experimental.pallas import tpu as pltpu
from jax.sharding import PartitionSpec as P

NPSF = 4
TAPS = 7
ITERS = 2
LANES = 128
HALF = TAPS // 2
F32 = jnp.float32
BF16 = jnp.bfloat16
I32 = jnp.int32
VMEM_BYTES = 24 * 1024 * 1024

smem = lambda: pl.BlockSpec(memory_space=pltpu.SMEM)
vmem = lambda: pl.BlockSpec(memory_space=pltpu.VMEM)
hbm = lambda: pl.BlockSpec(memory_space=pltpu.HBM)


def params(share=1.0):
    return pltpu.CompilerParams(vmem_limit_bytes=int(share * VMEM_BYTES))


SHIFT = 16
PLACE = 13


def low(word):
    return word & ((1 << SHIFT) - 1)


def high(word):
    return lax.shift_right_logical(word, SHIFT)


def aligned(rows):
    return -(-rows // 16) * 16


def first_and_sent(word):
    mask = (1 << PLACE) - 1
    return word & mask, lax.shift_right_logical(word, PLACE) & mask


def pack_slots(begin, count, plane_ref, row_ref, cover_ref, tile_rows, height, rows_each, x_ref, packed_ref):
    capacity = plane_ref.shape[1]

    def peer(d, _):
        at = d * rows_each
        for c in range(capacity):
            first = jnp.maximum(plane_ref[d, c], 0) * tile_rows + row_ref[d, c]
            packed_ref[pl.ds(at, height), :] = x_ref[pl.ds(first, height), :]
            at = at + cover_ref[d, c]
        return 0

    lax.fori_loop(begin, begin + count, peer, 0, unroll=2)


def bank_rows(taps, height):
    count, width = taps.shape

    def grid(columns):
        return (
            lax.broadcasted_iota(I32, (width, columns), 0),
            lax.broadcasted_iota(I32, (width, columns), 1),
        )

    def select(x, mask):
        parts = []
        for _ in range(3):
            parts.append(x.astype(BF16).astype(F32))
            x = x - parts[-1]
        picked = jnp.dot(
            jnp.concatenate(parts, axis=0).astype(BF16), mask.astype(F32).astype(BF16), preferred_element_type=F32
        )
        return picked[:count] + picked[count : 2 * count] + picked[2 * count :]

    k, l = grid(width)
    unit = taps / select(taps, k // TAPS == l // TAPS)
    k, l = grid(2 * NPSF * LANES)
    mirror, j, l = l // (NPSF * LANES), l // LANES % NPSF, (l + HALF) % LANES
    i, t = l // height, l % height
    valid = (i < TAPS) & (t < TAPS)
    row_tap = j * TAPS + jnp.where(mirror == 1, t, TAPS - 1 - t)
    col_tap = (NPSF + j) * TAPS + jnp.where(mirror == 1, TAPS - 1 - i, i)
    row_part = select(unit, valid & (k == row_tap))
    col_part = select(unit, valid & (k == col_tap))
    product = row_part * col_part * (1.0 / NPSF)
    return [
        sum(product[:, (m * NPSF + j) * LANES : (m * NPSF + j + 1) * LANES] for j in range(NPSF)) for m in range(2)
    ]


def first_send_kernel(
    tile_rows,
    height,
    rows_each,
    plane_in_ref,
    row_in_ref,
    cover_in_ref,
    taps_in_ref,
    model_ref,
    out_ref,
    plane_ref,
    row_ref,
    cover_ref,
    taps_ref,
    x_ref,
    packed_ref,
    bank_ref,
    block_ref,
    sems,
):
    peers = plane_ref.shape[0]
    total = model_ref.shape[0]
    cuts = max(n for n in (1, 2, 4) if total % (16 * n) == 0)
    pairs = [(plane_in_ref, plane_ref), (row_in_ref, row_ref), (cover_in_ref, cover_ref), (taps_in_ref, taps_ref)]
    for n in range(cuts):
        here = pl.ds(n * (total // cuts), total // cuts)
        pairs.append((model_ref.at[here, :], x_ref.at[here, :]))
    loads = [pltpu.make_async_copy(*pair, sems.at[n]) for n, pair in enumerate(pairs)]
    for load in loads:
        load.start()
    bank_ref[...] = jnp.zeros(bank_ref.shape, F32)
    taps_load = loads.pop(3)
    taps_load.wait()
    for m, row in enumerate(bank_rows(taps_ref[...], height)):
        for n in range(taps_ref.shape[0]):
            bank_ref[2 * n + m : 2 * n + m + 1, :] = row[n : n + 1, :]
    bank = bank_ref[...].astype(BF16)
    for load in loads:
        load.wait()
    parts = max(n for n in (1, 2, 4) if peers % n == 0)
    some = peers // parts
    sends = []
    for part in range(parts):
        here = pl.ds(part * some, some)
        pack_slots(part * some, some, plane_ref, row_ref, cover_ref, tile_rows, height, rows_each, x_ref, packed_ref)
        for d in range(part * some, (part + 1) * some):
            block_ref[d, :rows_each, :] = packed_ref[d * rows_each : (d + 1) * rows_each, :].astype(BF16)
            block_ref[d, rows_each:, :] = bank
        sends.append(pltpu.make_async_copy(block_ref.at[here], out_ref.at[here], sems.at[len(pairs) + part]))
        sends[-1].start()
    for send in sends:
        send.wait()


def update_kernel(bands, tile_rows, height, last, table_ref, factor_ref, returned_ref, *rest):
    if last:
        *model_refs, new_ref, back_ref, x_ref, more_ref, saved = rest
    else:
        *model_refs, x_ref, more_ref, out_ref, back_ref, packed_ref = rest
    peers, rows_each, _ = returned_ref.shape
    capacity = 2 * rows_each // height
    slots = peers * capacity
    total = x_ref.shape[0] - height
    planes = total // tile_rows
    tiles = planes // bands

    def clamped(value, pos, tile):
        inside = (pos >= table_ref[2 * slots + tile]) & (pos < table_ref[2 * slots + tiles + tile])
        return jnp.where(inside, jnp.maximum(value, 0.0), 0.0)

    pos = lax.broadcasted_iota(I32, (tile_rows, LANES), 0)
    for p in range(planes):
        here = slice(p * tile_rows, (p + 1) * tile_rows)
        if last:
            x_ref[here, :] = clamped(model_refs[0][here, :] + model_refs[1][here, :], pos, p // bands)
        else:
            x_ref[here, :] = model_refs[0][here, :]
    more_ref[...] = jnp.zeros(more_ref.shape, F32)
    for d in range(peers):
        back_ref[d * rows_each : (d + 1) * rows_each, :] = returned_ref[d].astype(F32)
    place = lax.broadcasted_iota(I32, (height, LANES), 0)

    sums = [x_ref, more_ref] if peers % 2 == 0 else [x_ref]

    def some_peers(step, _):
        for c in range(capacity):
            for n, ref in enumerate(sums):
                slot = (step * len(sums) + n) * capacity + c
                word = table_ref[slot]
                first, sent = first_and_sent(word)
                here = pl.ds(first, height)
                cover = lax.shift_right_logical(word, 2 * PLACE)
                piece = jnp.where(place < cover, back_ref[pl.ds(sent, height), :], 0.0)
                ref[here, :] = ref[here, :] - factor_ref[slot] * piece
        return 0

    lax.fori_loop(0, peers // len(sums), some_peers, 0)

    if last:
        saves = []
        for p in range(planes):
            here = slice(p * tile_rows, (p + 1) * tile_rows)
            x_ref[here, :] = clamped(x_ref[here, :] + more_ref[here, :], pos, p // bands)
            rows = pl.ds(p * tile_rows, tile_rows)
            saves.append(pltpu.make_async_copy(x_ref.at[rows, :], new_ref.at[rows, :], saved.at[p]))
            saves[-1].start()
        for save in saves:
            save.wait()
        return

    def pack(slot, _):
        first, sent = first_and_sent(table_ref[slot])
        here = pl.ds(first, height)
        bounds = table_ref[slots + slot]
        inside = (place >= low(bounds)) & (place < high(bounds))
        piece = jnp.where(inside, jnp.maximum(x_ref[here, :] + more_ref[here, :], 0.0), 0.0)
        packed_ref[pl.ds(sent, height), :] = piece
        return 0

    lax.fori_loop(0, slots, pack, 0, unroll=16)
    for d in range(peers):
        out_ref[d] = packed_ref[d * rows_each : (d + 1) * rows_each, :].astype(BF16)


def tables_kernel(
    tile_rows,
    bands,
    height,
    rows_each,
    slot_ref,
    start_ref,
    stop_ref,
    batch_ref,
    plane_ref,
    row_ref,
    cover_ref,
    step_ref,
    lo_ref,
    hi_ref,
    blur_ref,
    update_ref,
    factor_ref,
    length_ref,
    begin_ref,
    scale_ref,
    foot_ref,
):
    pieces, exposures = slot_ref.shape
    peers, capacity = plane_ref.shape
    slots = peers * capacity

    def clear(s, _):
        length_ref[s] = 0
        return 0

    lax.fori_loop(0, slots, clear, 0, unroll=16)
    planes = scale_ref.shape[0]
    for p in range(planes):
        scale_ref[p] = step_ref[p % bands]
        foot_ref[p] = lo_ref[p // bands]
        foot_ref[planes + p] = hi_ref[p // bands]
    tiles = lo_ref.shape[0]
    for t in range(tiles):
        update_ref[2 * slots + t] = lo_ref[t]
        update_ref[2 * slots + tiles + t] = hi_ref[t]

    def measure(e, _):
        for k in range(pieces):
            s = slot_ref[k, e]
            s = jnp.where(s >= 0, s, slots)
            length_ref[s] = stop_ref[k, e] - start_ref[k, e]
        return 0

    lax.fori_loop(0, exposures, measure, 0, unroll=8)

    def lay(o, _):
        at = sent = o * rows_each
        for c in range(capacity):
            s = o * capacity + c
            begin_ref[s] = at
            at = at + length_ref[s]
            p = jnp.maximum(plane_ref[o, c], 0)
            cover = cover_ref[o, c]
            row = row_ref[o, c]
            update_ref[s] = (p * tile_rows + row) | (sent << PLACE) | (cover << 2 * PLACE)
            lo = jnp.clip(foot_ref[p] - row, 0, height)
            hi = jnp.clip(foot_ref[planes + p] - row, 0, height)
            update_ref[slots + s] = lo | (hi << SHIFT)
            factor_ref[s] = scale_ref[p]
            sent = sent + cover
        return 0

    lax.fori_loop(0, peers, lay, 0)

    def point(e, _):
        for k in range(pieces):
            s = slot_ref[k, e]
            live = s >= 0
            start = start_ref[k, e]
            begin = jnp.where(live, height + begin_ref[jnp.maximum(s, 0)] - start, 0)
            above = batch_ref[e] if k == 0 else jnp.where(live, start, height)
            blur_ref[k * exposures + e] = begin | (above << SHIFT)
        return 0

    lax.fori_loop(0, exposures, point, 0, unroll=8)


def blur_kernel(
    height,
    pieces,
    batches_each,
    last,
    table_ref,
    weight_ref,
    arrived_ref,
    seen_ref,
    *rest,
):
    if last:
        blur_ref, back_ref, out_ref, residual_ref, rows_ref, packed_ref, held_ref = rest
    else:
        out_ref, blur_ref, back_ref, rows_ref, packed_ref, held_ref, bank_ref = rest
    peers, rows_each, _ = out_ref.shape
    exposures = seen_ref.shape[0]
    place = lax.broadcasted_iota(I32, (height, LANES), 0)
    lane = lax.broadcasted_iota(I32, (height, LANES), 1)
    for o in range(peers):
        at = height + o * rows_each
        rows_ref[at : at + rows_each, :] = arrived_ref[o, :rows_each, :].astype(F32)
    if not last:
        extra = arrived_ref.shape[1] - rows_each
        for o in range(peers):
            bank_ref[o * extra : (o + 1) * extra, :] = arrived_ref[o, rows_each:, :].astype(F32)
        gap = lane % height - place
        near = (gap <= HALF) & (gap >= -HALF) & (lane < TAPS * height)

        def operators(o, _):
            for n in range(batches_each):
                for m, ref in enumerate((blur_ref, back_ref)):
                    taps = jnp.broadcast_to(bank_ref[pl.ds(o * extra + 2 * n + m, 1), :], (height, LANES))
                    ref[o * batches_each + n] = jnp.where(
                        near, pltpu.roll(taps, 0, 1, stride=1, stride_axis=0), 0.0
                    ).astype(BF16)
            return 0

        lax.fori_loop(0, peers, operators, 0, unroll=4)

    def shifted(x):
        parts = []
        for v in range(-HALF, HALF + 1):
            moved = x if v == 0 else pltpu.roll(x, v % LANES, 1)
            parts.append(jnp.where((lane >= v) & (lane < LANES + v), moved, jnp.zeros((), BF16)))
        parts.append(jnp.zeros((LANES - TAPS * height, LANES), BF16))
        return jnp.concatenate(parts, axis=0)

    def blur(e):
        stamp = rows_ref[pl.ds(low(table_ref[e]), height), :]
        for k in range(1, pieces):
            word = table_ref[k * exposures + e]
            stamp = jnp.where(place >= high(word), rows_ref[pl.ds(low(word), height), :], stamp)
        predicted = jnp.dot(
            blur_ref[high(table_ref[e])], shifted(stamp.astype(BF16)), preferred_element_type=F32
        )
        residual = weight_ref[e] * (predicted - seen_ref[e].astype(F32))
        if last:
            residual_ref[e] = residual
        held_ref[e * height : (e + 1) * height, :] = residual.astype(BF16)

    def correlate(e):
        result = jnp.dot(
            back_ref[high(table_ref[e])],
            shifted(held_ref[e * height : (e + 1) * height, :]),
            preferred_element_type=F32,
        )
        words = [table_ref[k * exposures + e] for k in range(pieces)]
        for k, word in enumerate(words):
            mask = place >= high(word) if k else None
            if k + 1 < pieces:
                before = place < high(words[k + 1])
                mask = before if mask is None else mask & before
            pltpu.store(packed_ref.at[pl.ds(low(word), height), :], result, mask=mask)

    for e in range(exposures):
        blur(e)
    for e in range(exposures):
        correlate(e)
    for o in range(peers):
        at = height + o * rows_each
        out_ref[o, :, :] = packed_ref[at : at + rows_each, :].astype(BF16)


def save_kernel(from_ref, to_ref, sems):
    parts = sems.shape[0]
    some = from_ref.shape[0] // parts
    copies = []
    for n in range(parts):
        here = pl.ds(n * some, some)
        copies.append(pltpu.make_async_copy(from_ref.at[here], to_ref.at[here], sems.at[n]))
        copies[-1].start()
    for copy in copies:
        copy.wait()


def body(
    model,
    exposures,
    inv_var,
    step_size,
    psf_taps,
    exp_batch,
    send_plane,
    send_row,
    send_cover,
    use_slot,
    use_start,
    use_stop,
    foot_lo,
    foot_hi,
):
    tile_count, bands, tile_rows, columns = model.shape
    count, height, _ = exposures.shape
    peers, capacity = send_plane.shape
    pieces = use_slot.shape[1]
    total = tile_count * bands * tile_rows
    rows_each = capacity * height // 2
    batches_each = psf_taps.shape[0]
    extra = aligned(batches_each * 2)
    block = rows_each + extra
    assert columns == LANES and rows_each % extra == 0 and TAPS * height <= LANES - HALF
    x = model.reshape(total, columns)

    def swap(a):
        return lax.all_to_all(a, "sky", split_axis=0, concat_axis=0, tiled=True)

    outbound = pl.pallas_call(
        functools.partial(first_send_kernel, tile_rows, height, rows_each),
        out_shape=jax.ShapeDtypeStruct((peers, block, columns), BF16),
        in_specs=[hbm()] * 5,
        out_specs=hbm(),
        scratch_shapes=[
            pltpu.SMEM(send_plane.shape, I32),
            pltpu.SMEM(send_row.shape, I32),
            pltpu.SMEM(send_cover.shape, I32),
            pltpu.VMEM(psf_taps.shape, F32),
            pltpu.VMEM((total + height, columns), F32),
            pltpu.VMEM((peers * rows_each + height, columns), F32),
            pltpu.VMEM((extra, columns), F32),
            pltpu.VMEM((peers, block, columns), BF16),
            pltpu.SemaphoreType.DMA((12,)),
        ],
        compiler_params=params(2.5),
        name="first_send",
    )(send_plane, send_row, send_cover, psf_taps, x)
    arrived = swap(outbound)
    slots = peers * capacity
    assert max(total, peers * rows_each) < 1 << PLACE and height < 1 << (31 - 2 * PLACE)
    assert max(peers * rows_each + 2 * height, psf_taps.shape[0] * peers) < 1 << (SHIFT - 1)
    blur_table, update_table, factors = pl.pallas_call(
        functools.partial(tables_kernel, tile_rows, bands, height, rows_each),
        out_shape=(
            jax.ShapeDtypeStruct((pieces * count,), I32),
            jax.ShapeDtypeStruct((2 * slots + 2 * tile_count,), I32),
            jax.ShapeDtypeStruct((slots,), F32),
        ),
        in_specs=[smem()] * 10,
        out_specs=(smem(), smem(), smem()),
        scratch_shapes=[
            pltpu.SMEM((slots + 1,), I32),
            pltpu.SMEM((slots,), I32),
            pltpu.SMEM((tile_count * bands,), F32),
            pltpu.SMEM((2 * tile_count * bands,), I32),
        ],
        compiler_params=params(),
        cost_estimate=pl.CostEstimate(flops=4_000_000, bytes_accessed=8_000_000, transcendentals=0),
        name="tables",
    )(
        use_slot.T,
        use_start.T,
        use_stop.T,
        exp_batch,
        send_plane,
        send_row,
        send_cover,
        step_size,
        foot_lo,
        foot_hi,
    )
    operators = []
    x = [x]
    for sweep in range(ITERS):
        last = sweep == ITERS - 1
        rows_shape = jax.ShapeDtypeStruct((peers, rows_each, columns), BF16)
        scratch = [
            pltpu.VMEM((peers * rows_each + 2 * height, columns), F32),
            pltpu.VMEM((peers * rows_each + 2 * height, columns), F32),
            pltpu.VMEM((count * height, columns), BF16),
        ]
        if last:
            out_shape, out_specs = (rows_shape, jax.ShapeDtypeStruct(exposures.shape, F32)), (vmem(), vmem())
        else:
            scratch.append(pltpu.VMEM((peers * extra, columns), F32))
            operator_shape = jax.ShapeDtypeStruct((peers * batches_each, height, columns), BF16)
            out_shape, out_specs = (rows_shape, operator_shape, operator_shape), (vmem(),) * 3
        outgoing, *others = pl.pallas_call(
            functools.partial(blur_kernel, height, pieces, batches_each, last),
            out_shape=out_shape,
            in_specs=[smem()] * 2 + [vmem()] * (4 if last else 2),
            out_specs=out_specs,
            scratch_shapes=scratch,
            compiler_params=params(),
            name="blur",
        )(blur_table, inv_var, arrived, exposures, *operators)
        operators = [] if last else others
        returned = swap(outgoing)
        new_shape = jax.ShapeDtypeStruct((total, columns), F32)
        padded = (total + height, columns)
        back = pltpu.VMEM((peers * rows_each + height, columns), F32)
        if last:
            out_shape, out_specs = jax.ShapeDtypeStruct((total, columns), F32), hbm()
            scratch = [back, pltpu.VMEM(padded, F32), pltpu.VMEM(padded, F32)]
            scratch.append(pltpu.SemaphoreType.DMA((tile_count * bands,)))
        else:
            out_shape = (jax.ShapeDtypeStruct(padded, F32), jax.ShapeDtypeStruct(padded, F32), rows_shape)
            out_specs, scratch = (vmem(),) * 3, [back, back]
        res = pl.pallas_call(
            functools.partial(update_kernel, bands, tile_rows, height, last),
            out_shape=out_shape,
            in_specs=[smem()] * 2 + [vmem()] * (1 + len(x)),
            out_specs=out_specs,
            scratch_shapes=scratch,
            compiler_params=params(),
            name="update",
        )(update_table, factors, returned, *x)
        if not last:
            *x, outbound = res
            arrived = swap(outbound)
    residual = pl.pallas_call(
        save_kernel,
        out_shape=jax.ShapeDtypeStruct(exposures.shape, F32),
        in_specs=[vmem()],
        out_specs=hbm(),
        scratch_shapes=[pltpu.SemaphoreType.DMA((max(n for n in (1, 2, 4) if count % n == 0),))],
        compiler_params=params(),
        cost_estimate=pl.CostEstimate(flops=4_000_000, bytes_accessed=8_000_000, transcendentals=0),
        name="save",
    )(others[0])
    return (res.reshape(model.shape), residual)


def solution(mesh):
    both = ("groups", "sky")
    return jax.shard_map(
        body,
        mesh=mesh,
        in_specs=(
            P(both, None, None, None),
            P(both, None, None),
            P(both),
            P(),
            P(both, None),
            P(both),
            P(both, None),
            P(both, None),
            P(both, None),
            P(both, None),
            P(both, None),
            P(both, None),
            P(both),
            P(both),
        ),
        out_specs=(P(both, None, None, None), P(both, None, None)),
        check_vma=False,
    )
```

```python
import functools

import jax
import jax.numpy as jnp
from jax import lax
from jax.experimental import pallas as pl
from jax.experimental.pallas import tpu as pltpu
from jax.sharding import PartitionSpec as P

NPSF = 4
TAPS = 7
ITERS = 2
LANES = 128
HALF = TAPS // 2
F32 = jnp.float32
BF16 = jnp.bfloat16
I32 = jnp.int32
VMEM_BYTES = 24 * 1024 * 1024

smem = lambda: pl.BlockSpec(memory_space=pltpu.SMEM)
vmem = lambda: pl.BlockSpec(memory_space=pltpu.VMEM)
hbm = lambda: pl.BlockSpec(memory_space=pltpu.HBM)


def params(share=1.0):
    return pltpu.CompilerParams(vmem_limit_bytes=int(share * VMEM_BYTES))


SHIFT = 16
PLACE = 13


def low(word):
    return word & ((1 << SHIFT) - 1)


def high(word):
    return lax.shift_right_logical(word, SHIFT)


def aligned(rows):
    return -(-rows // 16) * 16


def first_and_sent(word):
    mask = (1 << PLACE) - 1
    return word & mask, lax.shift_right_logical(word, PLACE) & mask


def pack_slots(begin, count, plane_ref, row_ref, cover_ref, tile_rows, height, rows_each, x_ref, packed_ref):
    capacity = plane_ref.shape[1]

    def peer(d, _):
        at = d * rows_each
        for c in range(capacity):
            first = jnp.maximum(plane_ref[d, c], 0) * tile_rows + row_ref[d, c]
            packed_ref[pl.ds(at, height), :] = x_ref[pl.ds(first, height), :]
            at = at + cover_ref[d, c]
        return 0

    lax.fori_loop(begin, begin + count, peer, 0, unroll=min(4, count))


def bank_rows(taps, height):
    count, width = taps.shape

    def grid(columns):
        return (
            lax.broadcasted_iota(I32, (width, columns), 0),
            lax.broadcasted_iota(I32, (width, columns), 1),
        )

    def select(x, mask):
        parts = []
        for _ in range(3):
            parts.append(x.astype(BF16).astype(F32))
            x = x - parts[-1]
        picked = jnp.dot(
            jnp.concatenate(parts, axis=0).astype(BF16), mask.astype(F32).astype(BF16), preferred_element_type=F32
        )
        return picked[:count] + picked[count : 2 * count] + picked[2 * count :]

    k, l = grid(2 * NPSF * LANES)
    mirror, j, l = l // (NPSF * LANES), l // LANES % NPSF, (l + HALF) % LANES
    i, t = l // height, l % height
    valid = (i < TAPS) & (t < TAPS)
    row_tap = j * TAPS + jnp.where(mirror == 1, t, TAPS - 1 - t)
    col_tap = (NPSF + j) * TAPS + jnp.where(mirror == 1, TAPS - 1 - i, i)
    picked = select(taps, valid & (k == row_tap)) * select(taps, valid & (k == col_tap))
    k, l = grid(NPSF * LANES)
    whole = select(taps, k // TAPS == l // LANES) * select(taps, k // TAPS == NPSF + l // LANES)
    product = picked / (jnp.concatenate([whole, whole], axis=1) * NPSF)
    return [
        sum(product[:, (m * NPSF + j) * LANES : (m * NPSF + j + 1) * LANES] for j in range(NPSF)) for m in range(2)
    ]


def first_send_kernel(
    tile_rows,
    height,
    rows_each,
    plane_in_ref,
    row_in_ref,
    cover_in_ref,
    taps_in_ref,
    model_ref,
    out_ref,
    plane_ref,
    row_ref,
    cover_ref,
    taps_ref,
    x_ref,
    packed_ref,
    bank_ref,
    block_ref,
    sems,
):
    peers = plane_ref.shape[0]
    total = model_ref.shape[0]
    cuts = max(n for n in (1, 2, 4) if total % (16 * n) == 0)
    pairs = [(plane_in_ref, plane_ref), (row_in_ref, row_ref), (cover_in_ref, cover_ref), (taps_in_ref, taps_ref)]
    for n in range(cuts):
        here = pl.ds(n * (total // cuts), total // cuts)
        pairs.append((model_ref.at[here, :], x_ref.at[here, :]))
    loads = [pltpu.make_async_copy(*pair, sems.at[n]) for n, pair in enumerate(pairs)]
    for load in loads:
        load.start()
    bank_ref[...] = jnp.zeros(bank_ref.shape, F32)
    taps_load = loads.pop(3)
    taps_load.wait()
    for m, row in enumerate(bank_rows(taps_ref[...], height)):
        for n in range(taps_ref.shape[0]):
            bank_ref[2 * n + m : 2 * n + m + 1, :] = row[n : n + 1, :]
    bank = bank_ref[...].astype(BF16)
    for load in loads:
        load.wait()
    parts = max(n for n in (1, 2, 4) if peers % n == 0)
    some = peers // parts
    sends = []
    for part in range(parts):
        here = pl.ds(part * some, some)
        pack_slots(part * some, some, plane_ref, row_ref, cover_ref, tile_rows, height, rows_each, x_ref, packed_ref)
        for d in range(part * some, (part + 1) * some):
            block_ref[d, :rows_each, :] = packed_ref[d * rows_each : (d + 1) * rows_each, :].astype(BF16)
            block_ref[d, rows_each:, :] = bank
        sends.append(pltpu.make_async_copy(block_ref.at[here], out_ref.at[here], sems.at[len(pairs) + part]))
        sends[-1].start()
    for send in sends:
        send.wait()


def update_kernel(bands, tile_rows, height, last, table_ref, factor_ref, returned_ref, model_ref, *rest):
    if last:
        new_ref, back_ref, x_ref, saved, *more_refs = rest
    else:
        x_ref, out_ref, back_ref, packed_ref, *more_refs = rest
    peers, rows_each, _ = returned_ref.shape
    capacity = 2 * rows_each // height
    slots = peers * capacity
    total = x_ref.shape[0] - height
    planes = total // tile_rows
    tiles = planes // bands
    x_ref[:total, :] = model_ref[:total, :]
    for ref in more_refs:
        ref[...] = jnp.zeros(ref.shape, F32)
    for d in range(peers):
        back_ref[d * rows_each : (d + 1) * rows_each, :] = returned_ref[d].astype(F32)
    place = lax.broadcasted_iota(I32, (height, LANES), 0)

    sums = [x_ref, *more_refs]

    def some_peers(step, _):
        for c in range(capacity):
            for n, ref in enumerate(sums):
                slot = (step * len(sums) + n) * capacity + c
                word = table_ref[slot]
                first, sent = first_and_sent(word)
                here = pl.ds(first, height)
                cover = lax.shift_right_logical(word, 2 * PLACE)
                piece = jnp.where(place < cover, back_ref[pl.ds(sent, height), :], 0.0)
                ref[here, :] = ref[here, :] - factor_ref[slot] * piece
        return 0

    lax.fori_loop(0, peers // len(sums), some_peers, 0, unroll=2)

    pos = lax.broadcasted_iota(I32, (tile_rows, LANES), 0)
    saves = []
    for p in range(planes):
        inside = (pos >= table_ref[slots + p // bands]) & (pos < table_ref[slots + tiles + p // bands])
        here = slice(p * tile_rows, (p + 1) * tile_rows)
        new = sum((ref[here, :] for ref in more_refs), x_ref[here, :])
        x_ref[here, :] = jnp.where(inside, jnp.maximum(new, 0.0), 0.0)
        if last:
            rows = pl.ds(p * tile_rows, tile_rows)
            saves.append(pltpu.make_async_copy(x_ref.at[rows, :], new_ref.at[rows, :], saved.at[p]))
            saves[-1].start()
    if not last:

        def pack(slot, _):
            first, sent = first_and_sent(table_ref[slot])
            packed_ref[pl.ds(sent, height), :] = x_ref[pl.ds(first, height), :]
            return 0

        lax.fori_loop(0, slots, pack, 0, unroll=64)
        for d in range(peers):
            out_ref[d, :, :] = packed_ref[d * rows_each : (d + 1) * rows_each, :].astype(BF16)
    for save in saves:
        save.wait()


def tables_kernel(
    tile_rows,
    bands,
    height,
    rows_each,
    slot_ref,
    start_ref,
    stop_ref,
    batch_ref,
    plane_ref,
    row_ref,
    cover_ref,
    step_ref,
    lo_ref,
    hi_ref,
    blur_ref,
    update_ref,
    factor_ref,
    length_ref,
    begin_ref,
    scale_ref,
):
    pieces, exposures = slot_ref.shape
    peers, capacity = plane_ref.shape
    slots = peers * capacity

    def clear(s, _):
        length_ref[s] = 0
        return 0

    lax.fori_loop(0, slots, clear, 0, unroll=16)
    for p in range(scale_ref.shape[0]):
        scale_ref[p] = step_ref[p % bands]
    tiles = lo_ref.shape[0]
    for t in range(tiles):
        update_ref[slots + t] = lo_ref[t]
        update_ref[slots + tiles + t] = hi_ref[t]

    def measure(e, _):
        for k in range(pieces):
            s = slot_ref[k, e]
            s = jnp.where(s >= 0, s, slots)
            length_ref[s] = stop_ref[k, e] - start_ref[k, e]
        return 0

    lax.fori_loop(0, exposures, measure, 0, unroll=8)

    def lay(o, _):
        at = sent = o * rows_each
        for c in range(capacity):
            s = o * capacity + c
            begin_ref[s] = at
            at = at + length_ref[s]
            p = jnp.maximum(plane_ref[o, c], 0)
            cover = cover_ref[o, c]
            update_ref[s] = (p * tile_rows + row_ref[o, c]) | (sent << PLACE) | (cover << 2 * PLACE)
            factor_ref[s] = scale_ref[p]
            sent = sent + cover
        return 0

    lax.fori_loop(0, peers, lay, 0)

    def point(e, _):
        for k in range(pieces):
            s = slot_ref[k, e]
            live = s >= 0
            start = start_ref[k, e]
            begin = jnp.where(live, height + begin_ref[jnp.maximum(s, 0)] - start, 0)
            above = batch_ref[e] if k == 0 else jnp.where(live, start, height)
            blur_ref[k * exposures + e] = begin | (above << SHIFT)
        return 0

    lax.fori_loop(0, exposures, point, 0, unroll=8)


def blur_kernel(
    height,
    pieces,
    batches_each,
    last,
    table_ref,
    weight_ref,
    arrived_ref,
    seen_ref,
    *rest,
):
    if last:
        blur_ref, back_ref, out_ref, residual_out_ref, rows_ref, packed_ref, held_ref, residual_ref, sent = rest
    else:
        out_ref, blur_ref, back_ref, rows_ref, packed_ref, held_ref, bank_ref = rest
    peers, rows_each, _ = out_ref.shape
    exposures = seen_ref.shape[0]
    place = lax.broadcasted_iota(I32, (height, LANES), 0)
    lane = lax.broadcasted_iota(I32, (height, LANES), 1)
    for o in range(peers):
        at = height + o * rows_each
        rows_ref[at : at + rows_each, :] = arrived_ref[o, :rows_each, :].astype(F32)
    if not last:
        extra = arrived_ref.shape[1] - rows_each
        for o in range(peers):
            bank_ref[o * extra : (o + 1) * extra, :] = arrived_ref[o, rows_each:, :].astype(F32)
        gap = lane % height - place
        near = (gap <= HALF) & (gap >= -HALF) & (lane < TAPS * height)

        def operators(o, _):
            for n in range(batches_each):
                for m, ref in enumerate((blur_ref, back_ref)):
                    taps = jnp.broadcast_to(bank_ref[pl.ds(o * extra + 2 * n + m, 1), :], (height, LANES))
                    ref[o * batches_each + n] = jnp.where(
                        near, pltpu.roll(taps, 0, 1, stride=1, stride_axis=0), 0.0
                    ).astype(BF16)
            return 0

        lax.fori_loop(0, peers, operators, 0, unroll=min(16, peers))

    def shifted(x):
        parts = []
        for v in range(-HALF, HALF + 1):
            moved = x if v == 0 else pltpu.roll(x, v % LANES, 1)
            parts.append(jnp.where((lane >= v) & (lane < LANES + v), moved, jnp.zeros((), BF16)))
        parts.append(jnp.zeros((LANES - TAPS * height, LANES), BF16))
        return jnp.concatenate(parts, axis=0)

    def blur(e):
        stamp = rows_ref[pl.ds(low(table_ref[e]), height), :]
        for k in range(1, pieces):
            word = table_ref[k * exposures + e]
            stamp = jnp.where(place >= high(word), rows_ref[pl.ds(low(word), height), :], stamp)
        predicted = jnp.dot(
            blur_ref[high(table_ref[e])], shifted(stamp.astype(BF16)), preferred_element_type=F32
        )
        residual = weight_ref[e] * (predicted - seen_ref[e].astype(F32))
        if last:
            residual_ref[e] = residual
        held_ref[e * height : (e + 1) * height, :] = residual.astype(BF16)

    def correlate(e):
        result = jnp.dot(
            back_ref[high(table_ref[e])],
            shifted(held_ref[e * height : (e + 1) * height, :]),
            preferred_element_type=F32,
        )
        words = [table_ref[k * exposures + e] for k in range(pieces)]
        for k, word in enumerate(words):
            mask = place >= high(word) if k else None
            if k + 1 < pieces:
                before = place < high(words[k + 1])
                mask = before if mask is None else mask & before
            pltpu.store(packed_ref.at[pl.ds(low(word), height), :], result, mask=mask)

    for e in range(exposures):
        blur(e)
    if last:
        send = pltpu.make_async_copy(residual_ref, residual_out_ref, sent)
        send.start()
    for e in range(exposures):
        correlate(e)
    for o in range(peers):
        at = height + o * rows_each
        out_ref[o, :, :] = packed_ref[at : at + rows_each, :].astype(BF16)
    if last:
        send.wait()


def body(
    model,
    exposures,
    inv_var,
    step_size,
    psf_taps,
    exp_batch,
    send_plane,
    send_row,
    send_cover,
    use_slot,
    use_start,
    use_stop,
    foot_lo,
    foot_hi,
):
    tile_count, bands, tile_rows, columns = model.shape
    count, height, _ = exposures.shape
    peers, capacity = send_plane.shape
    pieces = use_slot.shape[1]
    total = tile_count * bands * tile_rows
    rows_each = capacity * height // 2
    batches_each = psf_taps.shape[0]
    extra = aligned(batches_each * 2)
    block = rows_each + extra
    assert columns == LANES and rows_each % extra == 0 and TAPS * height <= LANES - HALF
    x = model.reshape(total, columns)

    def swap(a):
        return lax.all_to_all(a, "sky", split_axis=0, concat_axis=0, tiled=True)

    outbound = pl.pallas_call(
        functools.partial(first_send_kernel, tile_rows, height, rows_each),
        out_shape=jax.ShapeDtypeStruct((peers, block, columns), BF16),
        in_specs=[hbm()] * 5,
        out_specs=hbm(),
        scratch_shapes=[
            pltpu.SMEM(send_plane.shape, I32),
            pltpu.SMEM(send_row.shape, I32),
            pltpu.SMEM(send_cover.shape, I32),
            pltpu.VMEM(psf_taps.shape, F32),
            pltpu.VMEM((total + height, columns), F32),
            pltpu.VMEM((peers * rows_each + height, columns), F32),
            pltpu.VMEM((extra, columns), F32),
            pltpu.VMEM((peers, block, columns), BF16),
            pltpu.SemaphoreType.DMA((12,)),
        ],
        compiler_params=params(2.5),
        name="first_send",
    )(send_plane, send_row, send_cover, psf_taps, x)
    arrived = swap(outbound)
    slots = peers * capacity
    assert max(total, peers * rows_each) < 1 << PLACE and height < 1 << (31 - 2 * PLACE)
    assert max(peers * rows_each + 2 * height, psf_taps.shape[0] * peers) < 1 << (SHIFT - 1)
    blur_table, update_table, factors = pl.pallas_call(
        functools.partial(tables_kernel, tile_rows, bands, height, rows_each),
        out_shape=(
            jax.ShapeDtypeStruct((pieces * count,), I32),
            jax.ShapeDtypeStruct((slots + 2 * tile_count,), I32),
            jax.ShapeDtypeStruct((slots,), F32),
        ),
        in_specs=[smem()] * 10,
        out_specs=(smem(), smem(), smem()),
        scratch_shapes=[
            pltpu.SMEM((slots + 1,), I32),
            pltpu.SMEM((slots,), I32),
            pltpu.SMEM((tile_count * bands,), F32),
        ],
        compiler_params=params(),
        cost_estimate=pl.CostEstimate(flops=4_000_000, bytes_accessed=8_000_000, transcendentals=0),
        name="tables",
    )(
        use_slot.T,
        use_start.T,
        use_stop.T,
        exp_batch,
        send_plane,
        send_row,
        send_cover,
        step_size,
        foot_lo,
        foot_hi,
    )
    operators = []
    for sweep in range(ITERS):
        last = sweep == ITERS - 1
        rows_shape = jax.ShapeDtypeStruct((peers, rows_each, columns), BF16)
        scratch = [
            pltpu.VMEM((peers * rows_each + 2 * height, columns), F32),
            pltpu.VMEM((peers * rows_each + 2 * height, columns), F32),
            pltpu.VMEM((count * height, columns), BF16),
        ]
        if last:
            scratch += [pltpu.VMEM(exposures.shape, F32), pltpu.SemaphoreType.DMA]
            out_shape, out_specs = (rows_shape, jax.ShapeDtypeStruct(exposures.shape, F32)), (vmem(), hbm())
        else:
            scratch.append(pltpu.VMEM((peers * extra, columns), F32))
            operator_shape = jax.ShapeDtypeStruct((peers * batches_each, height, columns), BF16)
            out_shape, out_specs = (rows_shape, operator_shape, operator_shape), (vmem(),) * 3
        outgoing, *others = pl.pallas_call(
            functools.partial(blur_kernel, height, pieces, batches_each, last),
            out_shape=out_shape,
            in_specs=[smem()] * 2 + [vmem()] * (4 if last else 2),
            out_specs=out_specs,
            scratch_shapes=scratch,
            compiler_params=params(),
            name="blur",
        )(blur_table, inv_var, arrived, exposures, *operators)
        operators = [] if last else others
        returned = swap(outgoing)
        new_shape = jax.ShapeDtypeStruct((total, columns), F32)
        padded = (total + height, columns)
        scratch = [pltpu.VMEM((peers * rows_each + height, columns), F32)]
        if last:
            scratch += [pltpu.VMEM(padded, F32), pltpu.SemaphoreType.DMA((tile_count * bands,))]
        else:
            scratch.append(pltpu.VMEM((peers * rows_each + height, columns), F32))
        sums = max(n for n in (1, 2) if peers % n == 0)
        res = pl.pallas_call(
            functools.partial(update_kernel, bands, tile_rows, height, last),
            out_shape=jax.ShapeDtypeStruct((total, columns), F32)
            if last
            else (jax.ShapeDtypeStruct(padded, F32), rows_shape),
            in_specs=[smem()] * 2 + [vmem(), vmem()],
            out_specs=hbm() if last else (vmem(), vmem()),
            scratch_shapes=scratch + [pltpu.VMEM(padded, F32)] * (sums - 1),
            compiler_params=params(),
            name="update",
        )(update_table, factors, returned, x)
        if last:
            x = res
        else:
            x, outbound = res
            arrived = swap(outbound)
    return (x.reshape(model.shape), others[0])


def solution(mesh):
    both = ("groups", "sky")
    return jax.shard_map(
        body,
        mesh=mesh,
        in_specs=(
            P(both, None, None, None),
            P(both, None, None),
            P(both),
            P(),
            P(both, None),
            P(both),
            P(both, None),
            P(both, None),
            P(both, None),
            P(both, None),
            P(both, None),
            P(both, None),
            P(both),
            P(both),
        ),
        out_specs=(P(both, None, None, None), P(both, None, None)),
        check_vma=False,
    )
```

```python
import functools

import jax
import jax.numpy as jnp
from jax import lax
from jax.experimental import pallas as pl
from jax.experimental.pallas import tpu as pltpu
from jax.sharding import PartitionSpec as P

NPSF = 4
TAPS = 7
ITERS = 2
LANES = 128
HALF = TAPS // 2
F32 = jnp.float32
BF16 = jnp.bfloat16
I32 = jnp.int32
VMEM_BYTES = 24 * 1024 * 1024

smem = lambda: pl.BlockSpec(memory_space=pltpu.SMEM)
vmem = lambda: pl.BlockSpec(memory_space=pltpu.VMEM)
hbm = lambda: pl.BlockSpec(memory_space=pltpu.HBM)


def params(share=1.0):
    return pltpu.CompilerParams(vmem_limit_bytes=int(share * VMEM_BYTES))


SHIFT = 16
PLACE = 13


def low(word):
    return word & ((1 << SHIFT) - 1)


def high(word):
    return lax.shift_right_logical(word, SHIFT)


def aligned(rows):
    return -(-rows // 16) * 16


def first_and_sent(word):
    mask = (1 << PLACE) - 1
    return word & mask, lax.shift_right_logical(word, PLACE) & mask


def pack_slots(begin, count, plane_ref, row_ref, cover_ref, tile_rows, height, rows_each, x_ref, packed_ref):
    capacity = plane_ref.shape[1]

    def peer(d, _):
        at = d * rows_each
        for c in range(capacity):
            first = jnp.maximum(plane_ref[d, c], 0) * tile_rows + row_ref[d, c]
            packed_ref[pl.ds(at, height), :] = x_ref[pl.ds(first, height), :]
            at = at + cover_ref[d, c]
        return 0

    lax.fori_loop(begin, begin + count, peer, 0, unroll=min(4, count))


def bank_rows(taps, height):
    count, width = taps.shape

    def grid(columns):
        return (
            lax.broadcasted_iota(I32, (width, columns), 0),
            lax.broadcasted_iota(I32, (width, columns), 1),
        )

    def select(x, mask):
        parts = []
        for _ in range(3):
            parts.append(x.astype(BF16).astype(F32))
            x = x - parts[-1]
        picked = jnp.dot(
            jnp.concatenate(parts, axis=0).astype(BF16), mask.astype(F32).astype(BF16), preferred_element_type=F32
        )
        return picked[:count] + picked[count : 2 * count] + picked[2 * count :]

    k, l = grid(2 * NPSF * LANES)
    mirror, j, l = l // (NPSF * LANES), l // LANES % NPSF, (l + HALF) % LANES
    i, t = l // height, l % height
    valid = (i < TAPS) & (t < TAPS)
    row_tap = j * TAPS + jnp.where(mirror == 1, t, TAPS - 1 - t)
    col_tap = (NPSF + j) * TAPS + jnp.where(mirror == 1, TAPS - 1 - i, i)
    picked = select(taps, valid & (k == row_tap)) * select(taps, valid & (k == col_tap))
    k, l = grid(NPSF * LANES)
    whole = select(taps, k // TAPS == l // LANES) * select(taps, k // TAPS == NPSF + l // LANES)
    product = picked / (jnp.concatenate([whole, whole], axis=1) * NPSF)
    return [
        sum(product[:, (m * NPSF + j) * LANES : (m * NPSF + j + 1) * LANES] for j in range(NPSF)) for m in range(2)
    ]


def first_send_kernel(
    tile_rows,
    height,
    rows_each,
    plane_in_ref,
    row_in_ref,
    cover_in_ref,
    taps_in_ref,
    model_ref,
    out_ref,
    plane_ref,
    row_ref,
    cover_ref,
    taps_ref,
    x_ref,
    packed_ref,
    bank_ref,
    block_ref,
    sems,
):
    peers = plane_ref.shape[0]
    total = model_ref.shape[0]
    cuts = max(n for n in (1, 2, 4) if total % (16 * n) == 0)
    pairs = [(plane_in_ref, plane_ref), (row_in_ref, row_ref), (cover_in_ref, cover_ref), (taps_in_ref, taps_ref)]
    for n in range(cuts):
        here = pl.ds(n * (total // cuts), total // cuts)
        pairs.append((model_ref.at[here, :], x_ref.at[here, :]))
    loads = [pltpu.make_async_copy(*pair, sems.at[n]) for n, pair in enumerate(pairs)]
    for load in loads:
        load.start()
    bank_ref[...] = jnp.zeros(bank_ref.shape, F32)
    taps_load = loads.pop(3)
    taps_load.wait()
    for m, row in enumerate(bank_rows(taps_ref[...], height)):
        for n in range(taps_ref.shape[0]):
            bank_ref[2 * n + m : 2 * n + m + 1, :] = row[n : n + 1, :]
    bank = bank_ref[...].astype(BF16)
    for load in loads:
        load.wait()
    parts = max(n for n in (1, 2, 4) if peers % n == 0)
    some = peers // parts
    sends = []
    for part in range(parts):
        here = pl.ds(part * some, some)
        pack_slots(part * some, some, plane_ref, row_ref, cover_ref, tile_rows, height, rows_each, x_ref, packed_ref)
        for d in range(part * some, (part + 1) * some):
            block_ref[d, :rows_each, :] = packed_ref[d * rows_each : (d + 1) * rows_each, :].astype(BF16)
            block_ref[d, rows_each:, :] = bank
        sends.append(pltpu.make_async_copy(block_ref.at[here], out_ref.at[here], sems.at[len(pairs) + part]))
        sends[-1].start()
    for send in sends:
        send.wait()


def update_kernel(bands, tile_rows, height, last, table_ref, factor_ref, returned_ref, model_ref, *rest):
    if last:
        new_ref, back_ref, x_ref, saved, *more_refs = rest
    else:
        x_ref, out_ref, back_ref, packed_ref, *more_refs = rest
    peers, rows_each, _ = returned_ref.shape
    capacity = 2 * rows_each // height
    slots = peers * capacity
    total = x_ref.shape[0] - height
    planes = total // tile_rows
    tiles = planes // bands
    x_ref[:total, :] = model_ref[:total, :]
    for ref in more_refs:
        ref[...] = jnp.zeros(ref.shape, F32)
    for d in range(peers):
        back_ref[d * rows_each : (d + 1) * rows_each, :] = returned_ref[d].astype(F32)
    place = lax.broadcasted_iota(I32, (height, LANES), 0)

    sums = [x_ref, *more_refs]

    def some_peers(step, _):
        for c in range(capacity):
            for n, ref in enumerate(sums):
                slot = (step * len(sums) + n) * capacity + c
                word = table_ref[slot]
                first, sent = first_and_sent(word)
                here = pl.ds(first, height)
                cover = lax.shift_right_logical(word, 2 * PLACE)
                piece = jnp.where(place < cover, back_ref[pl.ds(sent, height), :], 0.0)
                ref[here, :] = ref[here, :] - factor_ref[slot] * piece
        return 0

    lax.fori_loop(0, peers // len(sums), some_peers, 0, unroll=2)

    pos = lax.broadcasted_iota(I32, (tile_rows, LANES), 0)
    saves = []
    for p in range(planes):
        inside = (pos >= table_ref[slots + p // bands]) & (pos < table_ref[slots + tiles + p // bands])
        here = slice(p * tile_rows, (p + 1) * tile_rows)
        new = sum((ref[here, :] for ref in more_refs), x_ref[here, :])
        x_ref[here, :] = jnp.where(inside, jnp.maximum(new, 0.0), 0.0)
        if last:
            rows = pl.ds(p * tile_rows, tile_rows)
            saves.append(pltpu.make_async_copy(x_ref.at[rows, :], new_ref.at[rows, :], saved.at[p]))
            saves[-1].start()
    if not last:

        def pack(slot, _):
            first, sent = first_and_sent(table_ref[slot])
            packed_ref[pl.ds(sent, height), :] = x_ref[pl.ds(first, height), :]
            return 0

        lax.fori_loop(0, slots, pack, 0, unroll=64)
        for d in range(peers):
            out_ref[d, :, :] = packed_ref[d * rows_each : (d + 1) * rows_each, :].astype(BF16)
    for save in saves:
        save.wait()


def tables_kernel(
    tile_rows,
    bands,
    height,
    rows_each,
    slot_ref,
    start_ref,
    stop_ref,
    batch_ref,
    plane_ref,
    row_ref,
    cover_ref,
    step_ref,
    lo_ref,
    hi_ref,
    blur_ref,
    update_ref,
    factor_ref,
    length_ref,
    begin_ref,
    scale_ref,
):
    pieces, exposures = slot_ref.shape
    peers, capacity = plane_ref.shape
    slots = peers * capacity

    def clear(s, _):
        length_ref[s] = 0
        return 0

    lax.fori_loop(0, slots, clear, 0, unroll=16)
    for p in range(scale_ref.shape[0]):
        scale_ref[p] = step_ref[p % bands]
    tiles = lo_ref.shape[0]
    for t in range(tiles):
        update_ref[slots + t] = lo_ref[t]
        update_ref[slots + tiles + t] = hi_ref[t]

    def measure(e, _):
        for k in range(pieces):
            s = slot_ref[k, e]
            s = jnp.where(s >= 0, s, slots)
            length_ref[s] = stop_ref[k, e] - start_ref[k, e]
        return 0

    lax.fori_loop(0, exposures, measure, 0, unroll=8)

    def lay(o, _):
        at = sent = o * rows_each
        for c in range(capacity):
            s = o * capacity + c
            begin_ref[s] = at
            at = at + length_ref[s]
            p = jnp.maximum(plane_ref[o, c], 0)
            cover = cover_ref[o, c]
            update_ref[s] = (p * tile_rows + row_ref[o, c]) | (sent << PLACE) | (cover << 2 * PLACE)
            factor_ref[s] = scale_ref[p]
            sent = sent + cover
        return 0

    lax.fori_loop(0, peers, lay, 0)

    def point(e, _):
        for k in range(pieces):
            s = slot_ref[k, e]
            live = s >= 0
            start = start_ref[k, e]
            begin = jnp.where(live, height + begin_ref[jnp.maximum(s, 0)] - start, 0)
            above = batch_ref[e] if k == 0 else jnp.where(live, start, height)
            blur_ref[k * exposures + e] = begin | (above << SHIFT)
        return 0

    lax.fori_loop(0, exposures, point, 0, unroll=8)


def blur_kernel(
    height,
    pieces,
    batches_each,
    last,
    table_ref,
    weight_ref,
    arrived_ref,
    seen_ref,
    *rest,
):
    if last:
        blur_ref, back_ref, out_ref, residual_out_ref, rows_ref, packed_ref, held_ref, residual_ref, sent = rest
    else:
        out_ref, blur_ref, back_ref, rows_ref, packed_ref, held_ref, bank_ref = rest
    peers, rows_each, _ = out_ref.shape
    exposures = seen_ref.shape[0]
    place = lax.broadcasted_iota(I32, (height, LANES), 0)
    lane = lax.broadcasted_iota(I32, (height, LANES), 1)
    for o in range(peers):
        at = height + o * rows_each
        rows_ref[at : at + rows_each, :] = arrived_ref[o, :rows_each, :].astype(F32)
    if not last:
        extra = arrived_ref.shape[1] - rows_each
        for o in range(peers):
            bank_ref[o * extra : (o + 1) * extra, :] = arrived_ref[o, rows_each:, :].astype(F32)
        gap = lane % height - place
        near = (gap <= HALF) & (gap >= -HALF) & (lane < TAPS * height)

        def operators(o, _):
            for n in range(batches_each):
                for m, ref in enumerate((blur_ref, back_ref)):
                    taps = jnp.broadcast_to(bank_ref[pl.ds(o * extra + 2 * n + m, 1), :], (height, LANES))
                    ref[o * batches_each + n] = jnp.where(
                        near, pltpu.roll(taps, 0, 1, stride=1, stride_axis=0), 0.0
                    ).astype(BF16)
            return 0

        lax.fori_loop(0, peers, operators, 0, unroll=min(16, peers))

    def shifted(x):
        parts = []
        for v in range(-HALF, HALF + 1):
            moved = x if v == 0 else pltpu.roll(x, v % LANES, 1)
            parts.append(jnp.where((lane >= v) & (lane < LANES + v), moved, jnp.zeros((), BF16)))
        parts.append(jnp.zeros((LANES - TAPS * height, LANES), BF16))
        return jnp.concatenate(parts, axis=0)

    def blur(e):
        stamp = rows_ref[pl.ds(low(table_ref[e]), height), :]
        for k in range(1, pieces):
            word = table_ref[k * exposures + e]
            stamp = jnp.where(place >= high(word), rows_ref[pl.ds(low(word), height), :], stamp)
        predicted = jnp.dot(
            blur_ref[high(table_ref[e])], shifted(stamp.astype(BF16)), preferred_element_type=F32
        )
        residual = weight_ref[e] * (predicted - seen_ref[e].astype(F32))
        if last:
            residual_ref[e] = residual
        held_ref[e * height : (e + 1) * height, :] = residual.astype(BF16)

    def correlate(e):
        result = jnp.dot(
            back_ref[high(table_ref[e])],
            shifted(held_ref[e * height : (e + 1) * height, :]),
            preferred_element_type=F32,
        )
        words = [table_ref[k * exposures + e] for k in range(pieces)]
        for k, word in enumerate(words):
            mask = place >= high(word) if k else None
            if k + 1 < pieces:
                before = place < high(words[k + 1])
                mask = before if mask is None else mask & before
            pltpu.store(packed_ref.at[pl.ds(low(word), height), :], result, mask=mask)

    for e in range(exposures):
        blur(e)
    sends = []
    for e in range(exposures):
        if last and e == exposures // 2:
            parts = sent.shape[0]
            for n in range(parts):
                here = pl.ds(n * (exposures // parts), exposures // parts)
                sends.append(pltpu.make_async_copy(residual_ref.at[here], residual_out_ref.at[here], sent.at[n]))
                sends[-1].start()
        correlate(e)
    for o in range(peers):
        at = height + o * rows_each
        out_ref[o, :, :] = packed_ref[at : at + rows_each, :].astype(BF16)
    for send in sends:
        send.wait()


def body(
    model,
    exposures,
    inv_var,
    step_size,
    psf_taps,
    exp_batch,
    send_plane,
    send_row,
    send_cover,
    use_slot,
    use_start,
    use_stop,
    foot_lo,
    foot_hi,
):
    tile_count, bands, tile_rows, columns = model.shape
    count, height, _ = exposures.shape
    peers, capacity = send_plane.shape
    pieces = use_slot.shape[1]
    total = tile_count * bands * tile_rows
    rows_each = capacity * height // 2
    batches_each = psf_taps.shape[0]
    extra = aligned(batches_each * 2)
    block = rows_each + extra
    assert columns == LANES and rows_each % extra == 0 and TAPS * height <= LANES - HALF
    x = model.reshape(total, columns)

    def swap(a):
        return lax.all_to_all(a, "sky", split_axis=0, concat_axis=0, tiled=True)

    outbound = pl.pallas_call(
        functools.partial(first_send_kernel, tile_rows, height, rows_each),
        out_shape=jax.ShapeDtypeStruct((peers, block, columns), BF16),
        in_specs=[hbm()] * 5,
        out_specs=hbm(),
        scratch_shapes=[
            pltpu.SMEM(send_plane.shape, I32),
            pltpu.SMEM(send_row.shape, I32),
            pltpu.SMEM(send_cover.shape, I32),
            pltpu.VMEM(psf_taps.shape, F32),
            pltpu.VMEM((total + height, columns), F32),
            pltpu.VMEM((peers * rows_each + height, columns), F32),
            pltpu.VMEM((extra, columns), F32),
            pltpu.VMEM((peers, block, columns), BF16),
            pltpu.SemaphoreType.DMA((12,)),
        ],
        compiler_params=params(2.5),
        name="first_send",
    )(send_plane, send_row, send_cover, psf_taps, x)
    arrived = swap(outbound)
    slots = peers * capacity
    assert max(total, peers * rows_each) < 1 << PLACE and height < 1 << (31 - 2 * PLACE)
    assert max(peers * rows_each + 2 * height, psf_taps.shape[0] * peers) < 1 << (SHIFT - 1)
    blur_table, update_table, factors = pl.pallas_call(
        functools.partial(tables_kernel, tile_rows, bands, height, rows_each),
        out_shape=(
            jax.ShapeDtypeStruct((pieces * count,), I32),
            jax.ShapeDtypeStruct((slots + 2 * tile_count,), I32),
            jax.ShapeDtypeStruct((slots,), F32),
        ),
        in_specs=[smem()] * 10,
        out_specs=(smem(), smem(), smem()),
        scratch_shapes=[
            pltpu.SMEM((slots + 1,), I32),
            pltpu.SMEM((slots,), I32),
            pltpu.SMEM((tile_count * bands,), F32),
        ],
        compiler_params=params(),
        cost_estimate=pl.CostEstimate(flops=4_000_000, bytes_accessed=8_000_000, transcendentals=0),
        name="tables",
    )(
        use_slot.T,
        use_start.T,
        use_stop.T,
        exp_batch,
        send_plane,
        send_row,
        send_cover,
        step_size,
        foot_lo,
        foot_hi,
    )
    operators = []
    for sweep in range(ITERS):
        last = sweep == ITERS - 1
        rows_shape = jax.ShapeDtypeStruct((peers, rows_each, columns), BF16)
        scratch = [
            pltpu.VMEM((peers * rows_each + 2 * height, columns), F32),
            pltpu.VMEM((peers * rows_each + 2 * height, columns), F32),
            pltpu.VMEM((count * height, columns), BF16),
        ]
        if last:
            copies = max(n for n in (1, 2, 4) if count % n == 0)
            scratch += [pltpu.VMEM(exposures.shape, F32), pltpu.SemaphoreType.DMA((copies,))]
            out_shape, out_specs = (rows_shape, jax.ShapeDtypeStruct(exposures.shape, F32)), (vmem(), hbm())
        else:
            scratch.append(pltpu.VMEM((peers * extra, columns), F32))
            operator_shape = jax.ShapeDtypeStruct((peers * batches_each, height, columns), BF16)
            out_shape, out_specs = (rows_shape, operator_shape, operator_shape), (vmem(),) * 3
        outgoing, *others = pl.pallas_call(
            functools.partial(blur_kernel, height, pieces, batches_each, last),
            out_shape=out_shape,
            in_specs=[smem()] * 2 + [vmem()] * (4 if last else 2),
            out_specs=out_specs,
            scratch_shapes=scratch,
            compiler_params=params(),
            name="blur",
        )(blur_table, inv_var, arrived, exposures, *operators)
        operators = [] if last else others
        returned = swap(outgoing)
        new_shape = jax.ShapeDtypeStruct((total, columns), F32)
        padded = (total + height, columns)
        scratch = [pltpu.VMEM((peers * rows_each + height, columns), F32)]
        if last:
            scratch += [pltpu.VMEM(padded, F32), pltpu.SemaphoreType.DMA((tile_count * bands,))]
        else:
            scratch.append(pltpu.VMEM((peers * rows_each + height, columns), F32))
        sums = max(n for n in (1, 2) if peers % n == 0)
        res = pl.pallas_call(
            functools.partial(update_kernel, bands, tile_rows, height, last),
            out_shape=jax.ShapeDtypeStruct((total, columns), F32)
            if last
            else (jax.ShapeDtypeStruct(padded, F32), rows_shape),
            in_specs=[smem()] * 2 + [vmem(), vmem()],
            out_specs=hbm() if last else (vmem(), vmem()),
            scratch_shapes=scratch + [pltpu.VMEM(padded, F32)] * (sums - 1),
            compiler_params=params(),
            name="update",
        )(update_table, factors, returned, x)
        if last:
            x = res
        else:
            x, outbound = res
            arrived = swap(outbound)
    return (x.reshape(model.shape), others[0])


def solution(mesh):
    both = ("groups", "sky")
    return jax.shard_map(
        body,
        mesh=mesh,
        in_specs=(
            P(both, None, None, None),
            P(both, None, None),
            P(both),
            P(),
            P(both, None),
            P(both),
            P(both, None),
            P(both, None),
            P(both, None),
            P(both, None),
            P(both, None),
            P(both, None),
            P(both),
            P(both),
        ),
        out_specs=(P(both, None, None, None), P(both, None, None)),
        check_vma=False,
    )
```

```python
import functools

import jax
import jax.numpy as jnp
from jax import lax
from jax.experimental import pallas as pl
from jax.experimental.pallas import tpu as pltpu
from jax.sharding import PartitionSpec as P

NPSF = 4
TAPS = 7
ITERS = 2
LANES = 128
HALF = TAPS // 2
F32 = jnp.float32
BF16 = jnp.bfloat16
I32 = jnp.int32
VMEM_BYTES = 24 * 1024 * 1024

smem = lambda: pl.BlockSpec(memory_space=pltpu.SMEM)
vmem = lambda: pl.BlockSpec(memory_space=pltpu.VMEM)
hbm = lambda: pl.BlockSpec(memory_space=pltpu.HBM)


def params(share=1.0):
    return pltpu.CompilerParams(vmem_limit_bytes=int(share * VMEM_BYTES))


SHIFT = 16
PLACE = 13


def low(word):
    return word & ((1 << SHIFT) - 1)


def high(word):
    return lax.shift_right_logical(word, SHIFT)


def aligned(rows):
    return -(-rows // 16) * 16


def first_and_sent(word):
    mask = (1 << PLACE) - 1
    return word & mask, lax.shift_right_logical(word, PLACE) & mask


def pack_slots(begin, count, plane_ref, row_ref, cover_ref, tile_rows, height, rows_each, x_ref, packed_ref):
    capacity = plane_ref.shape[1]

    def peer(d, _):
        at = d * rows_each
        for c in range(capacity):
            first = jnp.maximum(plane_ref[d, c], 0) * tile_rows + row_ref[d, c]
            packed_ref[pl.ds(at, height), :] = x_ref[pl.ds(first, height), :]
            at = at + cover_ref[d, c]
        return 0

    lax.fori_loop(begin, begin + count, peer, 0, unroll=min(4, count))


def bank_rows(taps, height):
    count, width = taps.shape

    def grid(columns):
        return (
            lax.broadcasted_iota(I32, (width, columns), 0),
            lax.broadcasted_iota(I32, (width, columns), 1),
        )

    def select(x, mask):
        parts = []
        for _ in range(3):
            parts.append(x.astype(BF16).astype(F32))
            x = x - parts[-1]
        picked = jnp.dot(
            jnp.concatenate(parts, axis=0).astype(BF16), mask.astype(F32).astype(BF16), preferred_element_type=F32
        )
        return picked[:count] + picked[count : 2 * count] + picked[2 * count :]

    k, l = grid(2 * NPSF * LANES)
    mirror, j, l = l // (NPSF * LANES), l // LANES % NPSF, (l + HALF) % LANES
    i, t = l // height, l % height
    valid = (i < TAPS) & (t < TAPS)
    row_tap = j * TAPS + jnp.where(mirror == 1, t, TAPS - 1 - t)
    col_tap = (NPSF + j) * TAPS + jnp.where(mirror == 1, TAPS - 1 - i, i)
    picked = select(taps, valid & (k == row_tap)) * select(taps, valid & (k == col_tap))
    k, l = grid(NPSF * LANES)
    whole = select(taps, k // TAPS == l // LANES) * select(taps, k // TAPS == NPSF + l // LANES)
    product = picked / (jnp.concatenate([whole, whole], axis=1) * NPSF)
    return [
        sum(product[:, (m * NPSF + j) * LANES : (m * NPSF + j + 1) * LANES] for j in range(NPSF)) for m in range(2)
    ]


def first_send_kernel(
    tile_rows,
    height,
    rows_each,
    plane_in_ref,
    row_in_ref,
    cover_in_ref,
    taps_in_ref,
    model_ref,
    out_ref,
    plane_ref,
    row_ref,
    cover_ref,
    taps_ref,
    x_ref,
    packed_ref,
    bank_ref,
    block_ref,
    sems,
):
    peers = plane_ref.shape[0]
    total = model_ref.shape[0]
    cuts = max(n for n in (1, 2, 4) if total % (16 * n) == 0)
    pairs = [(plane_in_ref, plane_ref), (row_in_ref, row_ref), (cover_in_ref, cover_ref), (taps_in_ref, taps_ref)]
    for n in range(cuts):
        here = pl.ds(n * (total // cuts), total // cuts)
        pairs.append((model_ref.at[here, :], x_ref.at[here, :]))
    loads = [pltpu.make_async_copy(*pair, sems.at[n]) for n, pair in enumerate(pairs)]
    for load in loads:
        load.start()
    bank_ref[...] = jnp.zeros(bank_ref.shape, F32)
    taps_load = loads.pop(3)
    taps_load.wait()
    for m, row in enumerate(bank_rows(taps_ref[...], height)):
        for n in range(taps_ref.shape[0]):
            bank_ref[2 * n + m : 2 * n + m + 1, :] = row[n : n + 1, :]
    bank = bank_ref[...].astype(BF16)
    for load in loads:
        load.wait()
    parts = max(n for n in (1, 2, 4) if peers % n == 0)
    some = peers // parts
    sends = []
    for part in range(parts):
        here = pl.ds(part * some, some)
        pack_slots(part * some, some, plane_ref, row_ref, cover_ref, tile_rows, height, rows_each, x_ref, packed_ref)
        for d in range(part * some, (part + 1) * some):
            block_ref[d, :rows_each, :] = packed_ref[d * rows_each : (d + 1) * rows_each, :].astype(BF16)
            block_ref[d, rows_each:, :] = bank
        sends.append(pltpu.make_async_copy(block_ref.at[here], out_ref.at[here], sems.at[len(pairs) + part]))
        sends[-1].start()
    for copy in sends:
        copy.wait()


def update_kernel(bands, tile_rows, height, last, table_ref, factor_ref, returned_ref, model_ref, *rest):
    if last:
        new_ref, back_ref, x_ref, saved, *more_refs = rest
    else:
        x_ref, out_ref, back_ref, packed_ref, *more_refs = rest
    peers, rows_each, _ = returned_ref.shape
    capacity = 2 * rows_each // height
    slots = peers * capacity
    total = x_ref.shape[0] - height
    planes = total // tile_rows
    tiles = planes // bands
    x_ref[:total, :] = model_ref[:total, :]
    for ref in more_refs:
        ref[...] = jnp.zeros(ref.shape, F32)
    for d in range(peers):
        back_ref[d * rows_each : (d + 1) * rows_each, :] = returned_ref[d].astype(F32)
    place = lax.broadcasted_iota(I32, (height, LANES), 0)

    sums = [x_ref, *more_refs]

    def some_peers(step, _):
        for c in range(capacity):
            for n, ref in enumerate(sums):
                slot = (step * len(sums) + n) * capacity + c
                word = table_ref[slot]
                first, sent = first_and_sent(word)
                here = pl.ds(first, height)
                cover = lax.shift_right_logical(word, 2 * PLACE)
                piece = jnp.where(place < cover, back_ref[pl.ds(sent, height), :], 0.0)
                ref[here, :] = ref[here, :] - factor_ref[slot] * piece
        return 0

    lax.fori_loop(0, peers // len(sums), some_peers, 0, unroll=2)

    pos = lax.broadcasted_iota(I32, (tile_rows, LANES), 0)
    saves = []
    for p in range(planes):
        inside = (pos >= table_ref[slots + p // bands]) & (pos < table_ref[slots + tiles + p // bands])
        here = slice(p * tile_rows, (p + 1) * tile_rows)
        new = sum((ref[here, :] for ref in more_refs), x_ref[here, :])
        x_ref[here, :] = jnp.where(inside, jnp.maximum(new, 0.0), 0.0)
        if last:
            rows = pl.ds(p * tile_rows, tile_rows)
            saves.append(pltpu.make_async_copy(x_ref.at[rows, :], new_ref.at[rows, :], saved.at[p]))
            saves[-1].start()
    if not last:

        def pack(slot, _):
            first, sent = first_and_sent(table_ref[slot])
            packed_ref[pl.ds(sent, height), :] = x_ref[pl.ds(first, height), :]
            return 0

        lax.fori_loop(0, slots, pack, 0, unroll=64)
        for d in range(peers):
            out_ref[d, :, :] = packed_ref[d * rows_each : (d + 1) * rows_each, :].astype(BF16)
    for save in saves:
        save.wait()


def tables_kernel(
    tile_rows,
    bands,
    height,
    rows_each,
    slot_ref,
    start_ref,
    stop_ref,
    batch_ref,
    plane_ref,
    row_ref,
    cover_ref,
    step_ref,
    lo_ref,
    hi_ref,
    blur_ref,
    update_ref,
    factor_ref,
    length_ref,
    begin_ref,
    scale_ref,
):
    pieces, exposures = slot_ref.shape
    peers, capacity = plane_ref.shape
    slots = peers * capacity

    def clear(s, _):
        length_ref[s] = 0
        return 0

    lax.fori_loop(0, slots, clear, 0, unroll=16)
    for p in range(scale_ref.shape[0]):
        scale_ref[p] = step_ref[p % bands]
    tiles = lo_ref.shape[0]
    for t in range(tiles):
        update_ref[slots + t] = lo_ref[t]
        update_ref[slots + tiles + t] = hi_ref[t]

    def measure(e, _):
        for k in range(pieces):
            s = slot_ref[k, e]
            s = jnp.where(s >= 0, s, slots)
            length_ref[s] = stop_ref[k, e] - start_ref[k, e]
        return 0

    lax.fori_loop(0, exposures, measure, 0, unroll=8)

    def lay(o, _):
        at = sent = o * rows_each
        for c in range(capacity):
            s = o * capacity + c
            begin_ref[s] = at
            at = at + length_ref[s]
            p = jnp.maximum(plane_ref[o, c], 0)
            cover = cover_ref[o, c]
            update_ref[s] = (p * tile_rows + row_ref[o, c]) | (sent << PLACE) | (cover << 2 * PLACE)
            factor_ref[s] = scale_ref[p]
            sent = sent + cover
        return 0

    lax.fori_loop(0, peers, lay, 0)

    def point(e, _):
        for k in range(pieces):
            s = slot_ref[k, e]
            live = s >= 0
            start = start_ref[k, e]
            begin = jnp.where(live, height + begin_ref[jnp.maximum(s, 0)] - start, 0)
            above = batch_ref[e] if k == 0 else jnp.where(live, start, height)
            blur_ref[k * exposures + e] = begin | (above << SHIFT)
        return 0

    lax.fori_loop(0, exposures, point, 0, unroll=8)


def blur_kernel(
    height,
    pieces,
    batches_each,
    last,
    table_ref,
    weight_ref,
    arrived_ref,
    seen_ref,
    *rest,
):
    if last:
        blur_ref, back_ref, out_ref, residual_out_ref, rows_ref, packed_ref, held_ref, residual_ref, sent = rest
    else:
        out_ref, blur_ref, back_ref, rows_ref, packed_ref, held_ref, bank_ref = rest
    peers, rows_each, _ = out_ref.shape
    exposures = seen_ref.shape[0]
    place = lax.broadcasted_iota(I32, (height, LANES), 0)
    lane = lax.broadcasted_iota(I32, (height, LANES), 1)
    for o in range(peers):
        at = height + o * rows_each
        rows_ref[at : at + rows_each, :] = arrived_ref[o, :rows_each, :].astype(F32)
    if not last:
        extra = arrived_ref.shape[1] - rows_each
        for o in range(peers):
            bank_ref[o * extra : (o + 1) * extra, :] = arrived_ref[o, rows_each:, :].astype(F32)
        gap = lane % height - place
        near = (gap <= HALF) & (gap >= -HALF) & (lane < TAPS * height)

        def operators(o, _):
            for n in range(batches_each):
                for m, ref in enumerate((blur_ref, back_ref)):
                    taps = jnp.broadcast_to(bank_ref[pl.ds(o * extra + 2 * n + m, 1), :], (height, LANES))
                    ref[o * batches_each + n] = jnp.where(
                        near, pltpu.roll(taps, 0, 1, stride=1, stride_axis=0), 0.0
                    ).astype(BF16)
            return 0

        lax.fori_loop(0, peers, operators, 0, unroll=min(16, peers))

    def shifted(x):
        parts = []
        for v in range(-HALF, HALF + 1):
            moved = x if v == 0 else pltpu.roll(x, v % LANES, 1)
            parts.append(jnp.where((lane >= v) & (lane < LANES + v), moved, jnp.zeros((), BF16)))
        parts.append(jnp.zeros((LANES - TAPS * height, LANES), BF16))
        return jnp.concatenate(parts, axis=0)

    def blur(e):
        stamp = rows_ref[pl.ds(low(table_ref[e]), height), :]
        for k in range(1, pieces):
            word = table_ref[k * exposures + e]
            stamp = jnp.where(place >= high(word), rows_ref[pl.ds(low(word), height), :], stamp)
        predicted = jnp.dot(
            blur_ref[high(table_ref[e])], shifted(stamp.astype(BF16)), preferred_element_type=F32
        )
        residual = weight_ref[e] * (predicted - seen_ref[e].astype(F32))
        if last:
            residual_ref[e] = residual
        held_ref[e * height : (e + 1) * height, :] = residual.astype(BF16)

    def correlate(e):
        result = jnp.dot(
            back_ref[high(table_ref[e])],
            shifted(held_ref[e * height : (e + 1) * height, :]),
            preferred_element_type=F32,
        )
        words = [table_ref[k * exposures + e] for k in range(pieces)]
        for k, word in enumerate(words):
            mask = place >= high(word) if k else None
            if k + 1 < pieces:
                before = place < high(words[k + 1])
                mask = before if mask is None else mask & before
            pltpu.store(packed_ref.at[pl.ds(low(word), height), :], result, mask=mask)

    quarter = exposures // 4
    sends = []

    def send(n):
        here = pl.ds(n * quarter, quarter)
        sends.append(pltpu.make_async_copy(residual_ref.at[here], residual_out_ref.at[here], sent.at[n]))
        sends[-1].start()

    for e in range(3 * quarter):
        blur(e)
    for e in range(quarter):
        correlate(e)
    if last:
        for n in range(3):
            send(n)
    for e in range(3 * quarter, exposures):
        blur(e)
    for e in range(quarter, exposures):
        correlate(e)
    if last:
        send(3)
    for o in range(peers):
        at = height + o * rows_each
        out_ref[o, :, :] = packed_ref[at : at + rows_each, :].astype(BF16)
    for copy in sends:
        copy.wait()


def body(
    model,
    exposures,
    inv_var,
    step_size,
    psf_taps,
    exp_batch,
    send_plane,
    send_row,
    send_cover,
    use_slot,
    use_start,
    use_stop,
    foot_lo,
    foot_hi,
):
    tile_count, bands, tile_rows, columns = model.shape
    count, height, _ = exposures.shape
    peers, capacity = send_plane.shape
    pieces = use_slot.shape[1]
    total = tile_count * bands * tile_rows
    rows_each = capacity * height // 2
    batches_each = psf_taps.shape[0]
    extra = aligned(batches_each * 2)
    block = rows_each + extra
    assert columns == LANES and rows_each % extra == 0 and TAPS * height <= LANES - HALF and count % 4 == 0
    x = model.reshape(total, columns)

    def swap(a):
        return lax.all_to_all(a, "sky", split_axis=0, concat_axis=0, tiled=True)

    outbound = pl.pallas_call(
        functools.partial(first_send_kernel, tile_rows, height, rows_each),
        out_shape=jax.ShapeDtypeStruct((peers, block, columns), BF16),
        in_specs=[hbm()] * 5,
        out_specs=hbm(),
        scratch_shapes=[
            pltpu.SMEM(send_plane.shape, I32),
            pltpu.SMEM(send_row.shape, I32),
            pltpu.SMEM(send_cover.shape, I32),
            pltpu.VMEM(psf_taps.shape, F32),
            pltpu.VMEM((total + height, columns), F32),
            pltpu.VMEM((peers * rows_each + height, columns), F32),
            pltpu.VMEM((extra, columns), F32),
            pltpu.VMEM((peers, block, columns), BF16),
            pltpu.SemaphoreType.DMA((12,)),
        ],
        compiler_params=params(2.5),
        name="first_send",
    )(send_plane, send_row, send_cover, psf_taps, x)
    arrived = swap(outbound)
    slots = peers * capacity
    assert max(total, peers * rows_each) < 1 << PLACE and height < 1 << (31 - 2 * PLACE)
    assert max(peers * rows_each + 2 * height, psf_taps.shape[0] * peers) < 1 << (SHIFT - 1)
    blur_table, update_table, factors = pl.pallas_call(
        functools.partial(tables_kernel, tile_rows, bands, height, rows_each),
        out_shape=(
            jax.ShapeDtypeStruct((pieces * count,), I32),
            jax.ShapeDtypeStruct((slots + 2 * tile_count,), I32),
            jax.ShapeDtypeStruct((slots,), F32),
        ),
        in_specs=[smem()] * 10,
        out_specs=(smem(), smem(), smem()),
        scratch_shapes=[
            pltpu.SMEM((slots + 1,), I32),
            pltpu.SMEM((slots,), I32),
            pltpu.SMEM((tile_count * bands,), F32),
        ],
        compiler_params=params(),
        cost_estimate=pl.CostEstimate(flops=4_000_000, bytes_accessed=8_000_000, transcendentals=0),
        name="tables",
    )(
        use_slot.T,
        use_start.T,
        use_stop.T,
        exp_batch,
        send_plane,
        send_row,
        send_cover,
        step_size,
        foot_lo,
        foot_hi,
    )
    operators = []
    for sweep in range(ITERS):
        last = sweep == ITERS - 1
        rows_shape = jax.ShapeDtypeStruct((peers, rows_each, columns), BF16)
        scratch = [
            pltpu.VMEM((peers * rows_each + 2 * height, columns), F32),
            pltpu.VMEM((peers * rows_each + 2 * height, columns), F32),
            pltpu.VMEM((count * height, columns), BF16),
        ]
        if last:
            scratch += [pltpu.VMEM(exposures.shape, F32), pltpu.SemaphoreType.DMA((4,))]
            out_shape, out_specs = (rows_shape, jax.ShapeDtypeStruct(exposures.shape, F32)), (vmem(), hbm())
        else:
            scratch.append(pltpu.VMEM((peers * extra, columns), F32))
            operator_shape = jax.ShapeDtypeStruct((peers * batches_each, height, columns), BF16)
            out_shape, out_specs = (rows_shape, operator_shape, operator_shape), (vmem(),) * 3
        outgoing, *others = pl.pallas_call(
            functools.partial(blur_kernel, height, pieces, batches_each, last),
            out_shape=out_shape,
            in_specs=[smem()] * 2 + [vmem()] * (4 if last else 2),
            out_specs=out_specs,
            scratch_shapes=scratch,
            compiler_params=params(),
            name="blur",
        )(blur_table, inv_var, arrived, exposures, *operators)
        operators = [] if last else others
        returned = swap(outgoing)
        new_shape = jax.ShapeDtypeStruct((total, columns), F32)
        padded = (total + height, columns)
        scratch = [pltpu.VMEM((peers * rows_each + height, columns), F32)]
        if last:
            scratch += [pltpu.VMEM(padded, F32), pltpu.SemaphoreType.DMA((tile_count * bands,))]
        else:
            scratch.append(pltpu.VMEM((peers * rows_each + height, columns), F32))
        sums = max(n for n in (1, 2) if peers % n == 0)
        res = pl.pallas_call(
            functools.partial(update_kernel, bands, tile_rows, height, last),
            out_shape=jax.ShapeDtypeStruct((total, columns), F32)
            if last
            else (jax.ShapeDtypeStruct(padded, F32), rows_shape),
            in_specs=[smem()] * 2 + [vmem(), vmem()],
            out_specs=hbm() if last else (vmem(), vmem()),
            scratch_shapes=scratch + [pltpu.VMEM(padded, F32)] * (sums - 1),
            compiler_params=params(),
            name="update",
        )(update_table, factors, returned, x)
        if last:
            x = res
        else:
            x, outbound = res
            arrived = swap(outbound)
    return (x.reshape(model.shape), others[0])


def solution(mesh):
    both = ("groups", "sky")
    return jax.shard_map(
        body,
        mesh=mesh,
        in_specs=(
            P(both, None, None, None),
            P(both, None, None),
            P(both),
            P(),
            P(both, None),
            P(both),
            P(both, None),
            P(both, None),
            P(both, None),
            P(both, None),
            P(both, None),
            P(both, None),
            P(both),
            P(both),
        ),
        out_specs=(P(both, None, None, None), P(both, None, None)),
        check_vma=False,
    )
```

```python
import functools

import jax
import jax.numpy as jnp
from jax import lax
from jax.experimental import pallas as pl
from jax.experimental.pallas import tpu as pltpu
from jax.sharding import PartitionSpec as P

NPSF = 4
TAPS = 7
ITERS = 2
LANES = 128
HALF = TAPS // 2
F32 = jnp.float32
BF16 = jnp.bfloat16
I32 = jnp.int32
VMEM_BYTES = 24 * 1024 * 1024

smem = lambda: pl.BlockSpec(memory_space=pltpu.SMEM)
vmem = lambda: pl.BlockSpec(memory_space=pltpu.VMEM)
hbm = lambda: pl.BlockSpec(memory_space=pltpu.HBM)


def params(share=1.0):
    return pltpu.CompilerParams(vmem_limit_bytes=int(share * VMEM_BYTES))


SHIFT = 16
PLACE = 13


def low(word):
    return word & ((1 << SHIFT) - 1)


def high(word):
    return lax.shift_right_logical(word, SHIFT)


def aligned(rows):
    return -(-rows // 16) * 16


def first_and_sent(word):
    mask = (1 << PLACE) - 1
    return word & mask, lax.shift_right_logical(word, PLACE) & mask


def pack_slots(begin, count, plane_ref, row_ref, cover_ref, tile_rows, height, rows_each, x_ref, packed_ref):
    capacity = plane_ref.shape[1]

    def peer(d, _):
        at = d * rows_each
        for c in range(capacity):
            first = jnp.maximum(plane_ref[d, c], 0) * tile_rows + row_ref[d, c]
            packed_ref[pl.ds(at, height), :] = x_ref[pl.ds(first, height), :]
            at = at + cover_ref[d, c]
        return 0

    lax.fori_loop(begin, begin + count, peer, 0, unroll=min(4, count))


def bank_rows(taps, height):
    count, width = taps.shape

    def grid(columns):
        return (
            lax.broadcasted_iota(I32, (width, columns), 0),
            lax.broadcasted_iota(I32, (width, columns), 1),
        )

    def select(x, mask):
        parts = []
        for _ in range(3):
            parts.append(x.astype(BF16).astype(F32))
            x = x - parts[-1]
        picked = jnp.dot(
            jnp.concatenate(parts, axis=0).astype(BF16), mask.astype(F32).astype(BF16), preferred_element_type=F32
        )
        return picked[:count] + picked[count : 2 * count] + picked[2 * count :]

    k, l = grid(2 * NPSF * LANES)
    mirror, j, l = l // (NPSF * LANES), l // LANES % NPSF, (l + HALF) % LANES
    i, t = l // height, l % height
    valid = (i < TAPS) & (t < TAPS)
    row_tap = j * TAPS + jnp.where(mirror == 1, t, TAPS - 1 - t)
    col_tap = (NPSF + j) * TAPS + jnp.where(mirror == 1, TAPS - 1 - i, i)
    picked = select(taps, valid & (k == row_tap)) * select(taps, valid & (k == col_tap))
    k, l = grid(NPSF * LANES)
    whole = select(taps, k // TAPS == l // LANES) * select(taps, k // TAPS == NPSF + l // LANES)
    product = picked / (jnp.concatenate([whole, whole], axis=1) * NPSF)
    return [
        sum(product[:, (m * NPSF + j) * LANES : (m * NPSF + j + 1) * LANES] for j in range(NPSF)) for m in range(2)
    ]


def first_send_kernel(
    tile_rows,
    height,
    rows_each,
    plane_in_ref,
    row_in_ref,
    cover_in_ref,
    taps_in_ref,
    model_ref,
    out_ref,
    plane_ref,
    row_ref,
    cover_ref,
    taps_ref,
    x_ref,
    packed_ref,
    bank_ref,
    block_ref,
    sems,
):
    peers = plane_ref.shape[0]
    total = model_ref.shape[0]
    cuts = max(n for n in (1, 2, 4) if total % (16 * n) == 0)
    pairs = [(plane_in_ref, plane_ref), (row_in_ref, row_ref), (cover_in_ref, cover_ref), (taps_in_ref, taps_ref)]
    for n in range(cuts):
        here = pl.ds(n * (total // cuts), total // cuts)
        pairs.append((model_ref.at[here, :], x_ref.at[here, :]))
    loads = [pltpu.make_async_copy(*pair, sems.at[n]) for n, pair in enumerate(pairs)]
    for load in loads:
        load.start()
    bank_ref[...] = jnp.zeros(bank_ref.shape, F32)
    taps_load = loads.pop(3)
    taps_load.wait()
    for m, row in enumerate(bank_rows(taps_ref[...], height)):
        for n in range(taps_ref.shape[0]):
            bank_ref[2 * n + m : 2 * n + m + 1, :] = row[n : n + 1, :]
    bank = bank_ref[...].astype(BF16)
    for load in loads:
        load.wait()
    parts = max(n for n in (1, 2, 4) if peers % n == 0)
    some = peers // parts
    sends = []
    for part in range(parts):
        here = pl.ds(part * some, some)
        pack_slots(part * some, some, plane_ref, row_ref, cover_ref, tile_rows, height, rows_each, x_ref, packed_ref)
        for d in range(part * some, (part + 1) * some):
            block_ref[d, :rows_each, :] = packed_ref[d * rows_each : (d + 1) * rows_each, :].astype(BF16)
            block_ref[d, rows_each:, :] = bank
        sends.append(pltpu.make_async_copy(block_ref.at[here], out_ref.at[here], sems.at[len(pairs) + part]))
        sends[-1].start()
    for copy in sends:
        copy.wait()


def update_kernel(bands, tile_rows, height, last, table_ref, factor_ref, returned_ref, model_ref, *rest):
    if last:
        new_ref, back_ref, x_ref, saved, *more_refs = rest
    else:
        x_ref, out_ref, back_ref, packed_ref, *more_refs = rest
    peers, rows_each, _ = returned_ref.shape
    capacity = 2 * rows_each // height
    slots = peers * capacity
    total = x_ref.shape[0] - height
    planes = total // tile_rows
    tiles = planes // bands
    x_ref[:total, :] = model_ref[:total, :]
    for ref in more_refs:
        ref[...] = jnp.zeros(ref.shape, F32)
    for d in range(peers):
        back_ref[d * rows_each : (d + 1) * rows_each, :] = returned_ref[d].astype(F32)
    place = lax.broadcasted_iota(I32, (height, LANES), 0)

    sums = [x_ref, *more_refs]

    def some_peers(step, _):
        for c in range(capacity):
            for n, ref in enumerate(sums):
                slot = (step * len(sums) + n) * capacity + c
                word = table_ref[slot]
                first, sent = first_and_sent(word)
                here = pl.ds(first, height)
                cover = lax.shift_right_logical(word, 2 * PLACE)
                piece = jnp.where(place < cover, back_ref[pl.ds(sent, height), :], 0.0)
                ref[here, :] = ref[here, :] - factor_ref[slot] * piece
        return 0

    lax.fori_loop(0, peers // len(sums), some_peers, 0, unroll=2)

    pos = lax.broadcasted_iota(I32, (tile_rows, LANES), 0)
    saves = []
    for p in range(planes):
        inside = (pos >= table_ref[slots + p // bands]) & (pos < table_ref[slots + tiles + p // bands])
        here = slice(p * tile_rows, (p + 1) * tile_rows)
        new = sum((ref[here, :] for ref in more_refs), x_ref[here, :])
        x_ref[here, :] = jnp.where(inside, jnp.maximum(new, 0.0), 0.0)
        if last:
            rows = pl.ds(p * tile_rows, tile_rows)
            saves.append(pltpu.make_async_copy(x_ref.at[rows, :], new_ref.at[rows, :], saved.at[p]))
            saves[-1].start()
    if not last:

        def pack(slot, _):
            first, sent = first_and_sent(table_ref[slot])
            packed_ref[pl.ds(sent, height), :] = x_ref[pl.ds(first, height), :]
            return 0

        lax.fori_loop(0, slots, pack, 0, unroll=64)
        for d in range(peers):
            out_ref[d, :, :] = packed_ref[d * rows_each : (d + 1) * rows_each, :].astype(BF16)
    for save in saves:
        save.wait()


def tables_kernel(
    tile_rows,
    bands,
    height,
    rows_each,
    slot_ref,
    start_ref,
    stop_ref,
    batch_ref,
    plane_ref,
    row_ref,
    cover_ref,
    step_ref,
    lo_ref,
    hi_ref,
    blur_ref,
    update_ref,
    factor_ref,
    length_ref,
    begin_ref,
    scale_ref,
):
    pieces, exposures = slot_ref.shape
    peers, capacity = plane_ref.shape
    slots = peers * capacity

    def clear(s, _):
        length_ref[s] = 0
        return 0

    lax.fori_loop(0, slots, clear, 0, unroll=16)
    for p in range(scale_ref.shape[0]):
        scale_ref[p] = step_ref[p % bands]
    tiles = lo_ref.shape[0]
    for t in range(tiles):
        update_ref[slots + t] = lo_ref[t]
        update_ref[slots + tiles + t] = hi_ref[t]

    def measure(e, _):
        for k in range(pieces):
            s = slot_ref[k, e]
            s = jnp.where(s >= 0, s, slots)
            length_ref[s] = stop_ref[k, e] - start_ref[k, e]
        return 0

    lax.fori_loop(0, exposures, measure, 0, unroll=8)

    def lay(o, _):
        at = sent = o * rows_each
        for c in range(capacity):
            s = o * capacity + c
            begin_ref[s] = at
            at = at + length_ref[s]
            p = jnp.maximum(plane_ref[o, c], 0)
            cover = cover_ref[o, c]
            update_ref[s] = (p * tile_rows + row_ref[o, c]) | (sent << PLACE) | (cover << 2 * PLACE)
            factor_ref[s] = scale_ref[p]
            sent = sent + cover
        return 0

    lax.fori_loop(0, peers, lay, 0)

    def point(e, _):
        for k in range(pieces):
            s = slot_ref[k, e]
            live = s >= 0
            start = start_ref[k, e]
            begin = jnp.where(live, height + begin_ref[jnp.maximum(s, 0)] - start, 0)
            above = batch_ref[e] if k == 0 else jnp.where(live, start, height)
            blur_ref[k * exposures + e] = begin | (above << SHIFT)
        return 0

    lax.fori_loop(0, exposures, point, 0, unroll=8)


def blur_kernel(
    height,
    pieces,
    batches_each,
    last,
    table_ref,
    weight_ref,
    arrived_ref,
    seen_ref,
    *rest,
):
    if last:
        blur_ref, back_ref, out_ref, residual_out_ref, rows_ref, packed_ref, held_ref, residual_ref, sent = rest
    else:
        out_ref, blur_ref, back_ref, rows_ref, packed_ref, held_ref, bank_ref = rest
    peers, rows_each, _ = out_ref.shape
    exposures = seen_ref.shape[0]
    place = lax.broadcasted_iota(I32, (height, LANES), 0)
    lane = lax.broadcasted_iota(I32, (height, LANES), 1)
    for o in range(peers):
        at = height + o * rows_each
        rows_ref[at : at + rows_each, :] = arrived_ref[o, :rows_each, :].astype(F32)
    if not last:
        extra = arrived_ref.shape[1] - rows_each
        for o in range(peers):
            bank_ref[o * extra : (o + 1) * extra, :] = arrived_ref[o, rows_each:, :].astype(F32)
        gap = lane % height - place
        near = (gap <= HALF) & (gap >= -HALF) & (lane < TAPS * height)

        def operators(o, _):
            for n in range(batches_each):
                for m, ref in enumerate((blur_ref, back_ref)):
                    taps = jnp.broadcast_to(bank_ref[pl.ds(o * extra + 2 * n + m, 1), :], (height, LANES))
                    ref[o * batches_each + n] = jnp.where(
                        near, pltpu.roll(taps, 0, 1, stride=1, stride_axis=0), 0.0
                    ).astype(BF16)
            return 0

        lax.fori_loop(0, peers, operators, 0, unroll=min(16, peers))

    def shifted(x):
        parts = []
        for v in range(-HALF, HALF + 1):
            moved = x if v == 0 else pltpu.roll(x, v % LANES, 1)
            parts.append(jnp.where((lane >= v) & (lane < LANES + v), moved, jnp.zeros((), BF16)))
        parts.append(jnp.zeros((LANES - TAPS * height, LANES), BF16))
        return jnp.concatenate(parts, axis=0)

    def blur(e):
        stamp = rows_ref[pl.ds(low(table_ref[e]), height), :]
        for k in range(1, pieces):
            word = table_ref[k * exposures + e]
            stamp = jnp.where(place >= high(word), rows_ref[pl.ds(low(word), height), :], stamp)
        predicted = jnp.dot(
            blur_ref[high(table_ref[e])], shifted(stamp.astype(BF16)), preferred_element_type=F32
        )
        residual = weight_ref[e] * (predicted - seen_ref[e].astype(F32))
        if last:
            residual_ref[e] = residual
        held_ref[e * height : (e + 1) * height, :] = residual.astype(BF16)

    def correlate(e):
        result = jnp.dot(
            back_ref[high(table_ref[e])],
            shifted(held_ref[e * height : (e + 1) * height, :]),
            preferred_element_type=F32,
        )
        words = [table_ref[k * exposures + e] for k in range(pieces)]
        for k, word in enumerate(words):
            mask = place >= high(word) if k else None
            if k + 1 < pieces:
                before = place < high(words[k + 1])
                mask = before if mask is None else mask & before
            pltpu.store(packed_ref.at[pl.ds(low(word), height), :], result, mask=mask)

    quarter = exposures // 4
    sends = []

    def send(n):
        here = pl.ds(n * quarter, quarter)
        sends.append(pltpu.make_async_copy(residual_ref.at[here], residual_out_ref.at[here], sent.at[n]))
        sends[-1].start()

    for stage in range(2):
        for e in range(2 * stage * quarter, 2 * (stage + 1) * quarter):
            blur(e)
        for e in range(stage * quarter, (2 * stage + 1) * quarter):
            correlate(e)
        if last:
            send(2 * stage)
            send(2 * stage + 1)
    for e in range(3 * quarter, exposures):
        correlate(e)
    for o in range(peers):
        at = height + o * rows_each
        out_ref[o, :, :] = packed_ref[at : at + rows_each, :].astype(BF16)
    for copy in sends:
        copy.wait()


def body(
    model,
    exposures,
    inv_var,
    step_size,
    psf_taps,
    exp_batch,
    send_plane,
    send_row,
    send_cover,
    use_slot,
    use_start,
    use_stop,
    foot_lo,
    foot_hi,
):
    tile_count, bands, tile_rows, columns = model.shape
    count, height, _ = exposures.shape
    peers, capacity = send_plane.shape
    pieces = use_slot.shape[1]
    total = tile_count * bands * tile_rows
    rows_each = capacity * height // 2
    batches_each = psf_taps.shape[0]
    extra = aligned(batches_each * 2)
    block = rows_each + extra
    assert columns == LANES and rows_each % extra == 0 and TAPS * height <= LANES - HALF and count % 4 == 0
    x = model.reshape(total, columns)

    def swap(a):
        return lax.all_to_all(a, "sky", split_axis=0, concat_axis=0, tiled=True)

    outbound = pl.pallas_call(
        functools.partial(first_send_kernel, tile_rows, height, rows_each),
        out_shape=jax.ShapeDtypeStruct((peers, block, columns), BF16),
        in_specs=[hbm()] * 5,
        out_specs=hbm(),
        scratch_shapes=[
            pltpu.SMEM(send_plane.shape, I32),
            pltpu.SMEM(send_row.shape, I32),
            pltpu.SMEM(send_cover.shape, I32),
            pltpu.VMEM(psf_taps.shape, F32),
            pltpu.VMEM((total + height, columns), F32),
            pltpu.VMEM((peers * rows_each + height, columns), F32),
            pltpu.VMEM((extra, columns), F32),
            pltpu.VMEM((peers, block, columns), BF16),
            pltpu.SemaphoreType.DMA((12,)),
        ],
        compiler_params=params(2.5),
        name="first_send",
    )(send_plane, send_row, send_cover, psf_taps, x)
    arrived = swap(outbound)
    slots = peers * capacity
    assert max(total, peers * rows_each) < 1 << PLACE and height < 1 << (31 - 2 * PLACE)
    assert max(peers * rows_each + 2 * height, psf_taps.shape[0] * peers) < 1 << (SHIFT - 1)
    blur_table, update_table, factors = pl.pallas_call(
        functools.partial(tables_kernel, tile_rows, bands, height, rows_each),
        out_shape=(
            jax.ShapeDtypeStruct((pieces * count,), I32),
            jax.ShapeDtypeStruct((slots + 2 * tile_count,), I32),
            jax.ShapeDtypeStruct((slots,), F32),
        ),
        in_specs=[smem()] * 10,
        out_specs=(smem(), smem(), smem()),
        scratch_shapes=[
            pltpu.SMEM((slots + 1,), I32),
            pltpu.SMEM((slots,), I32),
            pltpu.SMEM((tile_count * bands,), F32),
        ],
        compiler_params=params(),
        cost_estimate=pl.CostEstimate(flops=4_000_000, bytes_accessed=8_000_000, transcendentals=0),
        name="tables",
    )(
        use_slot.T,
        use_start.T,
        use_stop.T,
        exp_batch,
        send_plane,
        send_row,
        send_cover,
        step_size,
        foot_lo,
        foot_hi,
    )
    operators = []
    for sweep in range(ITERS):
        last = sweep == ITERS - 1
        rows_shape = jax.ShapeDtypeStruct((peers, rows_each, columns), BF16)
        scratch = [
            pltpu.VMEM((peers * rows_each + 2 * height, columns), F32),
            pltpu.VMEM((peers * rows_each + 2 * height, columns), F32),
            pltpu.VMEM((count * height, columns), BF16),
        ]
        if last:
            scratch += [pltpu.VMEM(exposures.shape, F32), pltpu.SemaphoreType.DMA((4,))]
            out_shape, out_specs = (rows_shape, jax.ShapeDtypeStruct(exposures.shape, F32)), (vmem(), hbm())
        else:
            scratch.append(pltpu.VMEM((peers * extra, columns), F32))
            operator_shape = jax.ShapeDtypeStruct((peers * batches_each, height, columns), BF16)
            out_shape, out_specs = (rows_shape, operator_shape, operator_shape), (vmem(),) * 3
        outgoing, *others = pl.pallas_call(
            functools.partial(blur_kernel, height, pieces, batches_each, last),
            out_shape=out_shape,
            in_specs=[smem()] * 2 + [vmem()] * (4 if last else 2),
            out_specs=out_specs,
            scratch_shapes=scratch,
            compiler_params=params(),
            name="blur",
        )(blur_table, inv_var, arrived, exposures, *operators)
        operators = [] if last else others
        returned = swap(outgoing)
        new_shape = jax.ShapeDtypeStruct((total, columns), F32)
        padded = (total + height, columns)
        scratch = [pltpu.VMEM((peers * rows_each + height, columns), F32)]
        if last:
            scratch += [pltpu.VMEM(padded, F32), pltpu.SemaphoreType.DMA((tile_count * bands,))]
        else:
            scratch.append(pltpu.VMEM((peers * rows_each + height, columns), F32))
        sums = max(n for n in (1, 2) if peers % n == 0)
        res = pl.pallas_call(
            functools.partial(update_kernel, bands, tile_rows, height, last),
            out_shape=jax.ShapeDtypeStruct((total, columns), F32)
            if last
            else (jax.ShapeDtypeStruct(padded, F32), rows_shape),
            in_specs=[smem()] * 2 + [vmem(), vmem()],
            out_specs=hbm() if last else (vmem(), vmem()),
            scratch_shapes=scratch + [pltpu.VMEM(padded, F32)] * (sums - 1),
            compiler_params=params(),
            name="update",
        )(update_table, factors, returned, x)
        if last:
            x = res
        else:
            x, outbound = res
            arrived = swap(outbound)
    return (x.reshape(model.shape), others[0])


def solution(mesh):
    both = ("groups", "sky")
    return jax.shard_map(
        body,
        mesh=mesh,
        in_specs=(
            P(both, None, None, None),
            P(both, None, None),
            P(both),
            P(),
            P(both, None),
            P(both),
            P(both, None),
            P(both, None),
            P(both, None),
            P(both, None),
            P(both, None),
            P(both, None),
            P(both),
            P(both),
        ),
        out_specs=(P(both, None, None, None), P(both, None, None)),
        check_vma=False,
    )
```
